128 devices in a mesh: row: 16 (over x, y), col: 8 (over z, core).
Axes of the slice: x: 4, y: 4, z: 4, core: 2. Of those that a mesh axis runs over, the one named last changes fastest.
Arguments:
- layer_input: bfloat16 [16384, 1024], P(('row', 'col')), may hold values from -3 to 3
- lengths: int32 [16, 3], P('row'), may hold values from 1 to 512, 1024 in all within a row
- choices: int32 [16384, 8], P(('row', 'col')), may hold values from 0 to 31, all different within a row; in each aligned block of 128 rows (0 to 127, 128 to 255, ...) at most 64 rows name the same one
- query_weight: bfloat16 [1024, 1024], P('row', 'col'), may hold values from -0.25 to 0.25
- key_matrix: bfloat16 [1024, 512], P('row', 'col'), may hold values from -0.25 to 0.25
- value_matrix: bfloat16 [1024, 512], P('row', 'col'), may hold values from -0.1875 to 0.1875
- project_weight: bfloat16 [1024, 1024], P('col', 'row'), may hold values from -2 to 2
- gate_weight: bfloat16 [32, 1024, 512], P('col', 'row'), may hold values from -0.1875 to 0.1875
- up_weight: bfloat16 [32, 1024, 512], P('col', 'row'), may hold values from -0.1875 to 0.1875
- down_weight: bfloat16 [32, 512, 1024], P('col', None, 'row'), may hold values from -2 to 2
- router_weight: bfloat16 [1024, 32], replicated, may hold values from -0.09375 to 0.09375
- attention_gain: float32 [1024], replicated, may hold values from 0.5 to 1.5
- expert_gain: float32 [1024], replicated, may hold values from 0.5 to 1.5
- grad_output: bfloat16 [16384, 1024], P(('row', 'col')), may hold values from -6 to 6
Outputs:
- block_output: float32 [16384, 1024], P(('row', 'col'))
- input_grad: float32 [16384, 1024], P(('row', 'col'))
- query_grad: float32 [1024, 1024], P('row', 'col')
- key_grad: float32 [1024, 512], P('row', 'col')
- value_grad: float32 [1024, 512], P('row', 'col')
- project_grad: float32 [1024, 1024], P('col', 'row')
- gate_grad: float32 [32, 1024, 512], P('col', 'row')
- up_grad: float32 [32, 1024, 512], P('col', 'row')
- down_grad: float32 [32, 512, 1024], P('col', None, 'row')
- router_grad: float32 [1024, 32], replicated
- attention_gain_grad: float32 [1024], replicated
- expert_gain_grad: float32 [1024], replicated
The draws below stay inside these ranges and needn't reach their ends.
Inputs may be any that keep to these rules, and one draw needn't show every extreme that they name: `choices`: the 8 experts of a token differ. Among the 128 rows of one device no expert is chosen more than 64 times, and some expert is chosen exactly 64 times there. The 3 lengths of a row sum to 1024; in every row the longest is 512.
All inputs are finite; a program needn't handle non-finite values.
Results may differ from the reference program's by a relative error of at most 0.02.
Values may be sent and summed in bfloat16 or wider, within the bound.
No kernel may reach another device: no remote copies, remote signals or barrier semaphores. Data moves between devices by JAX's collectives and lax.ppermute only.
A program may use at most 192 MiB of HBM per device.

```python
import math
import jax
import jax.numpy as jnp
import numpy as np
from jax import lax

MODEL_DIM = 1024
QUERY_HEADS = 16
KEY_VALUE_HEADS = 8
HEAD_SIZE = 64
EXPERTS = 32
FF = 512
TOP = 8
TOK_DEV = 128
ROW_TOKENS = 1024
MAXLEN = 512
NSEQ = 3
CAP = 64
TOKENS = 16384
N_ROW = 16
N_COL = 8


def shard_levels(rng, dims, cuts, low, high):
    factor_of = 1.0
    for dim, blocks in cuts:
        steps = jax.random.uniform(jax.random.fold_in(jax.random.fold_in(rng, 6), dim), (blocks,), jnp.float32, low / len(cuts), high / len(cuts))
        factor_of = factor_of * jnp.repeat(jnp.exp(steps), dims[dim] // blocks).reshape((-1,) + (1,) * (len(dims) - 1 - dim))
    return factor_of


def profile(number_of, total, bound, slope):
    portions = [(1 << 20) // math.isqrt(rank ** slope) + 1 for rank in range(2, number_of + 1)]
    rest, counts = total - bound - (number_of - 1), [1] * (number_of - 1)
    while rest > 0:
        free = [i for i in range(number_of - 1) if counts[i] < bound]
        whole, left = sum([portions[i] for i in free]), rest
        for i in free:
            extra = min(bound - counts[i], max(1, left * portions[i] // whole), rest)
            counts[i] = counts[i] + extra
            rest = rest - extra
    return np.array([bound] + counts)


def ragged_sizes(stream_key, amount, total, most, lean):
    if amount == 2:
        one = jax.random.randint(stream_key, (), max(1, total - most), min(most, total - 1) + 1)
        return jnp.stack([one, total - one])
    sizes = jnp.asarray(profile(amount, total, most, lean), jnp.int32)
    twos = (amount - 1) // 2
    source_of, taker = sizes[1:1 + 2 * twos:2], sizes[2:2 + 2 * twos:2]
    margin = jnp.minimum(source_of - 1, most - taker)
    shifted = jax.random.randint(jax.random.fold_in(stream_key, 1), (twos,), 0, 1 << 20) % (margin + 1)
    sizes = sizes.at[1:1 + 2 * twos:2].set(source_of - shifted).at[2:2 + 2 * twos:2].set(taker + shifted)
    return sizes[jax.random.permutation(jax.random.fold_in(stream_key, 2), amount)]


def routed_block(own_key, own, number, rows, count, top, limit, lean):
    sequence = jax.random.permutation(own_key, count)
    packed, usual = load_shares(count, rows * top, limit, lean, True), load_shares(count, rows * top, limit, lean, False)
    places = jnp.arange(count)

    def named(sizes, offset_by):
        used = int((sizes > 0).sum())
        fixed = max(1, used // 4)
        moved = fixed + (places - fixed + offset_by * (used - fixed)) % max(1, count - fixed)
        return jnp.zeros((count,), jnp.int32).at[sequence[jnp.where(places < fixed, places, moved)]].set(jnp.asarray(sizes, jnp.int32))

    sizes = jnp.where(number % 4 == 0, named(packed, number // 4), named(usual, number - number // 4 - 1))
    mixed = jax.random.permutation(jax.random.fold_in(own, 3), count)
    giver, sink = mixed[0:count // 2 * 2:2], mixed[1:count // 2 * 2:2]
    margin = jnp.minimum(sizes[giver] - 1, limit - sizes[sink]) // 2
    margin = jnp.where((giver == sequence[0]) | (sink == sequence[0]) | (sizes[sink] == 0), 0, jnp.maximum(margin, 0))
    moved = jax.random.randint(jax.random.fold_in(own, 4), (count // 2,), 0, 1 << 20) % (margin + 1)
    sizes = sizes.at[giver].add(-moved).at[sink].add(moved)
    items = jnp.searchsorted(jnp.cumsum(sizes), jnp.arange(rows * top), side="right").astype(jnp.int32)
    table = items.reshape(top, rows).T
    table = table[jax.random.permutation(jax.random.fold_in(own, 1), rows)]
    offset_by = jax.random.randint(jax.random.fold_in(own, 2), (rows, 1), 0, top)
    return jnp.take_along_axis(table, (jnp.arange(top)[None, :] + offset_by) % top, axis=1)


def load_shares(number_of, total, reach, slope, full):
    loads = [(1 << 20) // math.isqrt(standing ** slope) + 1 for standing in range(1, number_of + 1)]
    largest = reach if full else min(reach, max(-(-total // number_of), total * loads[0] // sum(loads)))
    least = 1 if total - largest >= number_of - 1 else 0
    counts, spare = [largest] + [least] * (number_of - 1), total - largest - least * (number_of - 1)
    while spare > 0:
        free = [i for i in range(1, number_of) if counts[i] < largest] or [i for i in range(1, number_of) if counts[i] < reach]
        whole, remaining = sum([loads[i] for i in free]), spare
        for i in free:
            addition = min(reach - counts[i], max(1, remaining * loads[i] // whole), spare)
            counts[i] = counts[i] + addition
            spare = spare - addition
    return np.array(counts)


def scatter_about(rng, shape, width, limit, split=(), kind=jnp.bfloat16):
    entries = width * jax.random.normal(rng, shape, jnp.float32)
    if split:
        entries = entries * shard_levels(rng, shape, split, -0.22, 0.18)
    return jnp.clip(entries, -limit, limit).astype(kind)


def setup_inputs(seed: int = 0) -> dict:
    seeds = jax.random.split(jax.random.key(seed), 15)
    layer_input = scatter_about(seeds[0], (TOKENS, MODEL_DIM), 0.5, 3.0, ((0, 128),))
    lengths = jax.vmap(lambda own: ragged_sizes(own, NSEQ, ROW_TOKENS, MAXLEN, 1))(jax.random.split(seeds[1], N_ROW)).reshape((N_ROW, NSEQ)).astype(jnp.int32)
    choices_keys = jax.random.split(jax.random.fold_in(seeds[2], 1), TOKENS // TOK_DEV)
    choices_turns = jax.random.permutation(jax.random.fold_in(seeds[2], 3), TOKENS // TOK_DEV)
    choices = jax.vmap(lambda own, number: routed_block(jax.random.fold_in(seeds[2], 2), own, number, TOK_DEV, EXPERTS, TOP, CAP, 1))(choices_keys, choices_turns).reshape((TOKENS, TOP))
    query_weight = scatter_about(seeds[3], (MODEL_DIM, QUERY_HEADS * HEAD_SIZE), (MODEL_DIM // 2) ** -0.5, 0.25, ((0, 16), (1, 8)))
    key_matrix = scatter_about(seeds[4], (MODEL_DIM, KEY_VALUE_HEADS * HEAD_SIZE), (MODEL_DIM // 2) ** -0.5, 0.25, ((0, 16), (1, 8)))
    value_matrix = scatter_about(seeds[5], (MODEL_DIM, KEY_VALUE_HEADS * HEAD_SIZE), MODEL_DIM ** -0.5, 0.1875, ((0, 16), (1, 8)))
    project_weight = scatter_about(seeds[6], (QUERY_HEADS * HEAD_SIZE, MODEL_DIM), (max(1, QUERY_HEADS * HEAD_SIZE // 128)) ** -0.5, 2.0, ((0, 8), (1, 16)))
    gate_weight = scatter_about(seeds[7], (EXPERTS, MODEL_DIM, FF), MODEL_DIM ** -0.5, 0.1875, ((0, 8), (1, 16)))
    up_weight = scatter_about(seeds[8], (EXPERTS, MODEL_DIM, FF), MODEL_DIM ** -0.5, 0.1875, ((0, 8), (1, 16)))
    down_weight = scatter_about(seeds[9], (EXPERTS, FF, MODEL_DIM), (max(1, FF // 64)) ** -0.5, 2.0, ((0, 8), (2, 16)))
    router_weight = scatter_about(seeds[10], (MODEL_DIM, EXPERTS), (4 * MODEL_DIM) ** -0.5, 0.09375)
    attention_gain = jnp.clip(1.0 + 0.1 * jax.random.normal(seeds[11], (MODEL_DIM,), jnp.float32), 0.5, 1.5)
    expert_gain = jnp.clip(1.0 + 0.1 * jax.random.normal(seeds[12], (MODEL_DIM,), jnp.float32), 0.5, 1.5)
    grad_output = scatter_about(seeds[13], (TOKENS, MODEL_DIM), 1.0, 6.0, ((0, 128),))
    return {"layer_input": layer_input, "lengths": lengths, "choices": choices, "query_weight": query_weight, "key_matrix": key_matrix, "value_matrix": value_matrix, "project_weight": project_weight, "gate_weight": gate_weight, "up_weight": up_weight, "down_weight": down_weight, "router_weight": router_weight, "attention_gain": attention_gain, "expert_gain": expert_gain, "grad_output": grad_output}


epsilon = 1e-06
residual_scale = 0.22
score_scale = 0.125
rope_base = 10000.0
highest = lax.Precision.HIGHEST

@jax.custom_vjp
def lower_half(v):
    return lax.optimization_barrier(v.astype(jnp.bfloat16)).astype(jnp.float32)

@jax.custom_vjp
def lower_half_grad(v):
    return v

def low_keep(v):
    return (lower_half(v), None)

def low_pass(kept, grad):
    return (grad,)

def back_keep(v):
    return (v, None)

def back_low(kept, grad):
    return (lower_half(grad),)
lower_half.defvjp(low_keep, low_pass)
lower_half_grad.defvjp(back_keep, back_low)

def rms_scale(values, gain_vec):
    return values * lax.rsqrt(lax.optimization_barrier(jnp.mean(values * values, axis=-1, keepdims=True)) + epsilon) * gain_vec

def softmax_last(values):
    largest = lax.optimization_barrier(jnp.max(values, axis=-1, keepdims=True))
    raised = jnp.exp(values - largest)
    return raised / lax.optimization_barrier(jnp.sum(raised, axis=-1, keepdims=True))

def layout(lengths_row):
    seq_ends = jnp.cumsum(lengths_row).astype(jnp.int32)
    starts = seq_ends - lengths_row
    places = jnp.arange(ROW_TOKENS, dtype=jnp.int32)
    segment = lax.optimization_barrier(jnp.sum((places[:, None] >= seq_ends[None, :]).astype(jnp.int32), axis=1))
    matches = segment[:, None] == jnp.arange(NSEQ, dtype=jnp.int32)[None, :]
    position = places - lax.optimization_barrier(jnp.sum(jnp.where(matches, starts[None, :], 0), axis=1))
    return (segment, position)

def rope_tables(position):
    frequency = rope_base ** (-(jnp.arange(HEAD_SIZE // 2, dtype=jnp.float32) * 2.0 / HEAD_SIZE))
    angles = position.astype(jnp.float32)[:, None] * frequency[None, :]
    return (jnp.cos(angles), jnp.sin(angles))

def apply_rotation(values, cosine_table, sine_values, turning):
    half_size = values.shape[-1] // 2
    front_half = values[..., :half_size]
    back_half = values[..., half_size:]
    cos_part = cosine_table[:, None, :]
    sin_part = turning * sine_values[:, None, :]
    return jnp.concatenate([front_half * cos_part - back_half * sin_part, back_half * cos_part + front_half * sin_part], axis=-1)

def slot_rows(group_choices):
    member = jnp.any(group_choices[:, :, None] == jnp.arange(EXPERTS, dtype=jnp.int32)[None, None, :], axis=1).T
    places = jnp.arange(ROW_TOKENS, dtype=jnp.int32)
    ranked = jnp.where(member, places[None, :], places[None, :] + ROW_TOKENS)
    ordering = jnp.argsort(ranked, axis=1)[:, :N_COL * CAP].astype(jnp.int32)
    is_taken = jnp.take_along_axis(member, ordering, axis=1)
    return jnp.where(is_taken, ordering, ROW_TOKENS).astype(jnp.int32)

def reference(layer_input, lengths, choices, query_weight, key_matrix, value_matrix, project_weight, gate_weight, up_weight, down_weight, router_weight, attention_gain, expert_gain, grad_output):
    floats = tuple((item.astype(jnp.float32) for item in (layer_input, query_weight, key_matrix, value_matrix, project_weight, gate_weight, up_weight, down_weight, router_weight, attention_gain, expert_gain)))
    segments, positions = jax.vmap(layout)(lengths)
    cosines, sines = jax.vmap(rope_tables)(positions)
    group_choices = choices.reshape(N_ROW, ROW_TOKENS, TOP)
    slot_index = jax.vmap(slot_rows)(group_choices)

    def forward(inputs, w_query, w_key, w_value, w_project, w_gate, w_up, w_down, w_router, gain_one, gain_two):

        def layer(group_item):
            group_in, segment, cosine_table, sine_values, chosen_ids, rows_index = group_item
            normed = lower_half(rms_scale(group_in, gain_one))
            query_unrotated = jnp.dot(normed, w_query, precision=highest)
            key_unrotated = jnp.dot(normed, w_key, precision=highest)
            value_projected = jnp.dot(normed, w_value, precision=highest)
            query_rows = lower_half(apply_rotation(lower_half_grad(query_unrotated).reshape(ROW_TOKENS, QUERY_HEADS, HEAD_SIZE), cosine_table, sine_values, 1.0)).reshape(ROW_TOKENS, KEY_VALUE_HEADS, QUERY_HEADS // KEY_VALUE_HEADS, HEAD_SIZE)
            keys_rotated = lower_half(apply_rotation(lower_half_grad(key_unrotated).reshape(ROW_TOKENS, KEY_VALUE_HEADS, HEAD_SIZE), cosine_table, sine_values, 1.0))
            value_rows_full = lower_half(lower_half_grad(value_projected)).reshape(ROW_TOKENS, KEY_VALUE_HEADS, HEAD_SIZE)
            places = jnp.arange(ROW_TOKENS, dtype=jnp.int32)
            allowed = (segment[:, None] == segment[None, :]) & (places[None, :] <= places[:, None])
            scores = lower_half_grad(jnp.einsum('qkgd,skd->kgqs', query_rows, keys_rotated, precision=highest) * score_scale)
            scores = jnp.where(allowed[None, None], scores, -1e+30)
            probs = lower_half(softmax_last(scores))
            context = jnp.einsum('kgqs,skd->qkgd', probs, value_rows_full, precision=highest).reshape(ROW_TOKENS, QUERY_HEADS * HEAD_SIZE)
            context = lower_half(lower_half_grad(context))
            attention = lower_half_grad(jnp.dot(context, w_project, precision=highest))
            middle = group_in + residual_scale * attention
            expert_in = lower_half(rms_scale(middle, gain_two))
            router_logits = jnp.dot(expert_in, w_router, precision=highest)
            selector = (chosen_ids[:, :, None] == jnp.arange(EXPERTS, dtype=jnp.int32)[None, None, :]).astype(jnp.float32)
            gate_values = softmax_last(lax.optimization_barrier(jnp.sum(selector * router_logits[:, None, :], axis=-1)))
            weight_of = lax.optimization_barrier(jnp.sum(gate_values[:, :, None] * selector, axis=1)).T
            padded = jnp.concatenate([expert_in, jnp.zeros((1, MODEL_DIM), jnp.float32)], axis=0)
            rows = lower_half_grad(padded[rows_index])
            gate_act = lower_half_grad(jnp.einsum('erd,edf->erf', rows, w_gate, precision=highest))
            up_act = lower_half_grad(jnp.einsum('erd,edf->erf', rows, w_up, precision=highest))
            hidden = lower_half(gate_act * jax.nn.sigmoid(gate_act) * up_act)
            expert_out = lower_half_grad(lower_half(jnp.einsum('erf,efd->erd', hidden, w_down, precision=highest)))
            padded_gates = jnp.concatenate([weight_of, jnp.zeros((EXPERTS, 1), jnp.float32)], axis=1)
            row_gate = jnp.take_along_axis(padded_gates, rows_index, axis=1)
            mixture = jnp.zeros((ROW_TOKENS + 1, MODEL_DIM), jnp.float32).at[rows_index.reshape(-1)].add((row_gate[:, :, None] * expert_out).reshape(-1, MODEL_DIM))[:ROW_TOKENS]
            return middle + residual_scale * mixture
        outputs = lax.map(jax.checkpoint(layer), (inputs.reshape(N_ROW, ROW_TOKENS, MODEL_DIM), segments, cosines, sines, group_choices, slot_index))
        return outputs.reshape(TOKENS, MODEL_DIM)
    block_output, pullback = jax.vjp(forward, *floats)
    gradients = pullback(grad_output.astype(jnp.float32))
    return (block_output, gradients[0], gradients[1], gradients[2], gradients[3], gradients[4], gradients[5], gradients[6], gradients[7], gradients[8], gradients[9], gradients[10])
```

```python
import functools

import jax
import jax.numpy as jnp
from jax import lax
from jax.experimental import pallas as pl
from jax.experimental.pallas import tpu as pltpu
from jax.sharding import PartitionSpec as P

HEAD = 64
LANES = 128
QB = 256
EPS = 1e-06
RES = 0.22
SCALE = 0.125
BASE = 10000.0
bf16 = jnp.bfloat16
f32 = jnp.float32
VMEM_MB = 1 << 20


def dot_nt(a, b):
    return lax.dot_general(a, b, (((1,), (1,)), ((), ())), preferred_element_type=f32)


def dot_nn(a, b):
    return lax.dot_general(a, b, (((1,), (0,)), ((), ())), preferred_element_type=f32)


def rms_scale(values, gain_vec):
    return values * lax.rsqrt(jnp.mean(values * values, axis=-1, keepdims=True) + EPS) * gain_vec


def core_swap(a):
    return lax.ppermute(a, "col", [(i, i ^ 1) for i in range(8)])


def z_shift(a, d):
    return lax.ppermute(a, "col", [(i, (i + 2 * d) % 8) for i in range(8)])


def y_shift(a, d):
    return lax.ppermute(a, "row", [(i, (i // 4) * 4 + (i + d) % 4) for i in range(16)])


def x_shift(a, d):
    return lax.ppermute(a, "row", [(i, (i + 4 * d) % 16) for i in range(16)])


def col_pieces(a, split):
    half = a.shape[split] // 2
    cut = lambda v, k: lax.slice_in_dim(v, k * half, (k + 1) * half, axis=split)
    other = core_swap(a)
    back = z_shift(a, 1)
    ahead = z_shift(a, -1)
    back_other = core_swap(back)
    ahead_other = core_swap(ahead)
    far0 = z_shift(cut(back, 0), 1)
    far1 = z_shift(cut(ahead, 1), -1)
    far = jnp.concatenate([far0, far1], axis=split)
    far_other = core_swap(far)
    return [
        (0, 0, a),
        (0, 1, other),
        (3, 0, back),
        (3, 1, back_other),
        (1, 0, ahead),
        (1, 1, ahead_other),
        (2, 0, far),
        (2, 1, far_other),
    ]


def gather_col(a, dim, split=0):
    me = lax.axis_index("col")
    z, core = me // 2, me % 2
    size = a.shape[dim]
    shape = list(a.shape)
    shape[dim] = size * 8
    out = jnp.zeros(shape, a.dtype)
    for dz, dc, piece in col_pieces(a, split):
        at = (((z + dz) % 4) * 2 + (core + dc) % 2) * size
        out = lax.dynamic_update_slice_in_dim(out, piece, at, axis=dim)
    return out


def sum_col(a):
    me = lax.axis_index("col")
    z, core = me // 2, me % 2
    rows = a.shape[0] // 8
    tiles = a.reshape(4, 2, rows, a.shape[1])
    take = lambda c: lax.dynamic_slice_in_dim(tiles, c, 1, axis=1)[:, 0]
    got = core_swap(take(1 - core))
    mine = take(core).astype(f32) + got.astype(f32)
    block = lambda d: lax.dynamic_slice_in_dim(mine, (z + d) % 4, 1, axis=0)[0]
    half = rows // 2
    far = block(2).astype(bf16)
    via_up = z_shift(far[:half], 1)
    via_down = z_shift(far[half:], -1)
    up = block(1)
    down = block(3)
    up = jnp.concatenate([up[:half] + via_up.astype(f32), up[half:]], axis=0).astype(bf16)
    down = jnp.concatenate([down[:half], down[half:] + via_down.astype(f32)], axis=0).astype(bf16)
    return block(0) + z_shift(up, 1).astype(f32) + z_shift(down, -1).astype(f32)


def gather_row_small(a):
    me = lax.axis_index("row")
    x, y = me // 4, me % 4
    n = a.shape[0]
    line = jnp.zeros((4 * n, a.shape[1]), a.dtype)
    line = lax.dynamic_update_slice_in_dim(line, a, y * n, axis=0)
    for d in (1, 3, 2):
        line = lax.dynamic_update_slice_in_dim(line, y_shift(a, d), ((y + 4 - d) % 4) * n, axis=0)
    out = jnp.zeros((16 * n, a.shape[1]), a.dtype)
    out = lax.dynamic_update_slice_in_dim(out, line, x * 4 * n, axis=0)
    for d in (1, 3, 2):
        out = lax.dynamic_update_slice_in_dim(
            out, x_shift(line, d), ((x + 4 - d) % 4) * 4 * n, axis=0
        )
    return out


def sum_row_small(a):
    me = lax.axis_index("row")
    x, y = me // 4, me % 4
    n = a.shape[0] // 16
    part = lambda v, k, size: lax.dynamic_slice_in_dim(v, (k % 4) * size, size, axis=0)
    total = part(a, x, 4 * n).astype(f32)
    for d in (1, 3, 2):
        total = total + x_shift(part(a, x + d, 4 * n), d).astype(f32)
    low = total.astype(bf16)
    out = part(total, y, n)
    for d in (1, 3, 2):
        out = out + y_shift(part(low, y + d, n), d).astype(f32)
    return out


def sum_everywhere(v):
    for bit in (1, 2, 4):
        v = v + lax.ppermute(v, "col", [(i, i ^ bit) for i in range(8)])
    for bit in (1, 2, 4, 8):
        v = v + lax.ppermute(v, "row", [(i, i ^ bit) for i in range(16)])
    return v


def lane_of(shape):
    return lax.broadcasted_iota(jnp.int32, shape, 1)


def rotate(values, cos, sin):
    first = (lane_of(values.shape) % HEAD) < HEAD // 2
    swapped = jnp.where(first, pltpu.roll(values, 96, 1), pltpu.roll(values, 32, 1))
    return values * cos + swapped * sin


def allowed_keys(lo, count, row0, begin):
    key = lax.broadcasted_iota(jnp.int32, (count, QB), 0) + lo
    query = lax.broadcasted_iota(jnp.int32, (count, QB), 1) + row0
    return (key >= begin) & (key <= query)


def soft(kk, qh, ok):
    s = jnp.where(ok, dot_nt(kk, qh) * SCALE, -1e30)
    raised = jnp.exp(s - jnp.max(s, axis=0, keepdims=True))
    return raised / jnp.sum(raised, axis=0, keepdims=True)


def key_range(i):
    return max(0, i - 2) * QB, (i + 1) * QB


def attend_kernel(x_ref, gain_ref, w_ref, cos_ref, sin_ref, begin_ref, n_ref, q_ref, kk_ref, vv_ref, ctx_ref):
    total = x_ref.shape[0]
    left = lane_of((QB, LANES)) < HEAD
    for i in range(total // QB):
        rows = pl.ds(i * QB, QB)
        x = x_ref[rows, :].astype(f32)
        normed = rms_scale(x, gain_ref[...]).astype(bf16)
        n_ref[rows, :] = normed
        raw = dot_nn(normed, w_ref[...])
        cos, sin = cos_ref[rows, :], sin_ref[rows, :]
        q_ref[rows, :] = rotate(raw[:, :LANES], cos, sin).astype(bf16)
        kv = raw[:, LANES:]
        turned = rotate(kv, cos, sin)
        kk_ref[rows, :] = jnp.where(left, turned, pltpu.roll(turned, HEAD, 1)).astype(bf16)
        vv_ref[rows, :] = jnp.where(left, pltpu.roll(kv, HEAD, 1), kv).astype(bf16)
    vt = vv_ref[...].astype(f32).T.astype(bf16)
    upper = lax.broadcasted_iota(jnp.int32, (LANES, QB), 0) < HEAD
    for i in range(total // QB):
        rows = pl.ds(i * QB, QB)
        lo, hi = key_range(i)
        keys = kk_ref[lo:hi, :]
        ok = allowed_keys(lo, hi - lo, i * QB, begin_ref[:, i * QB : (i + 1) * QB])
        found = []
        for h in range(2):
            qh = jnp.where(left == (h == 0), q_ref[rows, :], jnp.zeros((QB, LANES), bf16))
            p = soft(keys, qh, ok).astype(bf16)
            found.append(dot_nn(vt[:, lo:hi], p))
        ctx_ref[rows, :] = jnp.where(upper, found[0], found[1]).T.astype(bf16)


def attend_back_kernel(
    ag_ref, wp_ref, q_ref, kk_ref, vv_ref, ctx_ref, n_ref, x_ref, cos_ref, sin_ref, begin_ref, w_ref,
    dn_ref, wg_ref, gain_ref, dctx_ref, dk_ref, dv_ref, dqkv_ref,
):
    total = ag_ref.shape[0]
    left = lane_of((QB, LANES)) < HEAD
    upper = lax.broadcasted_iota(jnp.int32, (LANES, QB), 0) < HEAD
    dctx_ref[...] = dot_nn(ag_ref[...], wp_ref[...]).astype(bf16)
    dk_ref[...] = jnp.zeros_like(dk_ref)
    dv_ref[...] = jnp.zeros_like(dv_ref)
    kt = kk_ref[...].astype(f32).T.astype(bf16)
    for i in range(total // QB):
        rows = pl.ds(i * QB, QB)
        lo, hi = key_range(i)
        keys = kk_ref[lo:hi, :]
        ok = allowed_keys(lo, hi - lo, i * QB, begin_ref[:, i * QB : (i + 1) * QB])
        found = []
        for h in range(2):
            mine = left == (h == 0)
            qh = jnp.where(mine, q_ref[rows, :], jnp.zeros((QB, LANES), bf16))
            dch = jnp.where(mine, dctx_ref[rows, :], jnp.zeros((QB, LANES), bf16))
            p = soft(keys, qh, ok)
            dp = dot_nt(vv_ref[lo:hi, :], dch)
            ds = (p * (dp - jnp.sum(dp * p, axis=0, keepdims=True))).astype(bf16)
            dk_ref[lo:hi, :] += dot_nn(ds, qh)
            dv_ref[lo:hi, :] += dot_nn(p.astype(bf16), dch)
            found.append(dot_nn(kt[:, lo:hi], ds))
        dq = jnp.where(upper, found[0], found[1]).T * SCALE
        dqkv_ref[rows, :LANES] = rotate(dq, cos_ref[rows, :], -sin_ref[rows, :]).astype(bf16)
    acc = jnp.zeros((1, n_ref.shape[1]), f32)
    for i in range(total // QB):
        rows = pl.ds(i * QB, QB)
        dk, dv = dk_ref[rows, :], dv_ref[rows, :]
        dk = (dk + pltpu.roll(dk, HEAD, 1)) * SCALE
        dk = rotate(dk, cos_ref[rows, :], -sin_ref[rows, :])
        dv = dv + pltpu.roll(dv, HEAD, 1)
        dqkv_ref[rows, LANES:] = jnp.where(left, dk, dv).astype(bf16)
        dn = dot_nt(dqkv_ref[rows, :], w_ref[...])
        dn_ref[rows, :] = dn.astype(bf16)
        x = x_ref[rows, :].astype(f32)
        hat = x * lax.rsqrt(jnp.mean(x * x, axis=-1, keepdims=True) + EPS)
        acc = acc + jnp.sum(dn * hat, axis=0, keepdims=True)
    gain_ref[...] = acc
    dqkv_t = dqkv_ref[...].astype(f32).T.astype(bf16)
    ctx_t = ctx_ref[...].astype(f32).T.astype(bf16)
    wg_ref[:, : 2 * LANES] = dot_nn(dqkv_t, n_ref[...]).T.astype(bf16)
    wg_ref[:, 2 * LANES :] = dot_nn(ctx_t, ag_ref[...]).T.astype(bf16)


def experts_kernel(
    base_ref, x_ref, dy_ref, gates_ref, w_ref, mix_ref, dx_ref, out_ref,
    xt_ref, dyt_ref, accm_ref, accx_ref, dg_ref, h_ref, dgu_ref,
):
    e = pl.program_id(0)
    ff = h_ref.shape[1]
    total = x_ref.shape[0]
    rb = 256

    @pl.when(e == 0)
    def _():
        for k in range(total // rb):
            xt_ref[:, k * rb : (k + 1) * rb] = x_ref[k * rb : (k + 1) * rb, :].T
            dyt_ref[:, k * rb : (k + 1) * rb] = dy_ref[k * rb : (k + 1) * rb, :].T
        accm_ref[...] = jnp.zeros_like(accm_ref)
        accx_ref[...] = jnp.zeros_like(accx_ref)
        dg_ref[...] = jnp.zeros_like(dg_ref)

    lane = lane_of((rb, LANES))
    pick = base_ref[0] + e

    def tokens(k, carry):
        rows = pl.ds(pl.multiple_of(k * rb, rb), rb)
        gu = dot_nn(x_ref[rows, :], w_ref[:, : 2 * ff])
        h0 = dot_nn(dy_ref[rows, :], w_ref[:, 2 * ff :]) * RES
        g, u = gu[:, :ff], gu[:, ff:]
        gate = jnp.sum(jnp.where(lane == pick, gates_ref[rows, :], 0.0), axis=1, keepdims=True)
        sg = jax.nn.sigmoid(g)
        sw = g * sg
        hid = sw * u
        dg = jnp.sum(hid * h0, axis=1, keepdims=True)
        dg_ref[rows, :] += jnp.where(lane == pick, dg, 0.0)
        h_ref[rows, :] = (gate * hid).astype(bf16)
        dh = gate * h0
        dgu_ref[rows, :ff] = (dh * u * sg * (1.0 + g * (1.0 - sg))).astype(bf16)
        dgu_ref[rows, ff:] = (dh * sw).astype(bf16)
        accm_ref[rows, :] += dot_nt(h_ref[rows, :], w_ref[:, 2 * ff :])
        accx_ref[rows, :] += dot_nt(dgu_ref[rows, :], w_ref[:, : 2 * ff])
        return carry

    lax.fori_loop(0, total // rb, tokens, 0)

    def widths(k, carry):
        rows = pl.ds(pl.multiple_of(k * rb, rb), rb)
        out_ref[rows, : 2 * ff] = dot_nn(xt_ref[rows, :], dgu_ref[...]).astype(bf16)
        out_ref[rows, 2 * ff :] = (dot_nn(dyt_ref[rows, :], h_ref[...]) * RES).astype(bf16)
        return carry

    lax.fori_loop(0, xt_ref.shape[0] // rb, widths, 0)

    @pl.when(e == pl.num_programs(0) - 1)
    def _():
        width = accx_ref.shape[1]
        mix_ref[...] = accm_ref[...].astype(bf16)
        dx_ref[:, :width] = accx_ref[...].astype(bf16)
        dg = dg_ref[...]
        high = dg.astype(bf16).astype(f32)
        mid = (dg - high).astype(bf16).astype(f32)
        low = dg - high - mid
        spread = high + pltpu.roll(mid, 32, 1) + pltpu.roll(low, 64, 1)
        dx_ref[:, width:] = spread.astype(bf16)


def params(mb):
    return pltpu.CompilerParams(vmem_limit_bytes=mb * VMEM_MB)


def attend(x_all, gain, w_qkv, cos, sin, begin):
    total, width = x_all.shape
    shape = lambda w: jax.ShapeDtypeStruct((total, w), bf16)
    return pl.pallas_call(
        attend_kernel,
        out_shape=(shape(width), shape(LANES), shape(LANES), shape(LANES), shape(LANES)),
        compiler_params=params(48),
    )(x_all, gain, w_qkv, cos, sin, begin)


def attend_back(ag, wp_own, q, kk, vv, ctx, normed, x_all, cos, sin, begin, w_qkv):
    total, width = x_all.shape
    return pl.pallas_call(
        attend_back_kernel,
        out_shape=(
            jax.ShapeDtypeStruct((total, width), bf16),
            jax.ShapeDtypeStruct((width, 3 * LANES), bf16),
            jax.ShapeDtypeStruct((1, width), f32),
        ),
        scratch_shapes=[
            pltpu.VMEM((total, LANES), bf16),
            pltpu.VMEM((total, LANES), f32),
            pltpu.VMEM((total, LANES), f32),
            pltpu.VMEM((total, 2 * LANES), bf16),
        ],
        compiler_params=params(48),
    )(ag, wp_own, q, kk, vv, ctx, normed, x_all, cos, sin, begin, w_qkv)


def experts(base, x, dy, gates, weights, count):
    total, width = x.shape
    ff = weights.shape[1] // (3 * count)
    whole = lambda w: pl.BlockSpec((total, w), lambda e, b: (0, 0))
    grid_spec = pltpu.PrefetchScalarGridSpec(
        num_scalar_prefetch=1,
        grid=(count,),
        in_specs=[
            whole(width),
            whole(width),
            whole(LANES),
            pl.BlockSpec((width, 3 * ff), lambda e, b: (0, e)),
        ],
        out_specs=[
            whole(width),
            whole(width + LANES),
            pl.BlockSpec((width, 3 * ff), lambda e, b: (0, e)),
        ],
        scratch_shapes=[
            pltpu.VMEM((width, total), bf16),
            pltpu.VMEM((width, total), bf16),
            pltpu.VMEM((total, width), f32),
            pltpu.VMEM((total, width), f32),
            pltpu.VMEM((total, LANES), f32),
            pltpu.VMEM((total, ff), bf16),
            pltpu.VMEM((total, 2 * ff), bf16),
        ],
    )
    return pl.pallas_call(
        experts_kernel,
        grid_spec=grid_spec,
        out_shape=(
            jax.ShapeDtypeStruct((total, width), bf16),
            jax.ShapeDtypeStruct((total, width + LANES), bf16),
            jax.ShapeDtypeStruct((width, 3 * ff * count), bf16),
        ),
        compiler_params=params(58),
        cost_estimate=pl.CostEstimate(
            flops=18 * total * width * ff * count,
            bytes_accessed=4 * width * 3 * ff * count,
            transcendentals=total * ff * count,
        ),
    )(base, x, dy, gates, weights)


def tables(lengths_row, group):
    ends = jnp.cumsum(lengths_row)
    starts = ends - lengths_row
    places = jnp.arange(group, dtype=jnp.int32)
    inside = (places[:, None] >= starts[None, :]) & (places[:, None] < ends[None, :])
    begin = jnp.sum(jnp.where(inside, starts[None, :], 0), axis=1)
    frequency = BASE ** (-(jnp.arange(HEAD // 2, dtype=f32) * 2.0 / HEAD))
    angles = (places - begin).astype(f32)[:, None] * frequency[None, :]
    cos, sin = jnp.cos(angles), jnp.sin(angles)
    return (
        begin.reshape(1, group),
        jnp.concatenate([cos] * 4, axis=1),
        jnp.concatenate([-sin, sin, -sin, sin], axis=1),
    )


def local(
    layer_input, lengths, choices, query_weight, key_matrix, value_matrix, project_weight,
    gate_weight, up_weight, down_weight, router_weight, attention_gain, expert_gain, grad_output,
):
    me = lax.axis_index("col")
    tokens, width = layer_input.shape
    group = tokens * 8
    kinds = router_weight.shape[1]
    count, _, ff = gate_weight.shape
    own = lambda v: lax.dynamic_slice_in_dim(v, me * tokens, tokens, axis=0)

    share = jnp.stack(
        [jnp.moveaxis(gate_weight, 0, 1), jnp.moveaxis(up_weight, 0, 1), jnp.transpose(down_weight, (2, 0, 1))],
        axis=2,
    ).reshape(-1, count * 3 * ff)
    expert_weights = lax.all_gather(share, "row", axis=0, tiled=True)

    small = jnp.concatenate([query_weight, key_matrix, value_matrix, project_weight.T], axis=1)
    small = gather_row_small(small)
    w_qkv, wp_own = small[:, : 2 * LANES], small[:, 2 * LANES :]

    spots = jnp.arange(LANES, dtype=jnp.int32)
    named = jnp.any(choices[:, :, None] == spots[None, None, :], axis=1).astype(bf16)
    entering = gather_col(jnp.concatenate([layer_input, named], axis=1), 0)
    x_all, named_all = entering[:, :width], entering[:, width:]

    begin, cos, sin = tables(lengths[0], group)
    gain_one = attention_gain.reshape(1, width)
    normed, q, kk, vv, ctx = attend(x_all, gain_one, w_qkv, cos, sin, begin)
    wp_all = gather_col(wp_own, 1)
    ctx_all = gather_col(ctx, 1)
    dy_all = gather_col(grad_output, 0)

    attention = dot_nt(ctx_all, wp_all)
    middle_all = x_all.astype(f32) + RES * attention
    expert_in = rms_scale(middle_all, expert_gain).astype(bf16)
    middle = own(middle_all)
    router_wide = jnp.pad(router_weight, ((0, 0), (0, LANES - kinds)))
    logits = dot_nn(expert_in, router_wide)
    logits = jnp.where(named_all > 0, logits, -1e30)
    raised = jnp.exp(logits - jnp.max(logits, axis=1, keepdims=True))
    gates_all = raised / jnp.sum(raised, axis=1, keepdims=True)

    mix, dx, expert_wgrad = experts(
        (me * count).astype(jnp.int32).reshape(1), expert_in, dy_all, gates_all, expert_weights, count
    )
    expert_sum = lax.psum_scatter(expert_wgrad, "row", scatter_dimension=0, tiled=True)

    arrived = sum_col(dx)
    upstream = grad_output.astype(f32)
    gates = own(gates_all)[:, :kinds]
    spread = arrived[:, width:]
    gates_grad = spread[:, :kinds] + spread[:, kinds : 2 * kinds] + spread[:, 2 * kinds : 3 * kinds]
    logits_grad = gates * (gates_grad - jnp.sum(gates * gates_grad, axis=1, keepdims=True))
    expert_in_grad = arrived[:, :width] + lax.dot_general(
        logits_grad, router_weight.astype(f32), (((1,), (1,)), ((), ())), precision=lax.Precision.HIGHEST
    )
    router_part = lax.dot_general(
        logits_grad, own(expert_in).astype(f32), (((0,), (0,)), ((), ())), precision=lax.Precision.HIGHEST
    )
    _, second_back = jax.vjp(rms_scale, middle, expert_gain)
    middle_norm_grad, expert_gain_part = second_back(expert_in_grad)
    middle_grad = upstream + middle_norm_grad
    attention_grad = (RES * middle_grad).astype(bf16)
    ag_all = gather_col(attention_grad, 0)

    dn, attention_wgrad, gain_part = attend_back(
        ag_all, wp_own, q, kk, vv, ctx, normed, x_all, cos, sin, begin, w_qkv
    )
    normed_grad = sum_col(dn)
    _, first_back = jax.vjp(lambda v: rms_scale(v, attention_gain), layer_input.astype(f32))
    input_grad = middle_grad + first_back(normed_grad)[0]
    small_sum = sum_row_small(attention_wgrad)

    block_output = middle + RES * sum_col(mix)

    rows = jnp.concatenate([router_part, expert_gain_part.reshape(1, width)], axis=0)
    rows = sum_everywhere(rows)
    attention_gain_grad = sum_everywhere(gain_part)

    expert_sum = expert_sum.astype(f32).reshape(-1, count, 3, ff)
    return (
        block_output,
        input_grad,
        small_sum[:, :LANES],
        small_sum[:, LANES : LANES + HEAD],
        small_sum[:, LANES + HEAD : 2 * LANES],
        small_sum[:, 2 * LANES :].T,
        jnp.moveaxis(expert_sum[:, :, 0], 0, 1),
        jnp.moveaxis(expert_sum[:, :, 1], 0, 1),
        jnp.transpose(expert_sum[:, :, 2], (1, 2, 0)),
        rows[:kinds].T,
        attention_gain_grad.reshape(width),
        rows[kinds],
    )


def solution(mesh):
    both = P(("row", "col"), None)
    in_specs = (
        both, P("row", None), both, P("row", "col"), P("row", "col"), P("row", "col"), P("col", "row"),
        P("col", "row", None), P("col", "row", None), P("col", None, "row"), P(), P(), P(), both,
    )
    out_specs = (
        both, both, P("row", "col"), P("row", "col"), P("row", "col"), P("col", "row"),
        P("col", "row", None), P("col", "row", None), P("col", None, "row"), P(), P(), P(),
    )
    return jax.shard_map(local, mesh=mesh, in_specs=in_specs, out_specs=out_specs, check_vma=False)
```

```python
import functools

import jax
import jax.numpy as jnp
from jax import lax
from jax.experimental import pallas as pl
from jax.experimental.pallas import tpu as pltpu
from jax.sharding import PartitionSpec as P

HEAD = 64
LANES = 128
QB = 256
EPS = 1e-06
RES = 0.22
SCALE = 0.125
BASE = 10000.0
bf16 = jnp.bfloat16
f32 = jnp.float32
VMEM_MB = 1 << 20


def dot_nt(a, b):
    return lax.dot_general(a, b, (((1,), (1,)), ((), ())), preferred_element_type=f32)


def dot_nn(a, b):
    return lax.dot_general(a, b, (((1,), (0,)), ((), ())), preferred_element_type=f32)


def rms_scale(values, gain_vec):
    return values * lax.rsqrt(jnp.mean(values * values, axis=-1, keepdims=True) + EPS) * gain_vec


def core_swap(a):
    return lax.ppermute(a, "col", [(i, i ^ 1) for i in range(8)])


def z_shift(a, d):
    return lax.ppermute(a, "col", [(i, (i + 2 * d) % 8) for i in range(8)])


def y_shift(a, d):
    return lax.ppermute(a, "row", [(i, (i // 4) * 4 + (i + d) % 4) for i in range(16)])


def x_shift(a, d):
    return lax.ppermute(a, "row", [(i, (i + 4 * d) % 16) for i in range(16)])


def gather_col(a, at, beside=None):
    half = a.shape[0] // 2
    back = z_shift(a, 1)
    ahead = z_shift(a, -1)
    if beside is not None:
        back, ahead, beside = lax.optimization_barrier((back, ahead, beside))
    far0 = z_shift(back[:half], 1)
    far1 = z_shift(ahead[half:], -1)
    mine = pl.pallas_call(
        place_kernel,
        grid_spec=pltpu.PrefetchScalarGridSpec(
            num_scalar_prefetch=1,
            grid=(1,),
            in_specs=[whole(v) for v in (a, back, ahead, far0, far1)],
            out_specs=pl.BlockSpec((4,) + a.shape, lambda g, at: (0, 0, 0)),
        ),
        out_shape=jax.ShapeDtypeStruct((4,) + a.shape, a.dtype),
        compiler_params=params(32),
    )(at, a, back, ahead, far0, far1)
    return mine, core_swap(mine), beside


def sum_col(mine, theirs, beside=None, steps=()):
    steps = list(steps)
    half = mine.shape[1] // 2

    def phase(*values):
        nonlocal beside
        if steps:
            beside = steps.pop(0)(beside)
            values, beside = lax.optimization_barrier((values, beside))
        return values

    (got,) = phase(core_swap(theirs))
    total = mine.astype(f32) + got.astype(f32)
    far = total[2].astype(bf16)
    via_up, via_down = phase(z_shift(far[:half], 1), z_shift(far[half:], -1))
    up = jnp.concatenate([total[1, :half] + via_up.astype(f32), total[1, half:]], axis=0).astype(bf16)
    down = jnp.concatenate([total[3, :half], total[3, half:] + via_down.astype(f32)], axis=0).astype(bf16)
    up, down = phase(z_shift(up, 1), z_shift(down, -1))
    for step in steps:
        beside = step(beside)
    return total[0] + up.astype(f32) + down.astype(f32), beside


def gather_row_small(a):
    ways = lax.axis_size("row")
    sent = jnp.broadcast_to(a[None], (ways,) + a.shape)
    return lax.all_to_all(sent, "row", 0, 0, tiled=True).reshape(-1, a.shape[1])


def exchange_row(a):
    ways = lax.axis_size("row")
    return lax.all_to_all(a.reshape(ways, -1, a.shape[1]), "row", 0, 0, tiled=True)


def send_all(a, axis):
    sent = jnp.broadcast_to(a[None], (lax.axis_size(axis),) + a.shape)
    return lax.all_to_all(sent, axis, 0, 0, tiled=True)


def two_parts(v):
    high = v.astype(bf16)
    return high, (v - high.astype(f32)).astype(bf16)


def lane_of(shape):
    return lax.broadcasted_iota(jnp.int32, shape, 1)


def rotate(values, cos, sin):
    first = (lane_of(values.shape) % HEAD) < HEAD // 2
    swapped = jnp.where(first, pltpu.roll(values, 96, 1), pltpu.roll(values, 32, 1))
    return values * cos + swapped * sin


def allowed_keys(lo, count, row0, begin):
    key = lax.broadcasted_iota(jnp.int32, (count, QB), 0) + lo
    query = lax.broadcasted_iota(jnp.int32, (count, QB), 1) + row0
    return (key >= begin) & (key <= query)


def soft(kk, qh, ok):
    s = jnp.where(ok, dot_nt(kk, qh) * SCALE, -1e30)
    raised = jnp.exp(s - jnp.max(s, axis=0, keepdims=True))
    return raised / jnp.sum(raised, axis=0, keepdims=True)


def key_range(i):
    return max(0, i - 2) * QB, (i + 1) * QB


def whole(v):
    return pl.BlockSpec(v.shape, lambda g, at, r=len(v.shape): (0,) * r)


def place_kernel(at_ref, own_ref, back_ref, ahead_ref, far0_ref, far1_ref, out_ref):
    z = at_ref[0]
    half = own_ref.shape[0] // 2
    out_ref[z] = own_ref[...]
    out_ref[lax.rem(z + 3, 4)] = back_ref[...]
    out_ref[lax.rem(z + 1, 4)] = ahead_ref[...]
    out_ref[lax.rem(z + 2, 4), :half] = far0_ref[...]
    out_ref[lax.rem(z + 2, 4), half:] = far1_ref[...]


def merge_kernel(at_ref, mine_ref, other_ref, *refs):
    core = at_ref[1]
    for k in range(4):
        for src, c in ((mine_ref, core), (other_ref, 1 - core)):
            at = 0
            for ref in refs:
                w = ref.shape[-1]
                ref[k, c] = src[k, :, at : at + w]
                at += w


def merge(at, mine, other, widths):
    _, n, _ = mine.shape
    outs = [jax.ShapeDtypeStruct((4, 2, n, w), bf16) for w in widths]
    found = pl.pallas_call(
        merge_kernel,
        grid_spec=pltpu.PrefetchScalarGridSpec(
            num_scalar_prefetch=1,
            grid=(1,),
            in_specs=[whole(mine), whole(other)],
            out_specs=[whole(v) for v in outs],
        ),
        out_shape=outs,
        compiler_params=params(24),
    )(at, mine, other)
    return [v.reshape(8 * n, v.shape[-1]) for v in found]


def pack_kernel(g_ref, u_ref, d_ref, share_ref):
    count, _, ff = g_ref.shape
    for e in range(count):
        at = 3 * ff * e
        share_ref[:, at : at + ff] = g_ref[e]
        share_ref[:, at + ff : at + 2 * ff] = u_ref[e]
        share_ref[:, at + 2 * ff : at + 3 * ff] = d_ref[e]


def pack(gate, up, down):
    count, n, ff = gate.shape
    return pl.pallas_call(
        pack_kernel,
        out_shape=jax.ShapeDtypeStruct((n, 3 * ff * count), bf16),
        compiler_params=params(32),
    )(gate, up, jnp.swapaxes(down, 1, 2))


def unpack_kernel(s_ref, g_ref, u_ref, d_ref):
    count, _, ff = g_ref.shape
    for e in range(count):
        at = 3 * ff * e
        g_ref[e] = s_ref[:, at : at + ff].astype(f32)
        u_ref[e] = s_ref[:, at + ff : at + 2 * ff].astype(f32)
        d_ref[e] = s_ref[:, at + 2 * ff : at + 3 * ff].astype(f32)


def unpack(share, count, ff):
    n = share.shape[0]
    block = jax.ShapeDtypeStruct((count, n, ff), f32)
    gate, up, down = pl.pallas_call(
        unpack_kernel,
        out_shape=(block, block, block),
        compiler_params=params(32),
    )(share)
    return gate, up, jnp.swapaxes(down, 1, 2)


def project_kernel(
    at_ref, mine_ref, other_ref, x_ref, named_ref, gain_ref, router_ref, in_ref, gates_ref, own_ref, ctx_ref, wp_ref
):
    core = at_ref[1]
    total, width = x_ref.shape
    for k in range(4):
        for src, c in ((mine_ref, core), (other_ref, 1 - core)):
            lanes = pl.ds(pl.multiple_of((2 * k + c) * LANES, LANES), LANES)
            ctx_ref[:, lanes] = src[k, :total]
            wp_ref[:, lanes] = src[k, total:]
    me = 2 * at_ref[0] + core
    tokens = own_ref.shape[0]
    for i in range(total // QB):
        rows = pl.ds(i * QB, QB)
        middle = x_ref[rows, :].astype(f32) + RES * dot_nt(ctx_ref[rows, :], wp_ref[...])
        for half in range(QB // tokens):

            @pl.when(me == i * (QB // tokens) + half)
            def _():
                own_ref[...] = middle[half * tokens : (half + 1) * tokens]

        normed = rms_scale(middle, gain_ref[...]).astype(bf16)
        in_ref[rows, :] = normed
        logits = jnp.where(named_ref[rows, :] > 0, dot_nn(normed, router_ref[...]), -1e30)
        raised = jnp.exp(logits - jnp.max(logits, axis=1, keepdims=True))
        gates_ref[rows, :] = raised / jnp.sum(raised, axis=1, keepdims=True)


def project(at, mine, other, x, named, gain, router):
    total, width = x.shape
    outs = (
        jax.ShapeDtypeStruct((total, width), bf16),
        jax.ShapeDtypeStruct((total, LANES), f32),
        jax.ShapeDtypeStruct((total // 8, width), f32),
    )
    ins = (mine, other, x, named, gain, router)
    return pl.pallas_call(
        project_kernel,
        grid_spec=pltpu.PrefetchScalarGridSpec(
            num_scalar_prefetch=1,
            grid=(1,),
            in_specs=[whole(v) for v in ins],
            out_specs=[whole(v) for v in outs],
            scratch_shapes=[pltpu.VMEM((total, width), bf16), pltpu.VMEM((total, width), bf16)],
        ),
        out_shape=outs,
        compiler_params=params(32),
    )(at, *ins)


def split_blocks(at_ref, value_of, mine_ref, theirs_ref, n):
    z, core = at_ref[0], at_ref[1]
    for k in range(4):
        there = lax.rem(z + k, 4) * 2
        for ref, c in ((mine_ref, core), (theirs_ref, 1 - core)):
            value_of(ref, k, pl.ds(pl.multiple_of((there + c) * n, n), n))


def attend_kernel(x_ref, gain_ref, w_ref, cos_ref, sin_ref, begin_ref, n_ref, q_ref, kk_ref, vv_ref, heads_ref):
    total = x_ref.shape[0]
    left = lane_of((QB, LANES)) < HEAD
    for i in range(total // QB):
        rows = pl.ds(i * QB, QB)
        x = x_ref[rows, :].astype(f32)
        normed = rms_scale(x, gain_ref[...]).astype(bf16)
        n_ref[rows, :] = normed
        raw = dot_nn(normed, w_ref[:, : 2 * LANES])
        cos, sin = cos_ref[rows, :], sin_ref[rows, :]
        q_ref[rows, :] = rotate(raw[:, :LANES], cos, sin).astype(bf16)
        kv = raw[:, LANES:]
        turned = rotate(kv, cos, sin)
        kk_ref[rows, :] = jnp.where(left, turned, pltpu.roll(turned, HEAD, 1)).astype(bf16)
        vv_ref[rows, :] = jnp.where(left, pltpu.roll(kv, HEAD, 1), kv).astype(bf16)
    vt = vv_ref[...].astype(f32).T.astype(bf16)
    upper = lax.broadcasted_iota(jnp.int32, (LANES, QB), 0) < HEAD
    for i in range(total // QB):
        rows = pl.ds(i * QB, QB)
        lo, hi = key_range(i)
        keys = kk_ref[lo:hi, :]
        ok = allowed_keys(lo, hi - lo, i * QB, begin_ref[:, i * QB : (i + 1) * QB])
        found = []
        for h in range(2):
            qh = jnp.where(left == (h == 0), q_ref[rows, :], jnp.zeros((QB, LANES), bf16))
            p = soft(keys, qh, ok).astype(bf16)
            found.append(dot_nn(vt[:, lo:hi], p))
        heads_ref[rows, :] = jnp.where(upper, found[0], found[1]).T.astype(bf16)
    heads_ref[total:, :] = w_ref[:, 2 * LANES :]


def attend_back_kernel(
    at_ref, ag_ref, q_ref, kk_ref, vv_ref, heads_ref, x_ref, cos_ref, sin_ref, begin_ref, w_ref,
    mine_ref, theirs_ref, gain_ref, dqkv_ref, dctx_ref, dk_ref, dv_ref, dn_ref,
):
    total = ag_ref.shape[0]
    left = lane_of((QB, LANES)) < HEAD
    upper = lax.broadcasted_iota(jnp.int32, (LANES, QB), 0) < HEAD
    dctx_ref[...] = dot_nn(ag_ref[...], heads_ref[total:, :]).astype(bf16)
    dk_ref[...] = jnp.zeros_like(dk_ref)
    dv_ref[...] = jnp.zeros_like(dv_ref)
    kt = kk_ref[...].astype(f32).T.astype(bf16)
    for i in range(total // QB):
        rows = pl.ds(i * QB, QB)
        lo, hi = key_range(i)
        keys = kk_ref[lo:hi, :]
        ok = allowed_keys(lo, hi - lo, i * QB, begin_ref[:, i * QB : (i + 1) * QB])
        found = []
        for h in range(2):
            mine = left == (h == 0)
            qh = jnp.where(mine, q_ref[rows, :], jnp.zeros((QB, LANES), bf16))
            dch = jnp.where(mine, dctx_ref[rows, :], jnp.zeros((QB, LANES), bf16))
            p = soft(keys, qh, ok)
            dp = dot_nt(vv_ref[lo:hi, :], dch)
            ds = (p * (dp - jnp.sum(dp * p, axis=0, keepdims=True))).astype(bf16)
            dk_ref[lo:hi, :] += dot_nn(ds, qh)
            dv_ref[lo:hi, :] += dot_nn(p.astype(bf16), dch)
            found.append(dot_nn(kt[:, lo:hi], ds))
        dq = jnp.where(upper, found[0], found[1]).T * SCALE
        dqkv_ref[rows, :LANES] = rotate(dq, cos_ref[rows, :], -sin_ref[rows, :]).astype(bf16)
    acc = jnp.zeros((1, x_ref.shape[1]), f32)
    for i in range(total // QB):
        rows = pl.ds(i * QB, QB)
        dk, dv = dk_ref[rows, :], dv_ref[rows, :]
        dk = (dk + pltpu.roll(dk, HEAD, 1)) * SCALE
        dk = rotate(dk, cos_ref[rows, :], -sin_ref[rows, :])
        dv = dv + pltpu.roll(dv, HEAD, 1)
        dqkv_ref[rows, LANES:] = jnp.where(left, dk, dv).astype(bf16)
        dn = dot_nt(dqkv_ref[rows, :], w_ref[:, : 2 * LANES])
        dn_ref[rows, :] = dn.astype(bf16)
        x = x_ref[rows, :].astype(f32)
        hat = x * lax.rsqrt(jnp.mean(x * x, axis=-1, keepdims=True) + EPS)
        acc = acc + jnp.sum(dn * hat, axis=0, keepdims=True)
    gain_ref[...] = acc

    def give(ref, k, rows):
        ref[k] = dn_ref[rows, :]

    split_blocks(at_ref, give, mine_ref, theirs_ref, mine_ref.shape[1])


def attend_weights_kernel(dqkv_ref, normed_ref, heads_ref, ag_ref, in_ref, dl_ref, gains_ref, wg_ref):
    total = ag_ref.shape[0]
    dqkv_t = dqkv_ref[...].astype(f32).T.astype(bf16)
    ctx_t = heads_ref[:total, :].astype(f32).T.astype(bf16)
    wg_ref[:, : 2 * LANES] = dot_nn(dqkv_t, normed_ref[...]).T.astype(bf16)
    wg_ref[:, 2 * LANES : 3 * LANES] = dot_nn(ctx_t, ag_ref[...]).T.astype(bf16)
    dl_t = dl_ref[...].astype(f32).T.astype(bf16)
    parts = dot_nn(dl_t, in_ref[...])
    rows = parts[:HEAD] + parts[HEAD:]
    width = rows.shape[1]
    place = lax.broadcasted_iota(jnp.int32, (HEAD, width), 0)
    rows = jnp.where(place == 32, gains_ref[0:1, :], jnp.where(place == 33, gains_ref[1:2, :], rows))
    high = rows.astype(bf16).astype(f32)
    both = jnp.concatenate([high, rows - high], axis=0)
    wg_ref[:, 3 * LANES :] = both.T.astype(bf16)


def experts_kernel(
    at_ref, x_ref, dy_ref, gates_ref, w_ref, mine_ref, theirs_ref, acts_ref, accm_ref, accx_ref, dg_ref
):
    e = pl.program_id(0)
    ff = acts_ref.shape[1] // 3
    total = x_ref.shape[0]
    lane = lane_of((total, LANES))
    pick = (2 * at_ref[0] + at_ref[1]) * pl.num_programs(0) + e

    @pl.when(e == 0)
    def _():
        accm_ref[...] = jnp.zeros_like(accm_ref)
        accx_ref[...] = jnp.zeros_like(accx_ref)
        dg_ref[...] = jnp.zeros_like(dg_ref)

    gu = dot_nn(x_ref[...], w_ref[:, : 2 * ff])
    h0 = dot_nn(dy_ref[...], w_ref[:, 2 * ff :]) * RES
    g, u = gu[:, :ff], gu[:, ff:]
    gate = jnp.sum(jnp.where(lane == pick, gates_ref[...], 0.0), axis=1, keepdims=True)
    sg = jax.nn.sigmoid(g)
    sw = g * sg
    hid = sw * u
    dg = jnp.sum(hid * h0, axis=1, keepdims=True)
    dg_ref[...] += jnp.where(lane == pick, dg, 0.0)
    acts_ref[:, 2 * ff :] = (gate * hid).astype(bf16)
    dh = gate * h0
    acts_ref[:, :ff] = (dh * u * sg * (1.0 + g * (1.0 - sg))).astype(bf16)
    acts_ref[:, ff : 2 * ff] = (dh * sw).astype(bf16)
    accm_ref[...] += dot_nt(acts_ref[:, 2 * ff :], w_ref[:, 2 * ff :])
    accx_ref[...] += dot_nt(acts_ref[:, : 2 * ff], w_ref[:, : 2 * ff])

    @pl.when(e == pl.num_programs(0) - 1)
    def _():
        width = accx_ref.shape[1]
        dg = dg_ref[...]
        high = dg.astype(bf16).astype(f32)
        mid = (dg - high).astype(bf16).astype(f32)
        low = dg - high - mid
        dg_ref[...] = high + pltpu.roll(mid, 32, 1) + pltpu.roll(low, 64, 1)

        def give(ref, k, rows):
            ref[k, :, :width] = accx_ref[rows, :].astype(bf16)
            ref[k, :, width : 2 * width] = accm_ref[rows, :].astype(bf16)
            ref[k, :, 2 * width :] = dg_ref[rows, :].astype(bf16)

        split_blocks(at_ref, give, mine_ref, theirs_ref, mine_ref.shape[1])


def weights_kernel(x_ref, dy_ref, acts_ref, *refs):
    out_ref, turned_ref = refs[-2:]
    step = pl.program_id(0)

    @pl.when(step == 0)
    def _():
        turned_ref[0] = x_ref[...].T
        turned_ref[1] = dy_ref[...].T

    is_down = lax.rem(step, 3) == 2
    found = dot_nn(turned_ref[jnp.where(is_down, 1, 0)], acts_ref[...])
    out_ref[...] = (found * jnp.where(is_down, RES, 1.0)).astype(bf16)


def params(mb):
    return pltpu.CompilerParams(vmem_limit_bytes=mb * VMEM_MB)


def attend(x_all, gain, weights, cos, sin, begin):
    total, width = x_all.shape
    shape = lambda n, w: jax.ShapeDtypeStruct((n, w), bf16)
    one = shape(total, LANES)
    return pl.pallas_call(
        attend_kernel,
        out_shape=(shape(total, width), one, one, one, shape(total + width, LANES)),
        compiler_params=params(32),
    )(x_all, gain, weights, cos, sin, begin)


def attend_back(at, *ins):
    total, width = ins[0].shape
    block = jax.ShapeDtypeStruct((4, total // 8, width), bf16)
    outs = (
        block,
        block,
        jax.ShapeDtypeStruct((1, width), f32),
        jax.ShapeDtypeStruct((total, 2 * LANES), bf16),
    )
    return pl.pallas_call(
        attend_back_kernel,
        grid_spec=pltpu.PrefetchScalarGridSpec(
            num_scalar_prefetch=1,
            grid=(1,),
            in_specs=[whole(v) for v in ins],
            out_specs=[whole(v) for v in outs],
            scratch_shapes=[
                pltpu.VMEM((total, LANES), bf16),
                pltpu.VMEM((total, LANES), f32),
                pltpu.VMEM((total, LANES), f32),
                pltpu.VMEM((total, width), bf16),
            ],
        ),
        out_shape=outs,
        compiler_params=params(32),
    )(at, *ins)


def attend_weights(*ins):
    width = ins[3].shape[1]
    return pl.pallas_call(
        attend_weights_kernel,
        out_shape=jax.ShapeDtypeStruct((width, 4 * LANES), bf16),
        compiler_params=params(24),
    )(*ins)


def experts(at, x, dy, gates, weights, count):
    total, width = x.shape
    ff = weights.shape[1] // (3 * count)
    block = jax.ShapeDtypeStruct((4, total // 8, 2 * width + LANES), bf16)
    each = lambda rows, w: pl.BlockSpec((rows, w), lambda e, at: (0, e))
    return pl.pallas_call(
        experts_kernel,
        grid_spec=pltpu.PrefetchScalarGridSpec(
            num_scalar_prefetch=1,
            grid=(count,),
            in_specs=[whole(x), whole(dy), whole(gates), each(width, 3 * ff)],
            out_specs=[whole(block), whole(block), each(total, 3 * ff)],
            scratch_shapes=[
                pltpu.VMEM((total, width), f32),
                pltpu.VMEM((total, width), f32),
                pltpu.VMEM((total, LANES), f32),
            ],
        ),
        out_shape=(
            block,
            block,
            jax.ShapeDtypeStruct((total, 3 * ff * count), bf16),
        ),
        compiler_params=params(58),
        cost_estimate=pl.CostEstimate(
            flops=12 * total * width * ff * count,
            bytes_accessed=4 * width * 3 * ff * count,
            transcendentals=total * ff * count,
        ),
    )(at, x, dy, gates, weights)


def expert_weights_grad(x, dy, acts, filled, first, count, all_of):
    total, width = x.shape
    ff = acts.shape[1] // (3 * all_of)
    each = lambda rows: pl.BlockSpec((rows, ff), lambda s: (0, 3 * first + s))
    fixed = pl.BlockSpec((total, width), lambda s: (0, 0))
    ins = [x, dy, acts]
    in_specs = [fixed, fixed, each(total)]
    if filled is not None:
        ins.append(filled)
        in_specs.append(pl.BlockSpec(memory_space=pl.ANY))
    return pl.pallas_call(
        weights_kernel,
        grid=(3 * count,),
        in_specs=in_specs,
        out_specs=each(width),
        out_shape=jax.ShapeDtypeStruct((width, 3 * ff * all_of), bf16),
        scratch_shapes=[pltpu.VMEM((2, width, total), bf16)],
        input_output_aliases={} if filled is None else {3: 0},
        compiler_params=params(32),
        cost_estimate=pl.CostEstimate(
            flops=6 * total * width * ff * count,
            bytes_accessed=4 * width * 3 * ff * count,
            transcendentals=0,
        ),
    )(*ins)


def tables(lengths_row, group):
    ends = jnp.cumsum(lengths_row)
    starts = ends - lengths_row
    places = jnp.arange(group, dtype=jnp.int32)
    inside = (places[:, None] >= starts[None, :]) & (places[:, None] < ends[None, :])
    begin = jnp.sum(jnp.where(inside, starts[None, :], 0), axis=1)
    frequency = BASE ** (-(jnp.arange(HEAD // 2, dtype=f32) * 2.0 / HEAD))
    angles = (places - begin).astype(f32)[:, None] * frequency[None, :]
    cos, sin = jnp.cos(angles), jnp.sin(angles)
    return (
        begin.reshape(1, group),
        jnp.concatenate([cos] * 4, axis=1),
        jnp.concatenate([-sin, sin, -sin, sin], axis=1),
    )


def local(
    layer_input, lengths, choices, query_weight, key_matrix, value_matrix, project_weight,
    gate_weight, up_weight, down_weight, router_weight, attention_gain, expert_gain, grad_output,
):
    me = lax.axis_index("col")
    tokens, width = layer_input.shape
    group = tokens * 8
    kinds = router_weight.shape[1]
    count, _, ff = gate_weight.shape
    own = lambda v: lax.dynamic_slice_in_dim(v, me * tokens, tokens, axis=0)

    at = jnp.stack([me // 2, me % 2]).astype(jnp.int32)
    spots = jnp.arange(LANES, dtype=jnp.int32)
    named = jnp.any(choices[:, :, None] == spots[None, None, :], axis=1).astype(bf16)
    share = pack(gate_weight, up_weight, down_weight)
    expert_weights = lax.all_gather(share, "row", axis=0, tiled=True)
    small = gather_row_small(
        jnp.concatenate([query_weight, key_matrix, value_matrix, project_weight.T], axis=1)
    )
    *entering, small = gather_col(jnp.concatenate([layer_input, grad_output, named], axis=1), at, small)
    x_all, dy_all, named_all = merge(at, *entering, (width, width, LANES))

    begin, cos, sin = tables(lengths[0], group)
    gain_one = attention_gain.reshape(1, width)
    normed, q, kk, vv, heads = attend(x_all, gain_one, small, cos, sin, begin)
    heads_mine, heads_other, _ = gather_col(heads, at)
    router_wide = jnp.pad(router_weight, ((0, 0), (0, LANES - kinds)))
    expert_in, gates_all, middle = project(
        at, heads_mine, heads_other, x_all, named_all, expert_gain.reshape(1, width), router_wide
    )

    mine, theirs, acts = experts(at, expert_in, dy_all, gates_all, expert_weights, count)

    def piece(first, number):
        return lambda filled: expert_weights_grad(
            expert_in, dy_all, acts, filled, first, number, count
        )

    arrived, expert_wgrad = sum_col(mine, theirs, None, [piece(0, 1), piece(1, 1), piece(2, 2)])
    expert_sum = lax.psum_scatter(expert_wgrad, "row", scatter_dimension=0, tiled=True)

    upstream = grad_output.astype(f32)
    gates = own(gates_all)[:, :kinds]
    spread = arrived[:, 2 * width :]
    block_output = middle + RES * arrived[:, width : 2 * width]
    gates_grad = spread[:, :kinds] + spread[:, kinds : 2 * kinds] + spread[:, 2 * kinds : 3 * kinds]
    logits_grad = gates * (gates_grad - jnp.sum(gates * gates_grad, axis=1, keepdims=True))
    expert_in_grad = arrived[:, :width] + lax.dot_general(
        logits_grad, router_weight.astype(f32), (((1,), (1,)), ((), ())), precision=lax.Precision.HIGHEST
    )
    _, second_back = jax.vjp(rms_scale, middle, expert_gain)
    middle_norm_grad, expert_gain_part = second_back(expert_in_grad)
    middle_grad = upstream + middle_norm_grad
    attention_grad = (RES * middle_grad).astype(bf16)
    high, low = two_parts(logits_grad)
    logits_sent = jnp.concatenate(
        [jnp.pad(high, ((0, 0), (0, HEAD - kinds))), jnp.pad(low, ((0, 0), (0, HEAD - kinds)))], axis=1
    )
    back_mine, back_other, _ = gather_col(jnp.concatenate([attention_grad, logits_sent], axis=1), at)
    ag_all, logits_all = merge(at, back_mine, back_other, (width, LANES))

    dn_mine, dn_theirs, gain_part, dqkv = attend_back(
        at, ag_all, q, kk, vv, heads, x_all, cos, sin, begin, small
    )
    gains = jnp.concatenate([expert_gain_part.reshape(1, width), gain_part], axis=0)

    def opening(_):
        return attend_weights(dqkv, normed, heads, ag_all, expert_in, logits_all, gains)

    normed_grad, pieces = sum_col(dn_mine, dn_theirs, None, [opening, exchange_row])
    small_sum = jnp.sum(pieces.astype(f32), axis=0)
    extra = small_sum[:, 3 * LANES :]
    extra = extra[:, :HEAD] + extra[:, HEAD:]
    extra = send_all(jnp.concatenate(two_parts(extra), axis=1), "row").astype(f32)
    extra = (extra[:, :, :HEAD] + extra[:, :, HEAD:]).reshape(width, HEAD)
    gains = extra[:, kinds : kinds + 2]
    gains = send_all(jnp.concatenate(two_parts(gains.T), axis=0), "col").astype(f32)
    gains = jnp.sum(gains, axis=0)
    gains = gains[:2] + gains[2:]
    _, first_back = jax.vjp(lambda v: rms_scale(v, attention_gain), layer_input.astype(f32))
    input_grad = middle_grad + first_back(normed_grad)[0]

    gate_grad, up_grad, down_grad = unpack(expert_sum, count, ff)
    return (
        block_output,
        input_grad,
        small_sum[:, :LANES],
        small_sum[:, LANES : LANES + HEAD],
        small_sum[:, LANES + HEAD : 2 * LANES],
        small_sum[:, 2 * LANES : 3 * LANES].T,
        gate_grad,
        up_grad,
        down_grad,
        extra[:, :kinds],
        gains[1],
        gains[0],
    )


def solution(mesh):
    both = P(("row", "col"), None)
    in_specs = (
        both, P("row", None), both, P("row", "col"), P("row", "col"), P("row", "col"), P("col", "row"),
        P("col", "row", None), P("col", "row", None), P("col", None, "row"), P(), P(), P(), both,
    )
    out_specs = (
        both, both, P("row", "col"), P("row", "col"), P("row", "col"), P("col", "row"),
        P("col", "row", None), P("col", "row", None), P("col", None, "row"), P(), P(), P(),
    )
    return jax.shard_map(local, mesh=mesh, in_specs=in_specs, out_specs=out_specs, check_vma=False)
```

```python
import functools

import jax
import jax.numpy as jnp
from jax import lax
from jax.experimental import pallas as pl
from jax.experimental.pallas import tpu as pltpu
from jax.sharding import PartitionSpec as P

HEAD = 64
LANES = 128
QB = 256
EPS = 1e-06
RES = 0.22
SCALE = 0.125
BASE = 10000.0
bf16 = jnp.bfloat16
f32 = jnp.float32
VMEM_MB = 1 << 20


def dot_nt(a, b):
    return lax.dot_general(a, b, (((1,), (1,)), ((), ())), preferred_element_type=f32)


def dot_nn(a, b):
    return lax.dot_general(a, b, (((1,), (0,)), ((), ())), preferred_element_type=f32)


def rms_scale(values, gain_vec):
    return values * lax.rsqrt(jnp.mean(values * values, axis=-1, keepdims=True) + EPS) * gain_vec


def core_swap(a):
    return lax.ppermute(a, "col", [(i, i ^ 1) for i in range(8)])


def z_shift(a, d):
    return lax.ppermute(a, "col", [(i, (i + 2 * d) % 8) for i in range(8)])


def y_shift(a, d):
    return lax.ppermute(a, "row", [(i, (i // 4) * 4 + (i + d) % 4) for i in range(16)])


def x_shift(a, d):
    return lax.ppermute(a, "row", [(i, (i + 4 * d) % 16) for i in range(16)])


def gather_col(a, at, beside=None):
    half = a.shape[0] // 2
    back = z_shift(a, 1)
    ahead = z_shift(a, -1)
    if beside is not None:
        back, ahead, beside = lax.optimization_barrier((back, ahead, beside))
    far0 = z_shift(back[:half], 1)
    far1 = z_shift(ahead[half:], -1)
    mine = pl.pallas_call(
        place_kernel,
        grid_spec=pltpu.PrefetchScalarGridSpec(
            num_scalar_prefetch=1,
            grid=(1,),
            in_specs=[whole(v) for v in (a, back, ahead, far0, far1)],
            out_specs=pl.BlockSpec((4,) + a.shape, lambda g, at: (0, 0, 0)),
        ),
        out_shape=jax.ShapeDtypeStruct((4,) + a.shape, a.dtype),
        compiler_params=params(24),
    )(at, a, back, ahead, far0, far1)
    return mine, core_swap(mine), beside


def sum_col(mine, theirs, beside=None, steps=()):
    steps = list(steps)

    def phase(*values):
        nonlocal beside
        if steps:
            beside = steps.pop(0)(beside)
            values, beside = lax.optimization_barrier((values, beside))
        return values

    (got,) = phase(core_swap(theirs))
    own, ahead, behind, far0, far1 = fold(mine, got)
    via_up, via_down = phase(z_shift(far0, 1), z_shift(far1, -1))
    up, down = join(ahead, behind, via_up, via_down)
    up, down = phase(z_shift(up, 1), z_shift(down, -1))
    return (own, up, down), beside


def gather_row_small(a):
    ways = lax.axis_size("row")
    sent = jnp.broadcast_to(a[None], (ways,) + a.shape)
    return lax.all_to_all(sent, "row", 0, 0, tiled=True).reshape(-1, a.shape[1])


def exchange_row(a):
    ways = lax.axis_size("row")
    return lax.all_to_all(a.reshape(ways, -1, a.shape[1]), "row", 0, 0, tiled=True)


def send_all(a, axis):
    sent = jnp.broadcast_to(a[None], (lax.axis_size(axis),) + a.shape)
    return lax.all_to_all(sent, axis, 0, 0, tiled=True)


def two_parts(v):
    high = v.astype(bf16)
    return high, (v - high.astype(f32)).astype(bf16)


def row_step(v, bit):
    low = v.astype(bf16)
    got = lax.ppermute(low, "row", [(i, i ^ bit) for i in range(16)])
    return low.astype(f32) + got.astype(f32)


def lane_of(shape):
    return lax.broadcasted_iota(jnp.int32, shape, 1)


def rotate(values, cos, sin):
    first = (lane_of(values.shape) % HEAD) < HEAD // 2
    swapped = jnp.where(first, pltpu.roll(values, 96, 1), pltpu.roll(values, 32, 1))
    return values * cos + swapped * sin


def allowed_keys(lo, count, row0, begin):
    key = lax.broadcasted_iota(jnp.int32, (count, QB), 0) + lo
    query = lax.broadcasted_iota(jnp.int32, (count, QB), 1) + row0
    return (key >= begin) & (key <= query)


def soft(kk, qh, ok):
    s = jnp.where(ok, dot_nt(kk, qh) * SCALE, -1e30)
    raised = jnp.exp(s - jnp.max(s, axis=0, keepdims=True))
    return raised / jnp.sum(raised, axis=0, keepdims=True)


def key_range(i):
    return max(0, i - 2) * QB, (i + 1) * QB


def whole(v):
    return pl.BlockSpec(v.shape, lambda g, at, r=len(v.shape): (0,) * r)


def fold_kernel(mine_ref, got_ref, own_ref, ahead_ref, behind_ref, far0_ref, far1_ref):
    half = far0_ref.shape[0]
    add = lambda k, rows: mine_ref[k, rows].astype(f32) + got_ref[k, rows].astype(f32)
    every = slice(None)
    own_ref[...] = add(0, every)
    ahead_ref[...] = add(1, every)
    behind_ref[...] = add(3, every)
    far0_ref[...] = add(2, slice(0, half)).astype(bf16)
    far1_ref[...] = add(2, slice(half, 2 * half)).astype(bf16)


def fold(mine, got):
    _, n, w = mine.shape
    one = jax.ShapeDtypeStruct((n, w), f32)
    part = jax.ShapeDtypeStruct((n // 2, w), bf16)
    return pl.pallas_call(
        fold_kernel, out_shape=(one, one, one, part, part), compiler_params=params(24)
    )(mine, got)


def join_kernel(ahead_ref, behind_ref, via_up_ref, via_down_ref, up_ref, down_ref):
    half = via_up_ref.shape[0]
    up_ref[:half] = (ahead_ref[:half] + via_up_ref[...].astype(f32)).astype(bf16)
    up_ref[half:] = ahead_ref[half:].astype(bf16)
    down_ref[:half] = behind_ref[:half].astype(bf16)
    down_ref[half:] = (behind_ref[half:] + via_down_ref[...].astype(f32)).astype(bf16)


def join(ahead, behind, via_up, via_down):
    one = jax.ShapeDtypeStruct(ahead.shape, bf16)
    return pl.pallas_call(join_kernel, out_shape=(one, one), compiler_params=params(24))(
        ahead, behind, via_up, via_down
    )


def norm_back(x, grad, gain):
    inv = lax.rsqrt(jnp.mean(x * x, axis=-1, keepdims=True) + EPS)
    scaled = grad * gain
    hat = x * inv
    return inv * (scaled - hat * jnp.mean(hat * scaled, axis=-1, keepdims=True)), hat


def turn_kernel(
    own_ref, up_ref, down_ref, middle_ref, gates_ref, grad_ref, gain_ref, router_ref,
    block_ref, back_ref, sent_ref, gain_part_ref,
):
    width = middle_ref.shape[1]
    arrived = own_ref[...] + up_ref[...].astype(f32) + down_ref[...].astype(f32)
    middle = middle_ref[...]
    block_ref[...] = middle + RES * arrived[:, width : 2 * width]
    parts = arrived[:, 2 * width :]
    gates_grad = parts + pltpu.roll(parts, 96, 1) + pltpu.roll(parts, 64, 1)
    gates = gates_ref[...]
    logits_grad = gates * (gates_grad - jnp.sum(gates * gates_grad, axis=1, keepdims=True))
    high = logits_grad.astype(bf16)
    rest = logits_grad - high.astype(f32)
    low = rest.astype(bf16)
    router = widened(router_ref[...])
    grad = arrived[:, :width] + dot_nn(high, router) + dot_nn(low, router)
    back, hat = norm_back(middle, grad, gain_ref[...])
    back = grad_ref[...].astype(f32) + back
    back_ref[...] = back
    sent_ref[:, :width] = (RES * back).astype(bf16)
    sent_ref[:, width:] = (high.astype(f32) + pltpu.roll(low.astype(f32), HEAD, 1)).astype(bf16)
    gain_part_ref[...] = jnp.sum(grad * hat, axis=0, keepdims=True)


def turn(own, up, down, middle, gates, grad, gain, router):
    n, width = middle.shape
    return pl.pallas_call(
        turn_kernel,
        out_shape=(
            jax.ShapeDtypeStruct((n, width), f32),
            jax.ShapeDtypeStruct((n, width), f32),
            jax.ShapeDtypeStruct((n, width + LANES), bf16),
            jax.ShapeDtypeStruct((1, width), f32),
        ),
        compiler_params=params(24),
    )(own, up, down, middle, gates, grad, gain, router)


def close_kernel(own_ref, up_ref, down_ref, x_ref, back_ref, gain_ref, out_ref):
    grad = own_ref[...] + up_ref[...].astype(f32) + down_ref[...].astype(f32)
    out_ref[...] = back_ref[...] + norm_back(x_ref[...].astype(f32), grad, gain_ref[...])[0]


def close(own, up, down, x, back, gain):
    return pl.pallas_call(
        close_kernel, out_shape=jax.ShapeDtypeStruct(own.shape, f32), compiler_params=params(24)
    )(own, up, down, x, back, gain)


def place_kernel(at_ref, own_ref, back_ref, ahead_ref, far0_ref, far1_ref, out_ref):
    z = at_ref[0]
    half = own_ref.shape[0] // 2
    out_ref[z] = own_ref[...]
    out_ref[lax.rem(z + 3, 4)] = back_ref[...]
    out_ref[lax.rem(z + 1, 4)] = ahead_ref[...]
    out_ref[lax.rem(z + 2, 4), :half] = far0_ref[...]
    out_ref[lax.rem(z + 2, 4), half:] = far1_ref[...]


def merge_kernel(at_ref, mine_ref, other_ref, *refs):
    core = at_ref[1]
    for k in range(4):
        for src, c in ((mine_ref, core), (other_ref, 1 - core)):
            at = 0
            for ref in refs:
                w = ref.shape[-1]
                ref[k, c] = src[k, :, at : at + w]
                at += w


def merge(at, mine, other, widths):
    _, n, _ = mine.shape
    outs = [jax.ShapeDtypeStruct((4, 2, n, w), bf16) for w in widths]
    found = pl.pallas_call(
        merge_kernel,
        grid_spec=pltpu.PrefetchScalarGridSpec(
            num_scalar_prefetch=1,
            grid=(1,),
            in_specs=[whole(mine), whole(other)],
            out_specs=[whole(v) for v in outs],
        ),
        out_shape=outs,
        compiler_params=params(24),
    )(at, mine, other)
    return [v.reshape(8 * n, v.shape[-1]) for v in found]


def pack_kernel(g_ref, u_ref, d_ref, share_ref):
    count, _, ff = g_ref.shape
    for e in range(count):
        at = 3 * ff * e
        share_ref[:, at : at + ff] = g_ref[e]
        share_ref[:, at + ff : at + 2 * ff] = u_ref[e]
        share_ref[:, at + 2 * ff : at + 3 * ff] = d_ref[e]


def pack(gate, up, down):
    count, n, ff = gate.shape
    return pl.pallas_call(
        pack_kernel,
        out_shape=jax.ShapeDtypeStruct((n, 3 * ff * count), bf16),
        compiler_params=params(60),
    )(gate, up, jnp.swapaxes(down, 1, 2))


def unpack_kernel(s_ref, g_ref, u_ref, d_ref):
    count, _, ff = g_ref.shape
    for e in range(count):
        at = 3 * ff * e
        g_ref[e] = s_ref[:, at : at + ff].astype(f32)
        u_ref[e] = s_ref[:, at + ff : at + 2 * ff].astype(f32)
        d_ref[e] = s_ref[:, at + 2 * ff : at + 3 * ff].astype(f32)


def unpack(share, count, ff):
    n = share.shape[0]
    block = jax.ShapeDtypeStruct((count, n, ff), f32)
    gate, up, down = pl.pallas_call(
        unpack_kernel,
        out_shape=(block, block, block),
        compiler_params=params(24),
    )(share)
    return gate, up, jnp.swapaxes(down, 1, 2)


def widened(router):
    kinds, width = router.shape
    return jnp.concatenate([router, jnp.zeros((LANES - kinds, width), router.dtype)], axis=0)


def project_kernel(
    at_ref, mine_ref, other_ref, x_ref, named_ref, gain_ref, router_ref, in_ref, gates_ref, own_ref, own_gates_ref, ctx_ref, wp_ref
):
    core = at_ref[1]
    total, width = x_ref.shape
    for k in range(4):
        for src, c in ((mine_ref, core), (other_ref, 1 - core)):
            lanes = pl.ds(pl.multiple_of((2 * k + c) * LANES, LANES), LANES)
            ctx_ref[:, lanes] = src[k, :total]
            wp_ref[:, lanes] = src[k, total:]
    me = 2 * at_ref[0] + core
    tokens = own_ref.shape[0]
    router = widened(router_ref[...])
    for i in range(total // QB):
        rows = pl.ds(i * QB, QB)
        middle = x_ref[rows, :].astype(f32) + RES * dot_nt(ctx_ref[rows, :], wp_ref[...])
        normed = rms_scale(middle, gain_ref[...]).astype(bf16)
        in_ref[rows, :] = normed
        logits = jnp.where(named_ref[rows, :] > 0, dot_nt(normed, router), -1e30)
        raised = jnp.exp(logits - jnp.max(logits, axis=1, keepdims=True))
        gates = raised / jnp.sum(raised, axis=1, keepdims=True)
        gates_ref[rows, :] = gates
        for half in range(QB // tokens):

            @pl.when(me == i * (QB // tokens) + half)
            def _():
                own_ref[...] = middle[half * tokens : (half + 1) * tokens]
                own_gates_ref[...] = gates[half * tokens : (half + 1) * tokens]


def project(at, mine, other, x, named, gain, router):
    total, width = x.shape
    outs = (
        jax.ShapeDtypeStruct((total, width), bf16),
        jax.ShapeDtypeStruct((total, LANES), f32),
        jax.ShapeDtypeStruct((total // 8, width), f32),
        jax.ShapeDtypeStruct((total // 8, LANES), f32),
    )
    ins = (mine, other, x, named, gain, router)
    return pl.pallas_call(
        project_kernel,
        grid_spec=pltpu.PrefetchScalarGridSpec(
            num_scalar_prefetch=1,
            grid=(1,),
            in_specs=[whole(v) for v in ins],
            out_specs=[whole(v) for v in outs],
            scratch_shapes=[pltpu.VMEM((total, width), bf16), pltpu.VMEM((total, width), bf16)],
        ),
        out_shape=outs,
        compiler_params=params(48),
    )(at, *ins)


def split_blocks(at_ref, value_of, mine_ref, theirs_ref, n):
    z, core = at_ref[0], at_ref[1]
    for k in range(4):
        there = lax.rem(z + k, 4) * 2
        for ref, c in ((mine_ref, core), (theirs_ref, 1 - core)):
            value_of(ref, k, pl.ds(pl.multiple_of((there + c) * n, n), n))


def attend_kernel(x_ref, gain_ref, w_ref, cos_ref, sin_ref, begin_ref, n_ref, q_ref, kk_ref, vv_ref, heads_ref):
    total = x_ref.shape[0]
    left = lane_of((QB, LANES)) < HEAD
    for i in range(total // QB):
        rows = pl.ds(i * QB, QB)
        x = x_ref[rows, :].astype(f32)
        normed = rms_scale(x, gain_ref[...]).astype(bf16)
        n_ref[rows, :] = normed
        raw = dot_nn(normed, w_ref[:, : 2 * LANES])
        cos, sin = cos_ref[rows, :], sin_ref[rows, :]
        q_ref[rows, :] = rotate(raw[:, :LANES], cos, sin).astype(bf16)
        kv = raw[:, LANES:]
        turned = rotate(kv, cos, sin)
        kk_ref[rows, :] = jnp.where(left, turned, pltpu.roll(turned, HEAD, 1)).astype(bf16)
        vv_ref[rows, :] = jnp.where(left, pltpu.roll(kv, HEAD, 1), kv).astype(bf16)
    vt = vv_ref[...].astype(f32).T.astype(bf16)
    upper = lax.broadcasted_iota(jnp.int32, (LANES, QB), 0) < HEAD
    for i in range(total // QB):
        rows = pl.ds(i * QB, QB)
        lo, hi = key_range(i)
        keys = kk_ref[lo:hi, :]
        ok = allowed_keys(lo, hi - lo, i * QB, begin_ref[:, i * QB : (i + 1) * QB])
        found = []
        for h in range(2):
            qh = jnp.where(left == (h == 0), q_ref[rows, :], jnp.zeros((QB, LANES), bf16))
            p = soft(keys, qh, ok).astype(bf16)
            found.append(dot_nn(vt[:, lo:hi], p))
        heads_ref[rows, :] = jnp.where(upper, found[0], found[1]).T.astype(bf16)
    heads_ref[total:, :] = w_ref[:, 2 * LANES :]


def attend_back_kernel(
    at_ref, ag_ref, q_ref, kk_ref, vv_ref, heads_ref, x_ref, cos_ref, sin_ref, begin_ref, w_ref,
    mine_ref, theirs_ref, gain_ref, dqkv_ref, dctx_ref, dk_ref, dv_ref, dn_ref,
):
    total = ag_ref.shape[0]
    left = lane_of((QB, LANES)) < HEAD
    upper = lax.broadcasted_iota(jnp.int32, (LANES, QB), 0) < HEAD
    dctx_ref[...] = dot_nn(ag_ref[...], heads_ref[total:, :]).astype(bf16)
    dk_ref[...] = jnp.zeros_like(dk_ref)
    dv_ref[...] = jnp.zeros_like(dv_ref)
    kt = kk_ref[...].astype(f32).T.astype(bf16)
    for i in range(total // QB):
        rows = pl.ds(i * QB, QB)
        lo, hi = key_range(i)
        keys = kk_ref[lo:hi, :]
        ok = allowed_keys(lo, hi - lo, i * QB, begin_ref[:, i * QB : (i + 1) * QB])
        found = []
        for h in range(2):
            mine = left == (h == 0)
            qh = jnp.where(mine, q_ref[rows, :], jnp.zeros((QB, LANES), bf16))
            dch = jnp.where(mine, dctx_ref[rows, :], jnp.zeros((QB, LANES), bf16))
            p = soft(keys, qh, ok)
            dp = dot_nt(vv_ref[lo:hi, :], dch)
            ds = (p * (dp - jnp.sum(dp * p, axis=0, keepdims=True))).astype(bf16)
            dk_ref[lo:hi, :] += dot_nn(ds, qh)
            dv_ref[lo:hi, :] += dot_nn(p.astype(bf16), dch)
            found.append(dot_nn(kt[:, lo:hi], ds))
        dq = jnp.where(upper, found[0], found[1]).T * SCALE
        dqkv_ref[rows, :LANES] = rotate(dq, cos_ref[rows, :], -sin_ref[rows, :]).astype(bf16)
    acc = jnp.zeros((1, x_ref.shape[1]), f32)
    for i in range(total // QB):
        rows = pl.ds(i * QB, QB)
        dk, dv = dk_ref[rows, :], dv_ref[rows, :]
        dk = (dk + pltpu.roll(dk, HEAD, 1)) * SCALE
        dk = rotate(dk, cos_ref[rows, :], -sin_ref[rows, :])
        dv = dv + pltpu.roll(dv, HEAD, 1)
        dqkv_ref[rows, LANES:] = jnp.where(left, dk, dv).astype(bf16)
        dn = dot_nt(dqkv_ref[rows, :], w_ref[:, : 2 * LANES])
        dn_ref[rows, :] = dn.astype(bf16)
        x = x_ref[rows, :].astype(f32)
        hat = x * lax.rsqrt(jnp.mean(x * x, axis=-1, keepdims=True) + EPS)
        acc = acc + jnp.sum(dn * hat, axis=0, keepdims=True)
    gain_ref[...] = acc

    def give(ref, k, rows):
        ref[k] = dn_ref[rows, :]

    split_blocks(at_ref, give, mine_ref, theirs_ref, mine_ref.shape[1])


def attend_weights_kernel(dqkv_ref, normed_ref, heads_ref, ag_ref, in_ref, dl_ref, wg_ref, rows_ref):
    total = ag_ref.shape[0]
    dqkv_t = dqkv_ref[...].astype(f32).T.astype(bf16)
    ctx_t = heads_ref[:total, :].astype(f32).T.astype(bf16)
    wg_ref[:, : 2 * LANES] = dot_nn(dqkv_t, normed_ref[...]).T.astype(bf16)
    wg_ref[:, 2 * LANES :] = dot_nn(ctx_t, ag_ref[...]).T.astype(bf16)
    parts = dot_nn(dl_ref[...].astype(f32).T.astype(bf16), in_ref[...])
    rows_ref[...] = parts[: rows_ref.shape[0]] + parts[HEAD : HEAD + rows_ref.shape[0]]


def experts_kernel(
    at_ref, x_ref, dy_ref, gates_ref, w_ref, mine_ref, theirs_ref, acts_ref, accm_ref, accx_ref, dg_ref
):
    e = pl.program_id(0)
    ff = acts_ref.shape[1] // 3
    total = x_ref.shape[0]
    lane = lane_of((total, LANES))
    pick = (2 * at_ref[0] + at_ref[1]) * pl.num_programs(0) + e

    @pl.when(e == 0)
    def _():
        accm_ref[...] = jnp.zeros_like(accm_ref)
        accx_ref[...] = jnp.zeros_like(accx_ref)
        dg_ref[...] = jnp.zeros_like(dg_ref)

    gu = dot_nn(x_ref[...], w_ref[:, : 2 * ff])
    h0 = dot_nn(dy_ref[...], w_ref[:, 2 * ff :]) * RES
    g, u = gu[:, :ff], gu[:, ff:]
    gate = jnp.sum(jnp.where(lane == pick, gates_ref[...], 0.0), axis=1, keepdims=True)
    sg = jax.nn.sigmoid(g)
    sw = g * sg
    hid = sw * u
    dg = jnp.sum(hid * h0, axis=1, keepdims=True)
    dg_ref[...] += jnp.where(lane == pick, dg, 0.0)
    acts_ref[:, 2 * ff :] = (gate * hid).astype(bf16)
    dh = gate * h0
    acts_ref[:, :ff] = (dh * u * sg * (1.0 + g * (1.0 - sg))).astype(bf16)
    acts_ref[:, ff : 2 * ff] = (dh * sw).astype(bf16)
    accm_ref[...] += dot_nt(acts_ref[:, 2 * ff :], w_ref[:, 2 * ff :])
    accx_ref[...] += dot_nt(acts_ref[:, : 2 * ff], w_ref[:, : 2 * ff])

    @pl.when(e == pl.num_programs(0) - 1)
    def _():
        width = accx_ref.shape[1]
        dg = dg_ref[...]
        high = dg.astype(bf16).astype(f32)
        mid = (dg - high).astype(bf16).astype(f32)
        low = dg - high - mid
        dg_ref[...] = high + pltpu.roll(mid, 32, 1) + pltpu.roll(low, 64, 1)

        def give(ref, k, rows):
            ref[k, :, :width] = accx_ref[rows, :].astype(bf16)
            ref[k, :, width : 2 * width] = accm_ref[rows, :].astype(bf16)
            ref[k, :, 2 * width :] = dg_ref[rows, :].astype(bf16)

        split_blocks(at_ref, give, mine_ref, theirs_ref, mine_ref.shape[1])


def weights_kernel(x_ref, dy_ref, acts_ref, *refs):
    out_ref, turned_ref = refs[-2:]
    step = pl.program_id(0)

    @pl.when(step == 0)
    def _():
        turned_ref[0] = x_ref[...].T
        turned_ref[1] = dy_ref[...].T

    is_down = lax.rem(step, 3) == 2
    found = dot_nn(turned_ref[jnp.where(is_down, 1, 0)], acts_ref[...])
    out_ref[...] = (found * jnp.where(is_down, RES, 1.0)).astype(bf16)


def params(mb):
    return pltpu.CompilerParams(vmem_limit_bytes=mb * VMEM_MB)


def attend(x_all, gain, weights, cos, sin, begin):
    total, width = x_all.shape
    shape = lambda n, w: jax.ShapeDtypeStruct((n, w), bf16)
    one = shape(total, LANES)
    return pl.pallas_call(
        attend_kernel,
        out_shape=(shape(total, width), one, one, one, shape(total + width, LANES)),
        compiler_params=params(48),
    )(x_all, gain, weights, cos, sin, begin)


def attend_back(at, *ins):
    total, width = ins[0].shape
    block = jax.ShapeDtypeStruct((4, total // 8, width), bf16)
    outs = (
        block,
        block,
        jax.ShapeDtypeStruct((1, width), f32),
        jax.ShapeDtypeStruct((total, 2 * LANES), bf16),
    )
    return pl.pallas_call(
        attend_back_kernel,
        grid_spec=pltpu.PrefetchScalarGridSpec(
            num_scalar_prefetch=1,
            grid=(1,),
            in_specs=[whole(v) for v in ins],
            out_specs=[whole(v) for v in outs],
            scratch_shapes=[
                pltpu.VMEM((total, LANES), bf16),
                pltpu.VMEM((total, LANES), f32),
                pltpu.VMEM((total, LANES), f32),
                pltpu.VMEM((total, width), bf16),
            ],
        ),
        out_shape=outs,
        compiler_params=params(32),
    )(at, *ins)


def attend_weights(*ins, kinds):
    width = ins[3].shape[1]
    return pl.pallas_call(
        attend_weights_kernel,
        out_shape=(
            jax.ShapeDtypeStruct((width, 3 * LANES), bf16),
            jax.ShapeDtypeStruct((kinds, width), f32),
        ),
        compiler_params=params(24),
    )(*ins)


def experts(at, x, dy, gates, weights, count):
    total, width = x.shape
    ff = weights.shape[1] // (3 * count)
    block = jax.ShapeDtypeStruct((4, total // 8, 2 * width + LANES), bf16)
    each = lambda rows, w: pl.BlockSpec((rows, w), lambda e, at: (0, e))
    return pl.pallas_call(
        experts_kernel,
        grid_spec=pltpu.PrefetchScalarGridSpec(
            num_scalar_prefetch=1,
            grid=(count,),
            in_specs=[whole(x), whole(dy), whole(gates), each(width, 3 * ff)],
            out_specs=[whole(block), whole(block), each(total, 3 * ff)],
            scratch_shapes=[
                pltpu.VMEM((total, width), f32),
                pltpu.VMEM((total, width), f32),
                pltpu.VMEM((total, LANES), f32),
            ],
        ),
        out_shape=(
            block,
            block,
            jax.ShapeDtypeStruct((total, 3 * ff * count), bf16),
        ),
        compiler_params=params(60),
        cost_estimate=pl.CostEstimate(
            flops=12 * total * width * ff * count,
            bytes_accessed=4 * width * 3 * ff * count,
            transcendentals=total * ff * count,
        ),
    )(at, x, dy, gates, weights)


def expert_weights_grad(x, dy, acts, filled, first, count, all_of):
    total, width = x.shape
    ff = acts.shape[1] // (3 * all_of)
    each = lambda rows: pl.BlockSpec((rows, ff), lambda s: (0, 3 * first + s))
    fixed = pl.BlockSpec((total, width), lambda s: (0, 0))
    ins = [x, dy, acts]
    in_specs = [fixed, fixed, each(total)]
    if filled is not None:
        ins.append(filled)
        in_specs.append(pl.BlockSpec(memory_space=pl.ANY))
    return pl.pallas_call(
        weights_kernel,
        grid=(3 * count,),
        in_specs=in_specs,
        out_specs=each(width),
        out_shape=jax.ShapeDtypeStruct((width, 3 * ff * all_of), bf16),
        scratch_shapes=[pltpu.VMEM((2, width, total), bf16)],
        input_output_aliases={} if filled is None else {3: 0},
        compiler_params=params(56),
        cost_estimate=pl.CostEstimate(
            flops=6 * total * width * ff * count,
            bytes_accessed=4 * width * 3 * ff * count,
            transcendentals=0,
        ),
    )(*ins)


def tables(lengths_row, group):
    ends = jnp.cumsum(lengths_row)
    starts = ends - lengths_row
    places = jnp.arange(group, dtype=jnp.int32)
    inside = (places[:, None] >= starts[None, :]) & (places[:, None] < ends[None, :])
    begin = jnp.sum(jnp.where(inside, starts[None, :], 0), axis=1)
    frequency = BASE ** (-(jnp.arange(HEAD // 2, dtype=f32) * 2.0 / HEAD))
    angles = (places - begin).astype(f32)[:, None] * frequency[None, :]
    cos, sin = jnp.cos(angles), jnp.sin(angles)
    return (
        begin.reshape(1, group),
        jnp.concatenate([cos] * 4, axis=1),
        jnp.concatenate([-sin, sin, -sin, sin], axis=1),
    )


def local(
    layer_input, lengths, choices, query_weight, key_matrix, value_matrix, project_weight,
    gate_weight, up_weight, down_weight, router_weight, attention_gain, expert_gain, grad_output,
):
    me = lax.axis_index("col")
    tokens, width = layer_input.shape
    group = tokens * 8
    kinds = router_weight.shape[1]
    count, _, ff = gate_weight.shape
    own = lambda v: lax.dynamic_slice_in_dim(v, me * tokens, tokens, axis=0)

    at = jnp.stack([me // 2, me % 2]).astype(jnp.int32)
    spots = jnp.arange(LANES, dtype=jnp.int32)
    named = jnp.any(choices[:, :, None] == spots[None, None, :], axis=1).astype(bf16)
    share = pack(gate_weight, up_weight, down_weight)
    expert_weights = lax.all_gather(share, "row", axis=0, tiled=True)
    small = gather_row_small(
        jnp.concatenate([query_weight, key_matrix, value_matrix, project_weight.T], axis=1)
    )
    *entering, small = gather_col(jnp.concatenate([layer_input, grad_output, named], axis=1), at, small)
    x_all, dy_all, named_all = merge(at, *entering, (width, width, LANES))

    begin, cos, sin = tables(lengths[0], group)
    gain_one = attention_gain.reshape(1, width)
    normed, q, kk, vv, heads = attend(x_all, gain_one, small, cos, sin, begin)
    heads_mine, heads_other, _ = gather_col(heads, at)
    router = router_weight.T
    gain_two = expert_gain.reshape(1, width)
    expert_in, gates_all, middle, gates = project(
        at, heads_mine, heads_other, x_all, named_all, gain_two, router
    )
    mine, theirs, acts = experts(at, expert_in, dy_all, gates_all, expert_weights, count)

    def piece(first, number):
        return lambda filled: expert_weights_grad(
            expert_in, dy_all, acts, filled, first, number, count
        )

    half = count // 2
    arrived, expert_wgrad = sum_col(mine, theirs, None, [piece(0, half), piece(half, count - half)])
    expert_sum = lax.psum_scatter(expert_wgrad, "row", scatter_dimension=0, tiled=True)

    block_output, middle_grad, sent, gain_two_part = turn(
        *arrived, middle, gates, grad_output, gain_two, router
    )
    back_mine, back_other, _ = gather_col(sent, at)
    ag_all, logits_all = merge(at, back_mine, back_other, (width, LANES))

    dn_mine, dn_theirs, gain_part, dqkv = attend_back(
        at, ag_all, q, kk, vv, heads, x_all, cos, sin, begin, small
    )
    gains = jnp.concatenate([gain_two_part, gain_part], axis=0)

    def opening(_):
        wg, rows = attend_weights(dqkv, normed, heads, ag_all, expert_in, logits_all, kinds=kinds)
        wg, both = lax.optimization_barrier((wg, jnp.concatenate(two_parts(gains), axis=0)))
        parts = jnp.sum(send_all(both, "col").astype(f32), axis=0)
        return wg, jnp.concatenate([rows, parts[:2] + parts[2:]], axis=0)

    sent = []

    def second(held):
        sent.append(exchange_row(held[0]))
        return row_step(held[1], 1)

    def third(rows):
        return row_step(rows, 2), sent[0]

    normed_grad, (rows, pieces) = sum_col(dn_mine, dn_theirs, None, [opening, second, third])
    input_grad = close(*normed_grad, layer_input, middle_grad, gain_one)
    rows = row_step(row_step(rows, 4), 8)
    small_sum = jnp.sum(pieces.astype(f32), axis=0)
    gate_grad, up_grad, down_grad = unpack(expert_sum, count, ff)
    return (
        block_output,
        input_grad,
        small_sum[:, :LANES],
        small_sum[:, LANES : LANES + HEAD],
        small_sum[:, LANES + HEAD : 2 * LANES],
        small_sum[:, 2 * LANES :].T,
        gate_grad,
        up_grad,
        down_grad,
        rows[:kinds].T,
        rows[kinds + 1],
        rows[kinds],
    )


def solution(mesh):
    both = P(("row", "col"), None)
    in_specs = (
        both, P("row", None), both, P("row", "col"), P("row", "col"), P("row", "col"), P("col", "row"),
        P("col", "row", None), P("col", "row", None), P("col", None, "row"), P(), P(), P(), both,
    )
    out_specs = (
        both, both, P("row", "col"), P("row", "col"), P("row", "col"), P("col", "row"),
        P("col", "row", None), P("col", "row", None), P("col", None, "row"), P(), P(), P(),
    )
    return jax.shard_map(local, mesh=mesh, in_specs=in_specs, out_specs=out_specs, check_vma=False)
```

```python
import functools

import jax
import jax.numpy as jnp
from jax import lax
from jax.experimental import pallas as pl
from jax.experimental.pallas import tpu as pltpu
from jax.sharding import PartitionSpec as P

HEAD = 64
LANES = 128
QB = 256
EPS = 1e-06
RES = 0.22
SCALE = 0.125
BASE = 10000.0
bf16 = jnp.bfloat16
f32 = jnp.float32
VMEM_MB = 1 << 20


def dot_nt(a, b):
    return lax.dot_general(a, b, (((1,), (1,)), ((), ())), preferred_element_type=f32)


def dot_nn(a, b):
    return lax.dot_general(a, b, (((1,), (0,)), ((), ())), preferred_element_type=f32)


def rms_scale(values, gain_vec):
    return values * lax.rsqrt(jnp.mean(values * values, axis=-1, keepdims=True) + EPS) * gain_vec


def core_swap(a):
    return lax.ppermute(a, "col", [(i, i ^ 1) for i in range(8)])


def z_shift(a, d):
    return lax.ppermute(a, "col", [(i, (i + 2 * d) % 8) for i in range(8)])


def y_shift(a, d):
    return lax.ppermute(a, "row", [(i, (i // 4) * 4 + (i + d) % 4) for i in range(16)])


def x_shift(a, d):
    return lax.ppermute(a, "row", [(i, (i + 4 * d) % 16) for i in range(16)])


def gather_col(a, at, beside=None):
    half = a.shape[0] // 2
    back = z_shift(a, 1)
    ahead = z_shift(a, -1)
    if beside is not None:
        back, ahead, beside = lax.optimization_barrier((back, ahead, beside))
    far0 = z_shift(back[:half], 1)
    far1 = z_shift(ahead[half:], -1)
    mine = pl.pallas_call(
        place_kernel,
        grid_spec=pltpu.PrefetchScalarGridSpec(
            num_scalar_prefetch=1,
            grid=(1,),
            in_specs=[whole(v) for v in (a, back, ahead, far0, far1)],
            out_specs=pl.BlockSpec((4,) + a.shape, lambda g, at: (0, 0, 0)),
        ),
        out_shape=jax.ShapeDtypeStruct((4,) + a.shape, a.dtype),
        compiler_params=params(24),
    )(at, a, back, ahead, far0, far1)
    return mine, core_swap(mine), beside


def sum_col(pairs, beside=None, steps=()):
    steps = list(steps)

    def phase(*values):
        nonlocal beside
        if steps:
            beside = steps.pop(0)(beside)
            values, beside = lax.optimization_barrier((values, beside))
        return values

    pairs = phase(*pairs)
    own, ahead, behind, far0, far1 = fold(*pairs)
    via_up, via_down = phase(z_shift(far0, 1), z_shift(far1, -1))
    up, down = join(ahead, behind, via_up, via_down)
    up, down = phase(z_shift(up, 1), z_shift(down, -1))
    return (own, up, down), beside


def gather_row_small(a):
    ways = lax.axis_size("row")
    sent = jnp.broadcast_to(a[None], (ways,) + a.shape)
    return lax.all_to_all(sent, "row", 0, 0, tiled=True).reshape(-1, a.shape[1])


def exchange_row(a):
    ways = lax.axis_size("row")
    return lax.all_to_all(a.reshape(ways, -1, a.shape[1]), "row", 0, 0, tiled=True)


def send_all(a, axis):
    sent = jnp.broadcast_to(a[None], (lax.axis_size(axis),) + a.shape)
    return lax.all_to_all(sent, axis, 0, 0, tiled=True)


def two_parts(v):
    high = v.astype(bf16)
    return high, (v - high.astype(f32)).astype(bf16)


def row_step(v, bit):
    low = v.astype(bf16)
    got = lax.ppermute(low, "row", [(i, i ^ bit) for i in range(16)])
    return low.astype(f32) + got.astype(f32)


def lane_of(shape):
    return lax.broadcasted_iota(jnp.int32, shape, 1)


def rotate(values, cos, sin):
    first = (lane_of(values.shape) % HEAD) < HEAD // 2
    swapped = jnp.where(first, pltpu.roll(values, 96, 1), pltpu.roll(values, 32, 1))
    return values * cos + swapped * sin


def allowed_keys(lo, count, row0, begin):
    key = lax.broadcasted_iota(jnp.int32, (count, QB), 0) + lo
    query = lax.broadcasted_iota(jnp.int32, (count, QB), 1) + row0
    return (key >= begin) & (key <= query)


def soft(kk, qh, ok):
    s = jnp.where(ok, dot_nt(kk, qh) * SCALE, -1e30)
    raised = jnp.exp(s - jnp.max(s, axis=0, keepdims=True))
    return raised / jnp.sum(raised, axis=0, keepdims=True)


def key_range(i):
    return max(0, i - 2) * QB, (i + 1) * QB


def whole(v):
    return pl.BlockSpec(v.shape, lambda g, at, r=len(v.shape): (0,) * r)


def fold_kernel(*refs):
    own_ref, ahead_ref, behind_ref, far0_ref, far1_ref = refs[-5:]
    half = far0_ref.shape[0]
    at = 0
    for mine, got in zip(refs[:-5:2], refs[1:-5:2]):
        cols = slice(at, at + mine.shape[-1])
        at += mine.shape[-1]
        add = lambda k: mine[k].astype(f32) + got[k].astype(f32)
        own_ref[:, cols] = add(0)
        ahead_ref[:, cols] = add(1)
        behind_ref[:, cols] = add(3)
        far = add(2).astype(bf16)
        far0_ref[:, cols] = far[:half]
        far1_ref[:, cols] = far[half:]


def fold(*pairs):
    n = pairs[0][0].shape[1]
    w = sum(mine.shape[2] for mine, _ in pairs)
    one = jax.ShapeDtypeStruct((n, w), f32)
    part = jax.ShapeDtypeStruct((n // 2, w), bf16)
    return pl.pallas_call(
        fold_kernel, out_shape=(one, one, one, part, part), compiler_params=params(24)
    )(*[v for pair in pairs for v in pair])


def join_kernel(ahead_ref, behind_ref, via_up_ref, via_down_ref, up_ref, down_ref):
    half = via_up_ref.shape[0]
    up_ref[:half] = (ahead_ref[:half] + via_up_ref[...].astype(f32)).astype(bf16)
    up_ref[half:] = ahead_ref[half:].astype(bf16)
    down_ref[:half] = behind_ref[:half].astype(bf16)
    down_ref[half:] = (behind_ref[half:] + via_down_ref[...].astype(f32)).astype(bf16)


def join(ahead, behind, via_up, via_down):
    one = jax.ShapeDtypeStruct(ahead.shape, bf16)
    return pl.pallas_call(join_kernel, out_shape=(one, one), compiler_params=params(24))(
        ahead, behind, via_up, via_down
    )


def norm_back(x, grad, gain):
    inv = lax.rsqrt(jnp.mean(x * x, axis=-1, keepdims=True) + EPS)
    scaled = grad * gain
    hat = x * inv
    return inv * (scaled - hat * jnp.mean(hat * scaled, axis=-1, keepdims=True)), hat


def turn_kernel(
    own_ref, up_ref, down_ref, middle_ref, gates_ref, grad_ref, gain_ref, router_ref,
    back_ref, sent_ref, gain_part_ref,
):
    width = middle_ref.shape[1]
    arrived = own_ref[...] + up_ref[...].astype(f32) + down_ref[...].astype(f32)
    middle = middle_ref[...]
    parts = arrived[:, width:]
    gates_grad = parts + pltpu.roll(parts, 96, 1) + pltpu.roll(parts, 64, 1)
    gates = gates_ref[...]
    logits_grad = gates * (gates_grad - jnp.sum(gates * gates_grad, axis=1, keepdims=True))
    high = logits_grad.astype(bf16)
    rest = logits_grad - high.astype(f32)
    low = rest.astype(bf16)
    router = widened(router_ref[...])
    grad = arrived[:, :width] + dot_nn(high, router) + dot_nn(low, router)
    back, hat = norm_back(middle, grad, gain_ref[...])
    back = grad_ref[...].astype(f32) + back
    back_ref[...] = back
    sent_ref[:, :width] = (RES * back).astype(bf16)
    sent_ref[:, width:] = (high.astype(f32) + pltpu.roll(low.astype(f32), HEAD, 1)).astype(bf16)
    gain_part_ref[...] = jnp.sum(grad * hat, axis=0, keepdims=True)


def turn(own, up, down, middle, gates, grad, gain, router):
    n, width = middle.shape
    return pl.pallas_call(
        turn_kernel,
        out_shape=(
            jax.ShapeDtypeStruct((n, width), f32),
            jax.ShapeDtypeStruct((n, width + LANES), bf16),
            jax.ShapeDtypeStruct((1, width), f32),
        ),
        compiler_params=params(24),
    )(own, up, down, middle, gates, grad, gain, router)


def close_kernel(own_ref, up_ref, down_ref, x_ref, back_ref, gain_ref, middle_ref, out_ref, block_ref):
    width = out_ref.shape[1]
    arrived = own_ref[...] + up_ref[...].astype(f32) + down_ref[...].astype(f32)
    grad = arrived[:, :width]
    out_ref[...] = back_ref[...] + norm_back(x_ref[...].astype(f32), grad, gain_ref[...])[0]
    block_ref[...] = middle_ref[...] + RES * arrived[:, width:]


def close(own, up, down, x, back, gain, middle):
    one = jax.ShapeDtypeStruct(middle.shape, f32)
    return pl.pallas_call(close_kernel, out_shape=(one, one), compiler_params=params(24))(
        own, up, down, x, back, gain, middle
    )


def place_kernel(at_ref, own_ref, back_ref, ahead_ref, far0_ref, far1_ref, out_ref):
    z = at_ref[0]
    half = own_ref.shape[0] // 2
    out_ref[z] = own_ref[...]
    out_ref[lax.rem(z + 3, 4)] = back_ref[...]
    out_ref[lax.rem(z + 1, 4)] = ahead_ref[...]
    out_ref[lax.rem(z + 2, 4), :half] = far0_ref[...]
    out_ref[lax.rem(z + 2, 4), half:] = far1_ref[...]


def merge_kernel(at_ref, mine_ref, other_ref, *refs):
    core = at_ref[1]
    for k in range(4):
        for src, c in ((mine_ref, core), (other_ref, 1 - core)):
            at = 0
            for ref in refs:
                w = ref.shape[-1]
                ref[k, c] = src[k, :, at : at + w]
                at += w


def merge(at, mine, other, widths):
    _, n, _ = mine.shape
    outs = [jax.ShapeDtypeStruct((4, 2, n, w), bf16) for w in widths]
    found = pl.pallas_call(
        merge_kernel,
        grid_spec=pltpu.PrefetchScalarGridSpec(
            num_scalar_prefetch=1,
            grid=(1,),
            in_specs=[whole(mine), whole(other)],
            out_specs=[whole(v) for v in outs],
        ),
        out_shape=outs,
        compiler_params=params(24),
    )(at, mine, other)
    return [v.reshape(8 * n, v.shape[-1]) for v in found]


def pack_kernel(g_ref, u_ref, d_ref, share_ref):
    count, _, ff = g_ref.shape
    for e in range(count):
        at = 3 * ff * e
        share_ref[:, at : at + ff] = g_ref[e]
        share_ref[:, at + ff : at + 2 * ff] = u_ref[e]
        share_ref[:, at + 2 * ff : at + 3 * ff] = d_ref[e]


def pack(gate, up, down):
    count, n, ff = gate.shape
    return pl.pallas_call(
        pack_kernel,
        out_shape=jax.ShapeDtypeStruct((n, 3 * ff * count), bf16),
        compiler_params=params(60),
    )(gate, up, jnp.swapaxes(down, 1, 2))


def unpack_kernel(s_ref, g_ref, u_ref, d_ref):
    count, _, ff = g_ref.shape
    for e in range(count):
        at = 3 * ff * e
        g_ref[e] = s_ref[:, at : at + ff].astype(f32)
        u_ref[e] = s_ref[:, at + ff : at + 2 * ff].astype(f32)
        d_ref[e] = s_ref[:, at + 2 * ff : at + 3 * ff].astype(f32)


def unpack(share, count, ff):
    n = share.shape[0]
    block = jax.ShapeDtypeStruct((count, n, ff), f32)
    gate, up, down = pl.pallas_call(
        unpack_kernel,
        out_shape=(block, block, block),
        compiler_params=params(24),
    )(share)
    return gate, up, jnp.swapaxes(down, 1, 2)


def widened(router):
    kinds, width = router.shape
    return jnp.concatenate([router, jnp.zeros((LANES - kinds, width), router.dtype)], axis=0)


def project_kernel(
    at_ref, mine_ref, other_ref, x_ref, named_ref, gain_ref, router_ref, in_ref, gates_ref, own_ref, own_gates_ref, ctx_ref, wp_ref
):
    core = at_ref[1]
    total, width = x_ref.shape
    for k in range(4):
        for src, c in ((mine_ref, core), (other_ref, 1 - core)):
            lanes = pl.ds(pl.multiple_of((2 * k + c) * LANES, LANES), LANES)
            ctx_ref[:, lanes] = src[k, :total]
            wp_ref[:, lanes] = src[k, total:]
    me = 2 * at_ref[0] + core
    tokens = own_ref.shape[0]
    router = widened(router_ref[...])
    for i in range(total // QB):
        rows = pl.ds(i * QB, QB)
        middle = x_ref[rows, :].astype(f32) + RES * dot_nt(ctx_ref[rows, :], wp_ref[...])
        normed = rms_scale(middle, gain_ref[...]).astype(bf16)
        in_ref[rows, :] = normed
        logits = jnp.where(named_ref[rows, :] > 0, dot_nt(normed, router), -1e30)
        raised = jnp.exp(logits - jnp.max(logits, axis=1, keepdims=True))
        gates = raised / jnp.sum(raised, axis=1, keepdims=True)
        gates_ref[rows, :] = gates
        for half in range(QB // tokens):

            @pl.when(me == i * (QB // tokens) + half)
            def _():
                own_ref[...] = middle[half * tokens : (half + 1) * tokens]
                own_gates_ref[...] = gates[half * tokens : (half + 1) * tokens]


def project(at, mine, other, x, named, gain, router):
    total, width = x.shape
    outs = (
        jax.ShapeDtypeStruct((total, width), bf16),
        jax.ShapeDtypeStruct((total, LANES), f32),
        jax.ShapeDtypeStruct((total // 8, width), f32),
        jax.ShapeDtypeStruct((total // 8, LANES), f32),
    )
    ins = (mine, other, x, named, gain, router)
    return pl.pallas_call(
        project_kernel,
        grid_spec=pltpu.PrefetchScalarGridSpec(
            num_scalar_prefetch=1,
            grid=(1,),
            in_specs=[whole(v) for v in ins],
            out_specs=[whole(v) for v in outs],
            scratch_shapes=[pltpu.VMEM((total, width), bf16), pltpu.VMEM((total, width), bf16)],
        ),
        out_shape=outs,
        compiler_params=params(60),
    )(at, *ins)


def split_blocks(at_ref, value_of, mine_ref, theirs_ref, n):
    z, core = at_ref[0], at_ref[1]
    for k in range(4):
        there = lax.rem(z + k, 4) * 2
        for ref, c in ((mine_ref, core), (theirs_ref, 1 - core)):
            value_of(ref, k, pl.ds(pl.multiple_of((there + c) * n, n), n))


def attend_kernel(x_ref, gain_ref, w_ref, cos_ref, sin_ref, begin_ref, n_ref, q_ref, kk_ref, vv_ref, heads_ref):
    total = x_ref.shape[0]
    left = lane_of((QB, LANES)) < HEAD
    for i in range(total // QB):
        rows = pl.ds(i * QB, QB)
        x = x_ref[rows, :].astype(f32)
        normed = rms_scale(x, gain_ref[...]).astype(bf16)
        n_ref[rows, :] = normed
        raw = dot_nn(normed, w_ref[:, : 2 * LANES])
        cos, sin = cos_ref[rows, :], sin_ref[rows, :]
        q_ref[rows, :] = rotate(raw[:, :LANES], cos, sin).astype(bf16)
        kv = raw[:, LANES:]
        turned = rotate(kv, cos, sin)
        kk_ref[rows, :] = jnp.where(left, turned, pltpu.roll(turned, HEAD, 1)).astype(bf16)
        vv_ref[rows, :] = jnp.where(left, pltpu.roll(kv, HEAD, 1), kv).astype(bf16)
    vt = vv_ref[...].astype(f32).T.astype(bf16)
    upper = lax.broadcasted_iota(jnp.int32, (LANES, QB), 0) < HEAD
    for i in range(total // QB):
        rows = pl.ds(i * QB, QB)
        lo, hi = key_range(i)
        keys = kk_ref[lo:hi, :]
        ok = allowed_keys(lo, hi - lo, i * QB, begin_ref[:, i * QB : (i + 1) * QB])
        found = []
        for h in range(2):
            qh = jnp.where(left == (h == 0), q_ref[rows, :], jnp.zeros((QB, LANES), bf16))
            p = soft(keys, qh, ok).astype(bf16)
            found.append(dot_nn(vt[:, lo:hi], p))
        heads_ref[rows, :] = jnp.where(upper, found[0], found[1]).T.astype(bf16)
    heads_ref[total:, :] = w_ref[:, 2 * LANES :]


def attend_back_kernel(
    at_ref, ag_ref, q_ref, kk_ref, vv_ref, heads_ref, x_ref, cos_ref, sin_ref, begin_ref, w_ref,
    mine_ref, theirs_ref, gain_ref, dqkv_ref, dctx_ref, dk_ref, dv_ref, dn_ref,
):
    total = ag_ref.shape[0]
    left = lane_of((QB, LANES)) < HEAD
    upper = lax.broadcasted_iota(jnp.int32, (LANES, QB), 0) < HEAD
    dctx_ref[...] = dot_nn(ag_ref[...], heads_ref[total:, :]).astype(bf16)
    dk_ref[...] = jnp.zeros_like(dk_ref)
    dv_ref[...] = jnp.zeros_like(dv_ref)
    kt = kk_ref[...].astype(f32).T.astype(bf16)
    for i in range(total // QB):
        rows = pl.ds(i * QB, QB)
        lo, hi = key_range(i)
        keys = kk_ref[lo:hi, :]
        ok = allowed_keys(lo, hi - lo, i * QB, begin_ref[:, i * QB : (i + 1) * QB])
        found = []
        for h in range(2):
            mine = left == (h == 0)
            qh = jnp.where(mine, q_ref[rows, :], jnp.zeros((QB, LANES), bf16))
            dch = jnp.where(mine, dctx_ref[rows, :], jnp.zeros((QB, LANES), bf16))
            p = soft(keys, qh, ok)
            dp = dot_nt(vv_ref[lo:hi, :], dch)
            ds = (p * (dp - jnp.sum(dp * p, axis=0, keepdims=True))).astype(bf16)
            dk_ref[lo:hi, :] += dot_nn(ds, qh)
            dv_ref[lo:hi, :] += dot_nn(p.astype(bf16), dch)
            found.append(dot_nn(kt[:, lo:hi], ds))
        dq = jnp.where(upper, found[0], found[1]).T * SCALE
        dqkv_ref[rows, :LANES] = rotate(dq, cos_ref[rows, :], -sin_ref[rows, :]).astype(bf16)
    acc = jnp.zeros((1, x_ref.shape[1]), f32)
    for i in range(total // QB):
        rows = pl.ds(i * QB, QB)
        dk, dv = dk_ref[rows, :], dv_ref[rows, :]
        dk = (dk + pltpu.roll(dk, HEAD, 1)) * SCALE
        dk = rotate(dk, cos_ref[rows, :], -sin_ref[rows, :])
        dv = dv + pltpu.roll(dv, HEAD, 1)
        dqkv_ref[rows, LANES:] = jnp.where(left, dk, dv).astype(bf16)
        dn = dot_nt(dqkv_ref[rows, :], w_ref[:, : 2 * LANES])
        dn_ref[rows, :] = dn.astype(bf16)
        x = x_ref[rows, :].astype(f32)
        hat = x * lax.rsqrt(jnp.mean(x * x, axis=-1, keepdims=True) + EPS)
        acc = acc + jnp.sum(dn * hat, axis=0, keepdims=True)
    gain_ref[...] = acc

    def give(ref, k, rows):
        ref[k] = dn_ref[rows, :]

    split_blocks(at_ref, give, mine_ref, theirs_ref, mine_ref.shape[1])


def attend_weights_kernel(dqkv_ref, normed_ref, heads_ref, ag_ref, in_ref, dl_ref, wg_ref, rows_ref):
    total = ag_ref.shape[0]
    dqkv_t = dqkv_ref[...].astype(f32).T.astype(bf16)
    ctx_t = heads_ref[:total, :].astype(f32).T.astype(bf16)
    wg_ref[:, : 2 * LANES] = dot_nn(dqkv_t, normed_ref[...]).T.astype(bf16)
    wg_ref[:, 2 * LANES :] = dot_nn(ctx_t, ag_ref[...]).T.astype(bf16)
    parts = dot_nn(dl_ref[...].astype(f32).T.astype(bf16), in_ref[...])
    rows_ref[...] = parts[: rows_ref.shape[0]] + parts[HEAD : HEAD + rows_ref.shape[0]]


def experts_kernel(
    at_ref, x_ref, dy_ref, gates_ref, w_ref, mine_ref, theirs_ref, mix_mine_ref, mix_theirs_ref, out_ref,
    acts_ref, xt_ref, dyt_ref, accm_ref, accx_ref, dg_ref,
):
    e = pl.program_id(0)
    ff = acts_ref.shape[1] // 3
    total = x_ref.shape[0]
    lane = lane_of((total, LANES))
    pick = (2 * at_ref[0] + at_ref[1]) * pl.num_programs(0) + e

    @pl.when(e == 0)
    def _():
        xt_ref[...] = x_ref[...].T
        dyt_ref[...] = dy_ref[...].T
        accm_ref[...] = jnp.zeros_like(accm_ref)
        accx_ref[...] = jnp.zeros_like(accx_ref)
        dg_ref[...] = jnp.zeros_like(dg_ref)

    gu = dot_nn(x_ref[...], w_ref[:, : 2 * ff])
    h0 = dot_nn(dy_ref[...], w_ref[:, 2 * ff :]) * RES
    g, u = gu[:, :ff], gu[:, ff:]
    gate = jnp.sum(jnp.where(lane == pick, gates_ref[...], 0.0), axis=1, keepdims=True)
    sg = jax.nn.sigmoid(g)
    sw = g * sg
    hid = sw * u
    dg = jnp.sum(hid * h0, axis=1, keepdims=True)
    dg_ref[...] += jnp.where(lane == pick, dg, 0.0)
    acts_ref[:, 2 * ff :] = (gate * hid).astype(bf16)
    dh = gate * h0
    acts_ref[:, :ff] = (dh * u * sg * (1.0 + g * (1.0 - sg))).astype(bf16)
    acts_ref[:, ff : 2 * ff] = (dh * sw).astype(bf16)
    accm_ref[...] += dot_nt(acts_ref[:, 2 * ff :], w_ref[:, 2 * ff :])
    accx_ref[...] += dot_nt(acts_ref[:, : 2 * ff], w_ref[:, : 2 * ff])
    out_ref[:, : 2 * ff] = dot_nn(xt_ref[...], acts_ref[:, : 2 * ff]).astype(bf16)
    out_ref[:, 2 * ff :] = (dot_nn(dyt_ref[...], acts_ref[:, 2 * ff :]) * RES).astype(bf16)

    @pl.when(e == pl.num_programs(0) - 1)
    def _():
        width = accx_ref.shape[1]
        dg = dg_ref[...]
        high = dg.astype(bf16).astype(f32)
        mid = (dg - high).astype(bf16).astype(f32)
        low = dg - high - mid
        dg_ref[...] = high + pltpu.roll(mid, 32, 1) + pltpu.roll(low, 64, 1)

        def give(ref, k, rows):
            ref[k, :, :width] = accx_ref[rows, :].astype(bf16)
            ref[k, :, width:] = dg_ref[rows, :].astype(bf16)

        def give_mix(ref, k, rows):
            ref[k] = accm_ref[rows, :].astype(bf16)

        split_blocks(at_ref, give, mine_ref, theirs_ref, mine_ref.shape[1])
        split_blocks(at_ref, give_mix, mix_mine_ref, mix_theirs_ref, mine_ref.shape[1])


def params(mb):
    return pltpu.CompilerParams(vmem_limit_bytes=mb * VMEM_MB)


def attend(x_all, gain, weights, cos, sin, begin):
    total, width = x_all.shape
    shape = lambda n, w: jax.ShapeDtypeStruct((n, w), bf16)
    one = shape(total, LANES)
    return pl.pallas_call(
        attend_kernel,
        out_shape=(shape(total, width), one, one, one, shape(total + width, LANES)),
        compiler_params=params(48),
    )(x_all, gain, weights, cos, sin, begin)


def attend_back(at, *ins):
    total, width = ins[0].shape
    block = jax.ShapeDtypeStruct((4, total // 8, width), bf16)
    outs = (
        block,
        block,
        jax.ShapeDtypeStruct((1, width), f32),
        jax.ShapeDtypeStruct((total, 2 * LANES), bf16),
    )
    return pl.pallas_call(
        attend_back_kernel,
        grid_spec=pltpu.PrefetchScalarGridSpec(
            num_scalar_prefetch=1,
            grid=(1,),
            in_specs=[whole(v) for v in ins],
            out_specs=[whole(v) for v in outs],
            scratch_shapes=[
                pltpu.VMEM((total, LANES), bf16),
                pltpu.VMEM((total, LANES), f32),
                pltpu.VMEM((total, LANES), f32),
                pltpu.VMEM((total, width), bf16),
            ],
        ),
        out_shape=outs,
        compiler_params=params(32),
    )(at, *ins)


def attend_weights(*ins, kinds):
    width = ins[3].shape[1]
    return pl.pallas_call(
        attend_weights_kernel,
        out_shape=(
            jax.ShapeDtypeStruct((width, 3 * LANES), bf16),
            jax.ShapeDtypeStruct((kinds, width), f32),
        ),
        compiler_params=params(24),
    )(*ins)


def experts(at, x, dy, gates, weights, count):
    total, width = x.shape
    ff = weights.shape[1] // (3 * count)
    block = jax.ShapeDtypeStruct((4, total // 8, width + LANES), bf16)
    mix = jax.ShapeDtypeStruct((4, total // 8, width), bf16)
    each = pl.BlockSpec((width, 3 * ff), lambda e, at: (0, e))
    return pl.pallas_call(
        experts_kernel,
        grid_spec=pltpu.PrefetchScalarGridSpec(
            num_scalar_prefetch=1,
            grid=(count,),
            in_specs=[whole(x), whole(dy), whole(gates), each],
            out_specs=[whole(block), whole(block), whole(mix), whole(mix), each],
            scratch_shapes=[
                pltpu.VMEM((total, 3 * ff), bf16),
                pltpu.VMEM((width, total), bf16),
                pltpu.VMEM((width, total), bf16),
                pltpu.VMEM((total, width), f32),
                pltpu.VMEM((total, width), f32),
                pltpu.VMEM((total, LANES), f32),
            ],
        ),
        out_shape=(block, block, mix, mix, jax.ShapeDtypeStruct((width, 3 * ff * count), bf16)),
        compiler_params=params(60),
        cost_estimate=pl.CostEstimate(
            flops=18 * total * width * ff * count,
            bytes_accessed=4 * width * 3 * ff * count,
            transcendentals=total * ff * count,
        ),
    )(at, x, dy, gates, weights)


def tables(lengths_row, group):
    ends = jnp.cumsum(lengths_row)
    starts = ends - lengths_row
    places = jnp.arange(group, dtype=jnp.int32)
    inside = (places[:, None] >= starts[None, :]) & (places[:, None] < ends[None, :])
    begin = jnp.sum(jnp.where(inside, starts[None, :], 0), axis=1)
    frequency = BASE ** (-(jnp.arange(HEAD // 2, dtype=f32) * 2.0 / HEAD))
    angles = (places - begin).astype(f32)[:, None] * frequency[None, :]
    cos, sin = jnp.cos(angles), jnp.sin(angles)
    return (
        begin.reshape(1, group),
        jnp.concatenate([cos] * 4, axis=1),
        jnp.concatenate([-sin, sin, -sin, sin], axis=1),
    )


def local(
    layer_input, lengths, choices, query_weight, key_matrix, value_matrix, project_weight,
    gate_weight, up_weight, down_weight, router_weight, attention_gain, expert_gain, grad_output,
):
    me = lax.axis_index("col")
    tokens, width = layer_input.shape
    group = tokens * 8
    kinds = router_weight.shape[1]
    count, _, ff = gate_weight.shape
    own = lambda v: lax.dynamic_slice_in_dim(v, me * tokens, tokens, axis=0)

    at = jnp.stack([me // 2, me % 2]).astype(jnp.int32)
    spots = jnp.arange(LANES, dtype=jnp.int32)
    named = jnp.any(choices[:, :, None] == spots[None, None, :], axis=1).astype(bf16)
    share = pack(gate_weight, up_weight, down_weight)
    expert_weights = lax.all_gather(share, "row", axis=0, tiled=True)
    small = gather_row_small(
        jnp.concatenate([query_weight, key_matrix, value_matrix, project_weight.T], axis=1)
    )
    *entering, small = gather_col(jnp.concatenate([layer_input, grad_output, named], axis=1), at, small)
    x_all, dy_all, named_all = merge(at, *entering, (width, width, LANES))

    begin, cos, sin = tables(lengths[0], group)
    gain_one = attention_gain.reshape(1, width)
    normed, q, kk, vv, heads = attend(x_all, gain_one, small, cos, sin, begin)
    heads_mine, heads_other, _ = gather_col(heads, at)
    router = router_weight.T
    gain_two = expert_gain.reshape(1, width)
    expert_in, gates_all, middle, gates = project(
        at, heads_mine, heads_other, x_all, named_all, gain_two, router
    )
    mine, theirs, mix_mine, mix_theirs, expert_wgrad = experts(
        at, expert_in, dy_all, gates_all, expert_weights, count
    )
    expert_sum = lax.psum_scatter(expert_wgrad, "row", scatter_dimension=0, tiled=True)

    arrived, _ = sum_col([(mine, core_swap(theirs))])
    middle_grad, sent, gain_two_part = turn(*arrived, middle, gates, grad_output, gain_two, router)
    back_mine, back_other, _ = gather_col(sent, at)
    ag_all, logits_all = merge(at, back_mine, back_other, (width, LANES))

    dn_mine, dn_theirs, gain_part, dqkv = attend_back(
        at, ag_all, q, kk, vv, heads, x_all, cos, sin, begin, small
    )
    sent = []

    def opening(_):
        wg, rows = attend_weights(dqkv, normed, heads, ag_all, expert_in, logits_all, kinds=kinds)
        sent.append(exchange_row(wg))
        return row_step(jnp.concatenate([rows, gain_two_part, gain_part], axis=0), 1)

    def third(rows):
        return row_step(rows, 4), sent[0]

    pairs = [(dn_mine, core_swap(dn_theirs)), (mix_mine, core_swap(mix_theirs))]
    terms, (rows, pieces) = sum_col(pairs, None, [opening, lambda v: row_step(v, 2), third])
    input_grad, block_output = close(*terms, layer_input, middle_grad, gain_one, middle)
    rows = row_step(rows, 8)
    both = jnp.concatenate(two_parts(rows[kinds:]), axis=0)
    gains = jnp.sum(send_all(both, "col").astype(f32), axis=0)
    gains = gains[:2] + gains[2:]
    small_sum = jnp.sum(pieces.astype(f32), axis=0)
    gate_grad, up_grad, down_grad = unpack(expert_sum, count, ff)
    return (
        block_output,
        input_grad,
        small_sum[:, :LANES],
        small_sum[:, LANES : LANES + HEAD],
        small_sum[:, LANES + HEAD : 2 * LANES],
        small_sum[:, 2 * LANES :].T,
        gate_grad,
        up_grad,
        down_grad,
        rows[:kinds].T,
        gains[1],
        gains[0],
    )


def solution(mesh):
    both = P(("row", "col"), None)
    in_specs = (
        both, P("row", None), both, P("row", "col"), P("row", "col"), P("row", "col"), P("col", "row"),
        P("col", "row", None), P("col", "row", None), P("col", None, "row"), P(), P(), P(), both,
    )
    out_specs = (
        both, both, P("row", "col"), P("row", "col"), P("row", "col"), P("col", "row"),
        P("col", "row", None), P("col", "row", None), P("col", None, "row"), P(), P(), P(),
    )
    return jax.shard_map(local, mesh=mesh, in_specs=in_specs, out_specs=out_specs, check_vma=False)
```

```python
import functools

import jax
import jax.numpy as jnp
from jax import lax
from jax.experimental import pallas as pl
from jax.experimental.pallas import tpu as pltpu
from jax.sharding import PartitionSpec as P

HEAD = 64
LANES = 128
QB = 256
EPS = 1e-06
RES = 0.22
SCALE = 0.125
BASE = 10000.0
bf16 = jnp.bfloat16
f32 = jnp.float32
VMEM_MB = 1 << 20


def dot_nt(a, b):
    return lax.dot_general(a, b, (((1,), (1,)), ((), ())), preferred_element_type=f32)


def dot_nn(a, b):
    return lax.dot_general(a, b, (((1,), (0,)), ((), ())), preferred_element_type=f32)


def rms_scale(values, gain_vec):
    return values * lax.rsqrt(jnp.mean(values * values, axis=-1, keepdims=True) + EPS) * gain_vec


def core_swap(a):
    return lax.ppermute(a, "col", [(i, i ^ 1) for i in range(8)])


def z_shift(a, d):
    return lax.ppermute(a, "col", [(i, (i + 2 * d) % 8) for i in range(8)])


def y_shift(a, d):
    return lax.ppermute(a, "row", [(i, (i // 4) * 4 + (i + d) % 4) for i in range(16)])


def x_shift(a, d):
    return lax.ppermute(a, "row", [(i, (i + 4 * d) % 16) for i in range(16)])


def gather_col(a, at, beside=None):
    half = a.shape[0] // 2
    back = z_shift(a, 1)
    ahead = z_shift(a, -1)
    if beside is not None:
        back, ahead, beside = lax.optimization_barrier((back, ahead, beside))
    far0 = z_shift(back[:half], 1)
    far1 = z_shift(ahead[half:], -1)
    mine = pl.pallas_call(
        place_kernel,
        grid_spec=pltpu.PrefetchScalarGridSpec(
            num_scalar_prefetch=1,
            grid=(1,),
            in_specs=[whole(v) for v in (a, back, ahead, far0, far1)],
            out_specs=pl.BlockSpec((4,) + a.shape, lambda g, at: (0, 0, 0)),
        ),
        out_shape=jax.ShapeDtypeStruct((4,) + a.shape, a.dtype),
        compiler_params=params(24),
    )(at, a, back, ahead, far0, far1)
    return mine, core_swap(mine), beside


def sum_col(pairs, beside=None, steps=()):
    steps = list(steps)

    def phase(*values):
        nonlocal beside
        if steps:
            beside = steps.pop(0)(beside)
            values, beside = lax.optimization_barrier((values, beside))
        return values

    pairs = phase(*pairs)
    own, ahead, behind, far0, far1 = fold(*pairs)
    via_up, via_down = phase(z_shift(far0, 1), z_shift(far1, -1))
    up, down = join(ahead, behind, via_up, via_down)
    up, down = phase(z_shift(up, 1), z_shift(down, -1))
    return (own, up, down), beside


def gather_row_small(a):
    ways = lax.axis_size("row")
    sent = jnp.broadcast_to(a[None], (ways,) + a.shape)
    return lax.all_to_all(sent, "row", 0, 0, tiled=True).reshape(-1, a.shape[1])


def exchange_row(a):
    ways = lax.axis_size("row")
    return lax.all_to_all(a.reshape(ways, -1, a.shape[1]), "row", 0, 0, tiled=True)


def send_all(a, axis):
    sent = jnp.broadcast_to(a[None], (lax.axis_size(axis),) + a.shape)
    return lax.all_to_all(sent, axis, 0, 0, tiled=True)


def two_parts(v):
    high = v.astype(bf16)
    return high, (v - high.astype(f32)).astype(bf16)


def row_step(v, bit):
    low = v.astype(bf16)
    got = lax.ppermute(low, "row", [(i, i ^ bit) for i in range(16)])
    return low.astype(f32) + got.astype(f32)


def lane_of(shape):
    return lax.broadcasted_iota(jnp.int32, shape, 1)


def rotate(values, cos, sin):
    first = (lane_of(values.shape) % HEAD) < HEAD // 2
    swapped = jnp.where(first, pltpu.roll(values, 96, 1), pltpu.roll(values, 32, 1))
    return values * cos + swapped * sin


def allowed_keys(lo, count, row0, begin):
    key = lax.broadcasted_iota(jnp.int32, (count, QB), 0) + lo
    query = lax.broadcasted_iota(jnp.int32, (count, QB), 1) + row0
    return (key >= begin) & (key <= query)


def soft(kk, qh, ok):
    s = jnp.where(ok, dot_nt(kk, qh) * SCALE, -1e30)
    raised = jnp.exp(s - jnp.max(s, axis=0, keepdims=True))
    return raised / jnp.sum(raised, axis=0, keepdims=True)


def key_range(i):
    return max(0, i - 2) * QB, (i + 1) * QB


def whole(v):
    return pl.BlockSpec(v.shape, lambda g, at, r=len(v.shape): (0,) * r)


def fold_kernel(*refs):
    own_ref, ahead_ref, behind_ref, far0_ref, far1_ref = refs[-5:]
    half = far0_ref.shape[0]
    at = 0
    for mine, got in zip(refs[:-5:2], refs[1:-5:2]):
        cols = slice(at, at + mine.shape[-1])
        at += mine.shape[-1]
        add = lambda k: mine[k].astype(f32) + got[k].astype(f32)
        own_ref[:, cols] = add(0)
        ahead_ref[:, cols] = add(1)
        behind_ref[:, cols] = add(3)
        far = add(2).astype(bf16)
        far0_ref[:, cols] = far[:half]
        far1_ref[:, cols] = far[half:]


def fold(*pairs):
    n = pairs[0][0].shape[1]
    w = sum(mine.shape[2] for mine, _ in pairs)
    one = jax.ShapeDtypeStruct((n, w), f32)
    part = jax.ShapeDtypeStruct((n // 2, w), bf16)
    return pl.pallas_call(
        fold_kernel, out_shape=(one, one, one, part, part), compiler_params=params(24)
    )(*[v for pair in pairs for v in pair])


def join_kernel(ahead_ref, behind_ref, via_up_ref, via_down_ref, up_ref, down_ref):
    half = via_up_ref.shape[0]
    up_ref[:half] = (ahead_ref[:half] + via_up_ref[...].astype(f32)).astype(bf16)
    up_ref[half:] = ahead_ref[half:].astype(bf16)
    down_ref[:half] = behind_ref[:half].astype(bf16)
    down_ref[half:] = (behind_ref[half:] + via_down_ref[...].astype(f32)).astype(bf16)


def join(ahead, behind, via_up, via_down):
    one = jax.ShapeDtypeStruct(ahead.shape, bf16)
    return pl.pallas_call(join_kernel, out_shape=(one, one), compiler_params=params(24))(
        ahead, behind, via_up, via_down
    )


def norm_back(x, grad, gain):
    inv = lax.rsqrt(jnp.mean(x * x, axis=-1, keepdims=True) + EPS)
    scaled = grad * gain
    hat = x * inv
    return inv * (scaled - hat * jnp.mean(hat * scaled, axis=-1, keepdims=True)), hat


def turn_kernel(
    own_ref, up_ref, down_ref, middle_ref, gates_ref, grad_ref, gain_ref, router_ref,
    back_ref, sent_ref, gain_part_ref,
):
    width = middle_ref.shape[1]
    arrived = own_ref[...] + up_ref[...].astype(f32) + down_ref[...].astype(f32)
    middle = middle_ref[...]
    parts = arrived[:, width:]
    gates_grad = parts + pltpu.roll(parts, 96, 1) + pltpu.roll(parts, 64, 1)
    gates = gates_ref[...]
    logits_grad = gates * (gates_grad - jnp.sum(gates * gates_grad, axis=1, keepdims=True))
    high = logits_grad.astype(bf16)
    rest = logits_grad - high.astype(f32)
    low = rest.astype(bf16)
    router = widened(router_ref[...])
    grad = arrived[:, :width] + dot_nn(high, router) + dot_nn(low, router)
    back, hat = norm_back(middle, grad, gain_ref[...])
    back = grad_ref[...].astype(f32) + back
    back_ref[...] = back
    sent_ref[:, :width] = (RES * back).astype(bf16)
    sent_ref[:, width:] = (high.astype(f32) + pltpu.roll(low.astype(f32), HEAD, 1)).astype(bf16)
    gain_part_ref[...] = jnp.sum(grad * hat, axis=0, keepdims=True)


def turn(own, up, down, middle, gates, grad, gain, router):
    n, width = middle.shape
    return pl.pallas_call(
        turn_kernel,
        out_shape=(
            jax.ShapeDtypeStruct((n, width), f32),
            jax.ShapeDtypeStruct((n, width + LANES), bf16),
            jax.ShapeDtypeStruct((1, width), f32),
        ),
        compiler_params=params(24),
    )(own, up, down, middle, gates, grad, gain, router)


def close_kernel(own_ref, up_ref, down_ref, x_ref, back_ref, gain_ref, middle_ref, out_ref, block_ref):
    width = out_ref.shape[1]
    arrived = own_ref[...] + up_ref[...].astype(f32) + down_ref[...].astype(f32)
    grad = arrived[:, :width]
    out_ref[...] = back_ref[...] + norm_back(x_ref[...].astype(f32), grad, gain_ref[...])[0]
    block_ref[...] = middle_ref[...] + RES * arrived[:, width:]


def close(own, up, down, x, back, gain, middle):
    one = jax.ShapeDtypeStruct(middle.shape, f32)
    return pl.pallas_call(close_kernel, out_shape=(one, one), compiler_params=params(24))(
        own, up, down, x, back, gain, middle
    )


def place_kernel(at_ref, own_ref, back_ref, ahead_ref, far0_ref, far1_ref, out_ref):
    z = at_ref[0]
    half = own_ref.shape[0] // 2
    out_ref[z] = own_ref[...]
    out_ref[lax.rem(z + 3, 4)] = back_ref[...]
    out_ref[lax.rem(z + 1, 4)] = ahead_ref[...]
    out_ref[lax.rem(z + 2, 4), :half] = far0_ref[...]
    out_ref[lax.rem(z + 2, 4), half:] = far1_ref[...]


def merge_kernel(at_ref, mine_ref, other_ref, *refs):
    core = at_ref[1]
    for k in range(4):
        for src, c in ((mine_ref, core), (other_ref, 1 - core)):
            at = 0
            for ref in refs:
                w = ref.shape[-1]
                ref[k, c] = src[k, :, at : at + w]
                at += w


def merge(at, mine, other, widths):
    _, n, _ = mine.shape
    outs = [jax.ShapeDtypeStruct((4, 2, n, w), bf16) for w in widths]
    found = pl.pallas_call(
        merge_kernel,
        grid_spec=pltpu.PrefetchScalarGridSpec(
            num_scalar_prefetch=1,
            grid=(1,),
            in_specs=[whole(mine), whole(other)],
            out_specs=[whole(v) for v in outs],
        ),
        out_shape=outs,
        compiler_params=params(24),
    )(at, mine, other)
    return [v.reshape(8 * n, v.shape[-1]) for v in found]


def pack_kernel(g_ref, u_ref, d_ref, share_ref):
    count, _, ff = g_ref.shape
    for e in range(count):
        at = 3 * ff * e
        share_ref[:, at : at + ff] = g_ref[e]
        share_ref[:, at + ff : at + 2 * ff] = u_ref[e]
        share_ref[:, at + 2 * ff : at + 3 * ff] = d_ref[e]


def pack(gate, up, down):
    count, n, ff = gate.shape
    return pl.pallas_call(
        pack_kernel,
        out_shape=jax.ShapeDtypeStruct((n, 3 * ff * count), bf16),
        compiler_params=params(60),
    )(gate, up, jnp.swapaxes(down, 1, 2))


def unpack_kernel(s_ref, g_ref, u_ref, d_ref):
    count, _, ff = g_ref.shape
    for e in range(count):
        at = 3 * ff * e
        g_ref[e] = s_ref[:, at : at + ff].astype(f32)
        u_ref[e] = s_ref[:, at + ff : at + 2 * ff].astype(f32)
        d_ref[e] = s_ref[:, at + 2 * ff : at + 3 * ff].astype(f32)


def unpack(share, count, ff):
    n = share.shape[0]
    block = jax.ShapeDtypeStruct((count, n, ff), f32)
    gate, up, down = pl.pallas_call(
        unpack_kernel,
        out_shape=(block, block, block),
        compiler_params=params(24),
    )(share)
    return gate, up, jnp.swapaxes(down, 1, 2)


def widened(router):
    kinds, width = router.shape
    return jnp.concatenate([router, jnp.zeros((LANES - kinds, width), router.dtype)], axis=0)


def project_kernel(
    at_ref, mine_ref, other_ref, x_ref, named_ref, gain_ref, router_ref, in_ref, gates_ref, own_ref, own_gates_ref, ctx_ref, wp_ref
):
    core = at_ref[1]
    total, width = x_ref.shape
    for k in range(4):
        for src, c in ((mine_ref, core), (other_ref, 1 - core)):
            lanes = pl.ds(pl.multiple_of((2 * k + c) * LANES, LANES), LANES)
            ctx_ref[:, lanes] = src[k, :total]
            wp_ref[:, lanes] = src[k, total:]
    me = 2 * at_ref[0] + core
    tokens = own_ref.shape[0]
    router = widened(router_ref[...])
    for i in range(total // QB):
        rows = pl.ds(i * QB, QB)
        middle = x_ref[rows, :].astype(f32) + RES * dot_nt(ctx_ref[rows, :], wp_ref[...])
        normed = rms_scale(middle, gain_ref[...]).astype(bf16)
        in_ref[rows, :] = normed
        logits = jnp.where(named_ref[rows, :] > 0, dot_nt(normed, router), -1e30)
        raised = jnp.exp(logits - jnp.max(logits, axis=1, keepdims=True))
        gates = raised / jnp.sum(raised, axis=1, keepdims=True)
        gates_ref[rows, :] = gates
        for half in range(QB // tokens):

            @pl.when(me == i * (QB // tokens) + half)
            def _():
                own_ref[...] = middle[half * tokens : (half + 1) * tokens]
                own_gates_ref[...] = gates[half * tokens : (half + 1) * tokens]


def project(at, mine, other, x, named, gain, router):
    total, width = x.shape
    outs = (
        jax.ShapeDtypeStruct((total, width), bf16),
        jax.ShapeDtypeStruct((total, LANES), f32),
        jax.ShapeDtypeStruct((total // 8, width), f32),
        jax.ShapeDtypeStruct((total // 8, LANES), f32),
    )
    ins = (mine, other, x, named, gain, router)
    return pl.pallas_call(
        project_kernel,
        grid_spec=pltpu.PrefetchScalarGridSpec(
            num_scalar_prefetch=1,
            grid=(1,),
            in_specs=[whole(v) for v in ins],
            out_specs=[whole(v) for v in outs],
            scratch_shapes=[pltpu.VMEM((total, width), bf16), pltpu.VMEM((total, width), bf16)],
        ),
        out_shape=outs,
        compiler_params=params(60),
    )(at, *ins)


def split_blocks(at_ref, value_of, mine_ref, theirs_ref, n):
    z, core = at_ref[0], at_ref[1]
    for k in range(4):
        there = lax.rem(z + k, 4) * 2
        for ref, c in ((mine_ref, core), (theirs_ref, 1 - core)):
            value_of(ref, k, pl.ds(pl.multiple_of((there + c) * n, n), n))


def attend_kernel(x_ref, gain_ref, w_ref, cos_ref, sin_ref, begin_ref, n_ref, q_ref, kk_ref, vv_ref, heads_ref):
    total = x_ref.shape[0]
    left = lane_of((QB, LANES)) < HEAD
    for i in range(total // QB):
        rows = pl.ds(i * QB, QB)
        x = x_ref[rows, :].astype(f32)
        normed = rms_scale(x, gain_ref[...]).astype(bf16)
        n_ref[rows, :] = normed
        raw = dot_nn(normed, w_ref[:, : 2 * LANES])
        cos, sin = cos_ref[rows, :], sin_ref[rows, :]
        q_ref[rows, :] = rotate(raw[:, :LANES], cos, sin).astype(bf16)
        kv = raw[:, LANES:]
        turned = rotate(kv, cos, sin)
        kk_ref[rows, :] = jnp.where(left, turned, pltpu.roll(turned, HEAD, 1)).astype(bf16)
        vv_ref[rows, :] = jnp.where(left, pltpu.roll(kv, HEAD, 1), kv).astype(bf16)
    vt = vv_ref[...].astype(f32).T.astype(bf16)
    upper = lax.broadcasted_iota(jnp.int32, (LANES, QB), 0) < HEAD
    for i in range(total // QB):
        rows = pl.ds(i * QB, QB)
        lo, hi = key_range(i)
        keys = kk_ref[lo:hi, :]
        ok = allowed_keys(lo, hi - lo, i * QB, begin_ref[:, i * QB : (i + 1) * QB])
        found = []
        for h in range(2):
            qh = jnp.where(left == (h == 0), q_ref[rows, :], jnp.zeros((QB, LANES), bf16))
            p = soft(keys, qh, ok).astype(bf16)
            found.append(dot_nn(vt[:, lo:hi], p))
        heads_ref[rows, :] = jnp.where(upper, found[0], found[1]).T.astype(bf16)
    heads_ref[total:, :] = w_ref[:, 2 * LANES :]


def attend_back_kernel(
    at_ref, ag_ref, q_ref, kk_ref, vv_ref, heads_ref, x_ref, cos_ref, sin_ref, begin_ref, w_ref,
    mine_ref, theirs_ref, gain_ref, dqkv_ref, dctx_ref, dk_ref, dv_ref, dn_ref,
):
    total = ag_ref.shape[0]
    left = lane_of((QB, LANES)) < HEAD
    upper = lax.broadcasted_iota(jnp.int32, (LANES, QB), 0) < HEAD
    dctx_ref[...] = dot_nn(ag_ref[...], heads_ref[total:, :]).astype(bf16)
    dk_ref[...] = jnp.zeros_like(dk_ref)
    dv_ref[...] = jnp.zeros_like(dv_ref)
    kt = kk_ref[...].astype(f32).T.astype(bf16)
    for i in range(total // QB):
        rows = pl.ds(i * QB, QB)
        lo, hi = key_range(i)
        keys = kk_ref[lo:hi, :]
        ok = allowed_keys(lo, hi - lo, i * QB, begin_ref[:, i * QB : (i + 1) * QB])
        found = []
        for h in range(2):
            mine = left == (h == 0)
            qh = jnp.where(mine, q_ref[rows, :], jnp.zeros((QB, LANES), bf16))
            dch = jnp.where(mine, dctx_ref[rows, :], jnp.zeros((QB, LANES), bf16))
            p = soft(keys, qh, ok)
            dp = dot_nt(vv_ref[lo:hi, :], dch)
            ds = (p * (dp - jnp.sum(dp * p, axis=0, keepdims=True))).astype(bf16)
            dk_ref[lo:hi, :] += dot_nn(ds, qh)
            dv_ref[lo:hi, :] += dot_nn(p.astype(bf16), dch)
            found.append(dot_nn(kt[:, lo:hi], ds))
        dq = jnp.where(upper, found[0], found[1]).T * SCALE
        dqkv_ref[rows, :LANES] = rotate(dq, cos_ref[rows, :], -sin_ref[rows, :]).astype(bf16)
    acc = jnp.zeros((1, x_ref.shape[1]), f32)
    for i in range(total // QB):
        rows = pl.ds(i * QB, QB)
        dk, dv = dk_ref[rows, :], dv_ref[rows, :]
        dk = (dk + pltpu.roll(dk, HEAD, 1)) * SCALE
        dk = rotate(dk, cos_ref[rows, :], -sin_ref[rows, :])
        dv = dv + pltpu.roll(dv, HEAD, 1)
        dqkv_ref[rows, LANES:] = jnp.where(left, dk, dv).astype(bf16)
        dn = dot_nt(dqkv_ref[rows, :], w_ref[:, : 2 * LANES])
        dn_ref[rows, :] = dn.astype(bf16)
        x = x_ref[rows, :].astype(f32)
        hat = x * lax.rsqrt(jnp.mean(x * x, axis=-1, keepdims=True) + EPS)
        acc = acc + jnp.sum(dn * hat, axis=0, keepdims=True)
    gain_ref[...] = acc

    def give(ref, k, rows):
        ref[k] = dn_ref[rows, :]

    split_blocks(at_ref, give, mine_ref, theirs_ref, mine_ref.shape[1])


def attend_weights_kernel(dqkv_ref, normed_ref, heads_ref, ag_ref, in_ref, dl_ref, wg_ref, rows_ref):
    total = ag_ref.shape[0]
    dqkv_t = dqkv_ref[...].astype(f32).T.astype(bf16)
    ctx_t = heads_ref[:total, :].astype(f32).T.astype(bf16)
    wg_ref[:, : 2 * LANES] = dot_nn(dqkv_t, normed_ref[...]).T.astype(bf16)
    wg_ref[:, 2 * LANES :] = dot_nn(ctx_t, ag_ref[...]).T.astype(bf16)
    parts = dot_nn(dl_ref[...].astype(f32).T.astype(bf16), in_ref[...])
    rows_ref[...] = parts[: rows_ref.shape[0]] + parts[HEAD : HEAD + rows_ref.shape[0]]


def experts_kernel(
    at_ref, x_ref, dy_ref, gates_ref, w_ref, mine_ref, theirs_ref, mix_mine_ref, mix_theirs_ref, out_ref,
    acts_ref, xt_ref, dyt_ref, accm_ref, accx_ref, dg_ref,
):
    e = pl.program_id(0)
    ff = acts_ref.shape[1] // 3
    total = x_ref.shape[0]
    lane = lane_of((total, LANES))
    pick = (2 * at_ref[0] + at_ref[1]) * pl.num_programs(0) + e

    @pl.when(e == 0)
    def _():
        xt_ref[...] = x_ref[...].T
        dyt_ref[...] = dy_ref[...].T
        accm_ref[...] = jnp.zeros_like(accm_ref)
        accx_ref[...] = jnp.zeros_like(accx_ref)
        dg_ref[...] = jnp.zeros_like(dg_ref)

    gu = dot_nn(x_ref[...], w_ref[:, : 2 * ff])
    h0 = dot_nn(dy_ref[...], w_ref[:, 2 * ff :]) * RES
    g, u = gu[:, :ff], gu[:, ff:]
    gate = jnp.sum(jnp.where(lane == pick, gates_ref[...], 0.0), axis=1, keepdims=True)
    sg = jax.nn.sigmoid(g)
    sw = g * sg
    hid = sw * u
    dg = jnp.sum(hid * h0, axis=1, keepdims=True)
    dg_ref[...] += jnp.where(lane == pick, dg, 0.0)
    acts_ref[:, 2 * ff :] = (gate * hid).astype(bf16)
    dh = gate * h0
    acts_ref[:, :ff] = (dh * u * sg * (1.0 + g * (1.0 - sg))).astype(bf16)
    acts_ref[:, ff : 2 * ff] = (dh * sw).astype(bf16)
    accm_ref[...] += dot_nt(acts_ref[:, 2 * ff :], w_ref[:, 2 * ff :])
    accx_ref[...] += dot_nt(acts_ref[:, : 2 * ff], w_ref[:, : 2 * ff])
    out_ref[:, : 2 * ff] = dot_nn(xt_ref[...], acts_ref[:, : 2 * ff]).astype(bf16)
    out_ref[:, 2 * ff :] = (dot_nn(dyt_ref[...], acts_ref[:, 2 * ff :]) * RES).astype(bf16)

    @pl.when(e == pl.num_programs(0) - 1)
    def _():
        width = accx_ref.shape[1]
        dg = dg_ref[...]
        high = dg.astype(bf16).astype(f32)
        mid = (dg - high).astype(bf16).astype(f32)
        low = dg - high - mid
        dg_ref[...] = high + pltpu.roll(mid, 32, 1) + pltpu.roll(low, 64, 1)

        def give(ref, k, rows):
            ref[k, :, :width] = accx_ref[rows, :].astype(bf16)
            ref[k, :, width:] = dg_ref[rows, :].astype(bf16)

        def give_mix(ref, k, rows):
            ref[k] = accm_ref[rows, :].astype(bf16)

        split_blocks(at_ref, give, mine_ref, theirs_ref, mine_ref.shape[1])
        split_blocks(at_ref, give_mix, mix_mine_ref, mix_theirs_ref, mine_ref.shape[1])


def params(mb):
    return pltpu.CompilerParams(vmem_limit_bytes=mb * VMEM_MB)


def attend(x_all, gain, weights, cos, sin, begin):
    total, width = x_all.shape
    shape = lambda n, w: jax.ShapeDtypeStruct((n, w), bf16)
    one = shape(total, LANES)
    return pl.pallas_call(
        attend_kernel,
        out_shape=(shape(total, width), one, one, one, shape(total + width, LANES)),
        compiler_params=params(48),
    )(x_all, gain, weights, cos, sin, begin)


def attend_back(at, *ins):
    total, width = ins[0].shape
    block = jax.ShapeDtypeStruct((4, total // 8, width), bf16)
    outs = (
        block,
        block,
        jax.ShapeDtypeStruct((1, width), f32),
        jax.ShapeDtypeStruct((total, 2 * LANES), bf16),
    )
    return pl.pallas_call(
        attend_back_kernel,
        grid_spec=pltpu.PrefetchScalarGridSpec(
            num_scalar_prefetch=1,
            grid=(1,),
            in_specs=[whole(v) for v in ins],
            out_specs=[whole(v) for v in outs],
            scratch_shapes=[
                pltpu.VMEM((total, LANES), bf16),
                pltpu.VMEM((total, LANES), f32),
                pltpu.VMEM((total, LANES), f32),
                pltpu.VMEM((total, width), bf16),
            ],
        ),
        out_shape=outs,
        compiler_params=params(32),
    )(at, *ins)


def attend_weights(*ins, kinds):
    width = ins[3].shape[1]
    return pl.pallas_call(
        attend_weights_kernel,
        out_shape=(
            jax.ShapeDtypeStruct((width, 3 * LANES), bf16),
            jax.ShapeDtypeStruct((kinds, width), f32),
        ),
        compiler_params=params(24),
    )(*ins)


def experts(at, x, dy, gates, weights, count):
    total, width = x.shape
    ff = weights.shape[1] // (3 * count)
    block = jax.ShapeDtypeStruct((4, total // 8, width + LANES), bf16)
    mix = jax.ShapeDtypeStruct((4, total // 8, width), bf16)
    each = pl.BlockSpec((width, 3 * ff), lambda e, at: (0, e))
    return pl.pallas_call(
        experts_kernel,
        grid_spec=pltpu.PrefetchScalarGridSpec(
            num_scalar_prefetch=1,
            grid=(count,),
            in_specs=[whole(x), whole(dy), whole(gates), each],
            out_specs=[whole(block), whole(block), whole(mix), whole(mix), each],
            scratch_shapes=[
                pltpu.VMEM((total, 3 * ff), bf16),
                pltpu.VMEM((width, total), bf16),
                pltpu.VMEM((width, total), bf16),
                pltpu.VMEM((total, width), f32),
                pltpu.VMEM((total, width), f32),
                pltpu.VMEM((total, LANES), f32),
            ],
        ),
        out_shape=(block, block, mix, mix, jax.ShapeDtypeStruct((width, 3 * ff * count), bf16)),
        compiler_params=params(60),
        cost_estimate=pl.CostEstimate(
            flops=18 * total * width * ff * count,
            bytes_accessed=4 * width * 3 * ff * count,
            transcendentals=total * ff * count,
        ),
    )(at, x, dy, gates, weights)


def tables(lengths_row, group):
    ends = jnp.cumsum(lengths_row)
    starts = ends - lengths_row
    places = jnp.arange(group, dtype=jnp.int32)
    inside = (places[:, None] >= starts[None, :]) & (places[:, None] < ends[None, :])
    begin = jnp.sum(jnp.where(inside, starts[None, :], 0), axis=1)
    frequency = BASE ** (-(jnp.arange(HEAD // 2, dtype=f32) * 2.0 / HEAD))
    angles = (places - begin).astype(f32)[:, None] * frequency[None, :]
    cos, sin = jnp.cos(angles), jnp.sin(angles)
    return (
        begin.reshape(1, group),
        jnp.concatenate([cos] * 4, axis=1),
        jnp.concatenate([-sin, sin, -sin, sin], axis=1),
    )


def local(
    layer_input, lengths, choices, query_weight, key_matrix, value_matrix, project_weight,
    gate_weight, up_weight, down_weight, router_weight, attention_gain, expert_gain, grad_output,
):
    me = lax.axis_index("col")
    tokens, width = layer_input.shape
    group = tokens * 8
    kinds = router_weight.shape[1]
    count, _, ff = gate_weight.shape
    own = lambda v: lax.dynamic_slice_in_dim(v, me * tokens, tokens, axis=0)

    at = jnp.stack([me // 2, me % 2]).astype(jnp.int32)
    spots = jnp.arange(LANES, dtype=jnp.int32)
    named = jnp.any(choices[:, :, None] == spots[None, None, :], axis=1).astype(bf16)
    share = pack(gate_weight, up_weight, down_weight)
    expert_weights = lax.all_gather(share, "row", axis=0, tiled=True)
    small = gather_row_small(
        jnp.concatenate([query_weight, key_matrix, value_matrix, project_weight.T], axis=1)
    )
    *entering, small = gather_col(jnp.concatenate([layer_input, grad_output, named], axis=1), at, small)
    x_all, dy_all, named_all = merge(at, *entering, (width, width, LANES))

    begin, cos, sin = tables(lengths[0], group)
    gain_one = attention_gain.reshape(1, width)
    normed, q, kk, vv, heads = attend(x_all, gain_one, small, cos, sin, begin)
    heads_mine, heads_other, _ = gather_col(heads, at)
    router = router_weight.T
    gain_two = expert_gain.reshape(1, width)
    expert_in, gates_all, middle, gates = project(
        at, heads_mine, heads_other, x_all, named_all, gain_two, router
    )
    mine, theirs, mix_mine, mix_theirs, expert_wgrad = experts(
        at, expert_in, dy_all, gates_all, expert_weights, count
    )
    expert_sum = lax.psum_scatter(expert_wgrad, "row", scatter_dimension=0, tiled=True)

    arrived, _ = sum_col([(mine, core_swap(theirs))])
    middle_grad, sent, gain_two_part = turn(*arrived, middle, gates, grad_output, gain_two, router)
    back_mine, back_other, _ = gather_col(sent, at)
    ag_all, logits_all = merge(at, back_mine, back_other, (width, LANES))

    dn_mine, dn_theirs, gain_part, dqkv = attend_back(
        at, ag_all, q, kk, vv, heads, x_all, cos, sin, begin, small
    )
    sent = []

    def opening(_):
        wg, rows = attend_weights(dqkv, normed, heads, ag_all, expert_in, logits_all, kinds=kinds)
        sent.append(exchange_row(wg))
        return jnp.concatenate([rows, gain_two_part, gain_part], axis=0)

    def third(rows):
        return row_step(rows, 2), sent[0]

    pairs = [(dn_mine, core_swap(dn_theirs)), (mix_mine, core_swap(mix_theirs))]
    terms, (rows, pieces) = sum_col(pairs, None, [opening, lambda v: row_step(v, 1), third])
    input_grad, block_output = close(*terms, layer_input, middle_grad, gain_one, middle)
    rows = row_step(row_step(rows, 4), 8)
    both = jnp.concatenate(two_parts(rows[kinds:]), axis=0)
    gains = jnp.sum(send_all(both, "col").astype(f32), axis=0)
    gains = gains[:2] + gains[2:]
    small_sum = jnp.sum(pieces.astype(f32), axis=0)
    gate_grad, up_grad, down_grad = unpack(expert_sum, count, ff)
    return (
        block_output,
        input_grad,
        small_sum[:, :LANES],
        small_sum[:, LANES : LANES + HEAD],
        small_sum[:, LANES + HEAD : 2 * LANES],
        small_sum[:, 2 * LANES :].T,
        gate_grad,
        up_grad,
        down_grad,
        rows[:kinds].T,
        gains[1],
        gains[0],
    )


def solution(mesh):
    both = P(("row", "col"), None)
    in_specs = (
        both, P("row", None), both, P("row", "col"), P("row", "col"), P("row", "col"), P("col", "row"),
        P("col", "row", None), P("col", "row", None), P("col", None, "row"), P(), P(), P(), both,
    )
    out_specs = (
        both, both, P("row", "col"), P("row", "col"), P("row", "col"), P("col", "row"),
        P("col", "row", None), P("col", "row", None), P("col", None, "row"), P(), P(), P(),
    )
    return jax.shard_map(local, mesh=mesh, in_specs=in_specs, out_specs=out_specs, check_vma=False)
```

```python
import functools

import jax
import jax.numpy as jnp
from jax import lax
from jax.experimental import pallas as pl
from jax.experimental.pallas import tpu as pltpu
from jax.sharding import PartitionSpec as P

HEAD = 64
LANES = 128
QB = 256
EPS = 1e-06
RES = 0.22
SCALE = 0.125
BASE = 10000.0
bf16 = jnp.bfloat16
f32 = jnp.float32
VMEM_MB = 1 << 20


def dot_nt(a, b):
    return lax.dot_general(a, b, (((1,), (1,)), ((), ())), preferred_element_type=f32)


def dot_nn(a, b):
    return lax.dot_general(a, b, (((1,), (0,)), ((), ())), preferred_element_type=f32)


def rms_scale(values, gain_vec):
    return values * lax.rsqrt(jnp.mean(values * values, axis=-1, keepdims=True) + EPS) * gain_vec


def core_swap(a):
    return lax.ppermute(a, "col", [(i, i ^ 1) for i in range(8)])


def z_shift(a, d):
    return lax.ppermute(a, "col", [(i, (i + 2 * d) % 8) for i in range(8)])


def y_shift(a, d):
    return lax.ppermute(a, "row", [(i, (i // 4) * 4 + (i + d) % 4) for i in range(16)])


def x_shift(a, d):
    return lax.ppermute(a, "row", [(i, (i + 4 * d) % 16) for i in range(16)])


def gather_col(a, at, beside=None):
    half = a.shape[0] // 2
    back = z_shift(a, 1)
    ahead = z_shift(a, -1)
    if beside is not None:
        back, ahead, beside = lax.optimization_barrier((back, ahead, beside))
    far0 = z_shift(back[:half], 1)
    far1 = z_shift(ahead[half:], -1)
    mine = pl.pallas_call(
        place_kernel,
        grid_spec=pltpu.PrefetchScalarGridSpec(
            num_scalar_prefetch=1,
            grid=(1,),
            in_specs=[whole(v) for v in (a, back, ahead, far0, far1)],
            out_specs=pl.BlockSpec((4,) + a.shape, lambda g, at: (0, 0, 0)),
        ),
        out_shape=jax.ShapeDtypeStruct((4,) + a.shape, a.dtype),
        compiler_params=params(24),
    )(at, a, back, ahead, far0, far1)
    return mine, core_swap(mine), beside


def sum_col(pairs, beside=None, steps=()):
    steps = list(steps)

    def phase(*values):
        nonlocal beside
        if steps:
            beside = steps.pop(0)(beside)
            values, beside = lax.optimization_barrier((values, beside))
        return values

    pairs = phase(*pairs)
    own, ahead, behind, far0, far1 = fold(*pairs)
    via_up, via_down = phase(z_shift(far0, 1), z_shift(far1, -1))
    up, down = join(ahead, behind, via_up, via_down, 60 if steps else 24)
    up, down = phase(z_shift(up, 1), z_shift(down, -1))
    return (own, up, down), beside


def gather_row_small(a):
    ways = lax.axis_size("row")
    sent = jnp.broadcast_to(a[None], (ways,) + a.shape)
    return lax.all_to_all(sent, "row", 0, 0, tiled=True).reshape(-1, a.shape[1])


def exchange_row(a):
    ways = lax.axis_size("row")
    return lax.all_to_all(a.reshape(ways, -1, a.shape[1]), "row", 0, 0, tiled=True)


def send_all(a, axis):
    sent = jnp.broadcast_to(a[None], (lax.axis_size(axis),) + a.shape)
    return lax.all_to_all(sent, axis, 0, 0, tiled=True)


def two_parts(v):
    high = v.astype(bf16)
    return high, (v - high.astype(f32)).astype(bf16)


def row_step(v, bit):
    low = v.astype(bf16)
    got = lax.ppermute(low, "row", [(i, i ^ bit) for i in range(16)])
    return low.astype(f32) + got.astype(f32)


def lane_of(shape):
    return lax.broadcasted_iota(jnp.int32, shape, 1)


def rotate(values, cos, sin):
    first = (lane_of(values.shape) % HEAD) < HEAD // 2
    swapped = jnp.where(first, pltpu.roll(values, 96, 1), pltpu.roll(values, 32, 1))
    return values * cos + swapped * sin


def allowed_keys(lo, count, row0, begin):
    key = lax.broadcasted_iota(jnp.int32, (count, QB), 0) + lo
    query = lax.broadcasted_iota(jnp.int32, (count, QB), 1) + row0
    return (key >= begin) & (key <= query)


def soft(kk, qh, ok):
    s = jnp.where(ok, dot_nt(kk, qh) * SCALE, -1e30)
    raised = jnp.exp(s - jnp.max(s, axis=0, keepdims=True))
    return raised / jnp.sum(raised, axis=0, keepdims=True)


def key_range(i):
    return max(0, i - 2) * QB, (i + 1) * QB


def whole(v):
    return pl.BlockSpec(v.shape, lambda g, at, r=len(v.shape): (0,) * r)


def fold_kernel(*refs):
    own_ref, ahead_ref, behind_ref, far0_ref, far1_ref = refs[-5:]
    half = far0_ref.shape[0]
    at = 0
    for mine, got in zip(refs[:-5:2], refs[1:-5:2]):
        cols = slice(at, at + mine.shape[-1])
        at += mine.shape[-1]
        add = lambda k: mine[k].astype(f32) + got[k].astype(f32)
        own_ref[:, cols] = add(0)
        ahead_ref[:, cols] = add(1)
        behind_ref[:, cols] = add(3)
        far = add(2).astype(bf16)
        far0_ref[:, cols] = far[:half]
        far1_ref[:, cols] = far[half:]


def fold(*pairs):
    n = pairs[0][0].shape[1]
    w = sum(mine.shape[2] for mine, _ in pairs)
    one = jax.ShapeDtypeStruct((n, w), f32)
    part = jax.ShapeDtypeStruct((n // 2, w), bf16)
    return pl.pallas_call(
        fold_kernel, out_shape=(one, one, one, part, part), compiler_params=params(24)
    )(*[v for pair in pairs for v in pair])


def join_kernel(ahead_ref, behind_ref, via_up_ref, via_down_ref, up_ref, down_ref):
    half = via_up_ref.shape[0]
    up_ref[:half] = (ahead_ref[:half] + via_up_ref[...].astype(f32)).astype(bf16)
    up_ref[half:] = ahead_ref[half:].astype(bf16)
    down_ref[:half] = behind_ref[:half].astype(bf16)
    down_ref[half:] = (behind_ref[half:] + via_down_ref[...].astype(f32)).astype(bf16)


def join(ahead, behind, via_up, via_down, mb):
    one = jax.ShapeDtypeStruct(ahead.shape, bf16)
    return pl.pallas_call(join_kernel, out_shape=(one, one), compiler_params=params(mb))(
        ahead, behind, via_up, via_down
    )


def norm_back(x, grad, gain):
    inv = lax.rsqrt(jnp.mean(x * x, axis=-1, keepdims=True) + EPS)
    scaled = grad * gain
    hat = x * inv
    return inv * (scaled - hat * jnp.mean(hat * scaled, axis=-1, keepdims=True)), hat


def turn_kernel(
    own_ref, up_ref, down_ref, middle_ref, gates_ref, grad_ref, gain_ref, router_ref,
    back_ref, sent_ref, gain_part_ref,
):
    width = middle_ref.shape[1]
    arrived = own_ref[...] + up_ref[...].astype(f32) + down_ref[...].astype(f32)
    middle = middle_ref[...]
    parts = arrived[:, width:]
    gates_grad = parts + pltpu.roll(parts, 96, 1) + pltpu.roll(parts, 64, 1)
    gates = gates_ref[...]
    logits_grad = gates * (gates_grad - jnp.sum(gates * gates_grad, axis=1, keepdims=True))
    high = logits_grad.astype(bf16)
    rest = logits_grad - high.astype(f32)
    low = rest.astype(bf16)
    router = widened(router_ref[...])
    grad = arrived[:, :width] + dot_nn(high, router) + dot_nn(low, router)
    back, hat = norm_back(middle, grad, gain_ref[...])
    back = grad_ref[...].astype(f32) + back
    back_ref[...] = back
    sent_ref[:, :width] = (RES * back).astype(bf16)
    sent_ref[:, width:] = (high.astype(f32) + pltpu.roll(low.astype(f32), HEAD, 1)).astype(bf16)
    gain_part_ref[...] = jnp.sum(grad * hat, axis=0, keepdims=True)


def turn(own, up, down, middle, gates, grad, gain, router):
    n, width = middle.shape
    return pl.pallas_call(
        turn_kernel,
        out_shape=(
            jax.ShapeDtypeStruct((n, width), f32),
            jax.ShapeDtypeStruct((n, width + LANES), bf16),
            jax.ShapeDtypeStruct((1, width), f32),
        ),
        compiler_params=params(24),
    )(own, up, down, middle, gates, grad, gain, router)


def close_kernel(own_ref, up_ref, down_ref, x_ref, back_ref, gain_ref, middle_ref, out_ref, block_ref):
    width = out_ref.shape[1]
    arrived = own_ref[...] + up_ref[...].astype(f32) + down_ref[...].astype(f32)
    grad = arrived[:, :width]
    out_ref[...] = back_ref[...] + norm_back(x_ref[...].astype(f32), grad, gain_ref[...])[0]
    block_ref[...] = middle_ref[...] + RES * arrived[:, width:]


def close(own, up, down, x, back, gain, middle):
    one = jax.ShapeDtypeStruct(middle.shape, f32)
    return pl.pallas_call(close_kernel, out_shape=(one, one), compiler_params=params(24))(
        own, up, down, x, back, gain, middle
    )


def place_kernel(at_ref, own_ref, back_ref, ahead_ref, far0_ref, far1_ref, out_ref):
    z = at_ref[0]
    half = own_ref.shape[0] // 2
    out_ref[z] = own_ref[...]
    out_ref[lax.rem(z + 3, 4)] = back_ref[...]
    out_ref[lax.rem(z + 1, 4)] = ahead_ref[...]
    out_ref[lax.rem(z + 2, 4), :half] = far0_ref[...]
    out_ref[lax.rem(z + 2, 4), half:] = far1_ref[...]


def merge_kernel(at_ref, mine_ref, other_ref, *refs):
    core = at_ref[1]
    for k in range(4):
        for src, c in ((mine_ref, core), (other_ref, 1 - core)):
            at = 0
            for ref in refs:
                w = ref.shape[-1]
                ref[k, c] = src[k, :, at : at + w]
                at += w


def merge(at, mine, other, widths):
    _, n, _ = mine.shape
    outs = [jax.ShapeDtypeStruct((4, 2, n, w), bf16) for w in widths]
    found = pl.pallas_call(
        merge_kernel,
        grid_spec=pltpu.PrefetchScalarGridSpec(
            num_scalar_prefetch=1,
            grid=(1,),
            in_specs=[whole(mine), whole(other)],
            out_specs=[whole(v) for v in outs],
        ),
        out_shape=outs,
        compiler_params=params(24),
    )(at, mine, other)
    return [v.reshape(8 * n, v.shape[-1]) for v in found]


def pack_kernel(g_ref, u_ref, d_ref, share_ref):
    count, _, ff = g_ref.shape
    for e in range(count):
        at = 3 * ff * e
        share_ref[:, at : at + ff] = g_ref[e]
        share_ref[:, at + ff : at + 2 * ff] = u_ref[e]
        share_ref[:, at + 2 * ff : at + 3 * ff] = d_ref[e]


def pack(gate, up, down):
    count, n, ff = gate.shape
    return pl.pallas_call(
        pack_kernel,
        out_shape=jax.ShapeDtypeStruct((n, 3 * ff * count), bf16),
        compiler_params=params(60),
    )(gate, up, jnp.swapaxes(down, 1, 2))


def unpack_kernel(s_ref, g_ref, u_ref, d_ref):
    count, _, ff = g_ref.shape
    for e in range(count):
        at = 3 * ff * e
        g_ref[e] = s_ref[:, at : at + ff].astype(f32)
        u_ref[e] = s_ref[:, at + ff : at + 2 * ff].astype(f32)
        d_ref[e] = s_ref[:, at + 2 * ff : at + 3 * ff].astype(f32)


def unpack(share, count, ff):
    n = share.shape[0]
    block = jax.ShapeDtypeStruct((count, n, ff), f32)
    gate, up, down = pl.pallas_call(
        unpack_kernel,
        out_shape=(block, block, block),
        compiler_params=params(24),
    )(share)
    return gate, up, jnp.swapaxes(down, 1, 2)


def widened(router):
    kinds, width = router.shape
    return jnp.concatenate([router, jnp.zeros((LANES - kinds, width), router.dtype)], axis=0)


def project_kernel(
    at_ref, mine_ref, other_ref, x_ref, named_ref, gain_ref, router_ref, in_ref, gates_ref, own_ref, own_gates_ref, ctx_ref, wp_ref
):
    core = at_ref[1]
    total, width = x_ref.shape
    for k in range(4):
        for src, c in ((mine_ref, core), (other_ref, 1 - core)):
            lanes = pl.ds(pl.multiple_of((2 * k + c) * LANES, LANES), LANES)
            ctx_ref[:, lanes] = src[k, :total]
            wp_ref[:, lanes] = src[k, total:]
    me = 2 * at_ref[0] + core
    tokens = own_ref.shape[0]
    router = widened(router_ref[...])
    for i in range(total // QB):
        rows = pl.ds(i * QB, QB)
        middle = x_ref[rows, :].astype(f32) + RES * dot_nt(ctx_ref[rows, :], wp_ref[...])
        normed = rms_scale(middle, gain_ref[...]).astype(bf16)
        in_ref[rows, :] = normed
        logits = jnp.where(named_ref[rows, :] > 0, dot_nt(normed, router), -1e30)
        raised = jnp.exp(logits - jnp.max(logits, axis=1, keepdims=True))
        gates = raised / jnp.sum(raised, axis=1, keepdims=True)
        gates_ref[rows, :] = gates
        for half in range(QB // tokens):

            @pl.when(me == i * (QB // tokens) + half)
            def _():
                own_ref[...] = middle[half * tokens : (half + 1) * tokens]
                own_gates_ref[...] = gates[half * tokens : (half + 1) * tokens]


def project(at, mine, other, x, named, gain, router):
    total, width = x.shape
    outs = (
        jax.ShapeDtypeStruct((total, width), bf16),
        jax.ShapeDtypeStruct((total, LANES), f32),
        jax.ShapeDtypeStruct((total // 8, width), f32),
        jax.ShapeDtypeStruct((total // 8, LANES), f32),
    )
    ins = (mine, other, x, named, gain, router)
    return pl.pallas_call(
        project_kernel,
        grid_spec=pltpu.PrefetchScalarGridSpec(
            num_scalar_prefetch=1,
            grid=(1,),
            in_specs=[whole(v) for v in ins],
            out_specs=[whole(v) for v in outs],
            scratch_shapes=[pltpu.VMEM((total, width), bf16), pltpu.VMEM((total, width), bf16)],
        ),
        out_shape=outs,
        compiler_params=params(60),
    )(at, *ins)


def split_blocks(at_ref, value_of, mine_ref, theirs_ref, n):
    z, core = at_ref[0], at_ref[1]
    for k in range(4):
        there = lax.rem(z + k, 4) * 2
        for ref, c in ((mine_ref, core), (theirs_ref, 1 - core)):
            value_of(ref, k, pl.ds(pl.multiple_of((there + c) * n, n), n))


def attend_kernel(x_ref, gain_ref, w_ref, cos_ref, sin_ref, begin_ref, n_ref, q_ref, kk_ref, vv_ref, heads_ref):
    total = x_ref.shape[0]
    left = lane_of((QB, LANES)) < HEAD
    for i in range(total // QB):
        rows = pl.ds(i * QB, QB)
        x = x_ref[rows, :].astype(f32)
        normed = rms_scale(x, gain_ref[...]).astype(bf16)
        n_ref[rows, :] = normed
        raw = dot_nn(normed, w_ref[:, : 2 * LANES])
        cos, sin = cos_ref[rows, :], sin_ref[rows, :]
        q_ref[rows, :] = rotate(raw[:, :LANES], cos, sin).astype(bf16)
        kv = raw[:, LANES:]
        turned = rotate(kv, cos, sin)
        kk_ref[rows, :] = jnp.where(left, turned, pltpu.roll(turned, HEAD, 1)).astype(bf16)
        vv_ref[rows, :] = jnp.where(left, pltpu.roll(kv, HEAD, 1), kv).astype(bf16)
    vt = vv_ref[...].astype(f32).T.astype(bf16)
    upper = lax.broadcasted_iota(jnp.int32, (LANES, QB), 0) < HEAD
    for i in range(total // QB):
        rows = pl.ds(i * QB, QB)
        lo, hi = key_range(i)
        keys = kk_ref[lo:hi, :]
        ok = allowed_keys(lo, hi - lo, i * QB, begin_ref[:, i * QB : (i + 1) * QB])
        found = []
        for h in range(2):
            qh = jnp.where(left == (h == 0), q_ref[rows, :], jnp.zeros((QB, LANES), bf16))
            p = soft(keys, qh, ok).astype(bf16)
            found.append(dot_nn(vt[:, lo:hi], p))
        heads_ref[rows, :] = jnp.where(upper, found[0], found[1]).T.astype(bf16)
    heads_ref[total:, :] = w_ref[:, 2 * LANES :]


def attend_back_kernel(
    at_ref, ag_ref, q_ref, kk_ref, vv_ref, heads_ref, x_ref, cos_ref, sin_ref, begin_ref, w_ref,
    mine_ref, theirs_ref, gain_ref, dqkv_ref, dctx_ref, dk_ref, dv_ref, dn_ref,
):
    total = ag_ref.shape[0]
    left = lane_of((QB, LANES)) < HEAD
    upper = lax.broadcasted_iota(jnp.int32, (LANES, QB), 0) < HEAD
    dctx_ref[...] = dot_nn(ag_ref[...], heads_ref[total:, :]).astype(bf16)
    dk_ref[...] = jnp.zeros_like(dk_ref)
    dv_ref[...] = jnp.zeros_like(dv_ref)
    kt = kk_ref[...].astype(f32).T.astype(bf16)
    for i in range(total // QB):
        rows = pl.ds(i * QB, QB)
        lo, hi = key_range(i)
        keys = kk_ref[lo:hi, :]
        ok = allowed_keys(lo, hi - lo, i * QB, begin_ref[:, i * QB : (i + 1) * QB])
        found = []
        for h in range(2):
            mine = left == (h == 0)
            qh = jnp.where(mine, q_ref[rows, :], jnp.zeros((QB, LANES), bf16))
            dch = jnp.where(mine, dctx_ref[rows, :], jnp.zeros((QB, LANES), bf16))
            p = soft(keys, qh, ok)
            dp = dot_nt(vv_ref[lo:hi, :], dch)
            ds = (p * (dp - jnp.sum(dp * p, axis=0, keepdims=True))).astype(bf16)
            dk_ref[lo:hi, :] += dot_nn(ds, qh)
            dv_ref[lo:hi, :] += dot_nn(p.astype(bf16), dch)
            found.append(dot_nn(kt[:, lo:hi], ds))
        dq = jnp.where(upper, found[0], found[1]).T * SCALE
        dqkv_ref[rows, :LANES] = rotate(dq, cos_ref[rows, :], -sin_ref[rows, :]).astype(bf16)
    acc = jnp.zeros((1, x_ref.shape[1]), f32)
    for i in range(total // QB):
        rows = pl.ds(i * QB, QB)
        dk, dv = dk_ref[rows, :], dv_ref[rows, :]
        dk = (dk + pltpu.roll(dk, HEAD, 1)) * SCALE
        dk = rotate(dk, cos_ref[rows, :], -sin_ref[rows, :])
        dv = dv + pltpu.roll(dv, HEAD, 1)
        dqkv_ref[rows, LANES:] = jnp.where(left, dk, dv).astype(bf16)
        dn = dot_nt(dqkv_ref[rows, :], w_ref[:, : 2 * LANES])
        dn_ref[rows, :] = dn.astype(bf16)
        x = x_ref[rows, :].astype(f32)
        hat = x * lax.rsqrt(jnp.mean(x * x, axis=-1, keepdims=True) + EPS)
        acc = acc + jnp.sum(dn * hat, axis=0, keepdims=True)
    gain_ref[...] = acc

    def give(ref, k, rows):
        ref[k] = dn_ref[rows, :]

    split_blocks(at_ref, give, mine_ref, theirs_ref, mine_ref.shape[1])


def attend_weights_kernel(dqkv_ref, normed_ref, heads_ref, ag_ref, in_ref, dl_ref, wg_ref, rows_ref):
    total = ag_ref.shape[0]
    dqkv_t = dqkv_ref[...].astype(f32).T.astype(bf16)
    ctx_t = heads_ref[:total, :].astype(f32).T.astype(bf16)
    wg_ref[:, : 2 * LANES] = dot_nn(dqkv_t, normed_ref[...]).T.astype(bf16)
    wg_ref[:, 2 * LANES :] = dot_nn(ctx_t, ag_ref[...]).T.astype(bf16)
    parts = dot_nn(dl_ref[...].astype(f32).T.astype(bf16), in_ref[...])
    rows_ref[...] = parts[: rows_ref.shape[0]] + parts[HEAD : HEAD + rows_ref.shape[0]]


def experts_kernel(
    at_ref, x_ref, dy_ref, gates_ref, w_ref, mine_ref, theirs_ref, mix_mine_ref, mix_theirs_ref, out_ref,
    acts_ref, xt_ref, dyt_ref, accm_ref, accx_ref, dg_ref,
):
    e = pl.program_id(0)
    ff = acts_ref.shape[1] // 3
    total = x_ref.shape[0]
    lane = lane_of((total, LANES))
    pick = (2 * at_ref[0] + at_ref[1]) * pl.num_programs(0) + e

    @pl.when(e == 0)
    def _():
        xt_ref[...] = x_ref[...].T
        dyt_ref[...] = dy_ref[...].T
        accm_ref[...] = jnp.zeros_like(accm_ref)
        accx_ref[...] = jnp.zeros_like(accx_ref)
        dg_ref[...] = jnp.zeros_like(dg_ref)

    gu = dot_nn(x_ref[...], w_ref[:, : 2 * ff])
    h0 = dot_nn(dy_ref[...], w_ref[:, 2 * ff :]) * RES
    g, u = gu[:, :ff], gu[:, ff:]
    gate = jnp.sum(jnp.where(lane == pick, gates_ref[...], 0.0), axis=1, keepdims=True)
    sg = jax.nn.sigmoid(g)
    sw = g * sg
    hid = sw * u
    dg = jnp.sum(hid * h0, axis=1, keepdims=True)
    dg_ref[...] += jnp.where(lane == pick, dg, 0.0)
    acts_ref[:, 2 * ff :] = (gate * hid).astype(bf16)
    dh = gate * h0
    acts_ref[:, :ff] = (dh * u * sg * (1.0 + g * (1.0 - sg))).astype(bf16)
    acts_ref[:, ff : 2 * ff] = (dh * sw).astype(bf16)
    accm_ref[...] += dot_nt(acts_ref[:, 2 * ff :], w_ref[:, 2 * ff :])
    accx_ref[...] += dot_nt(acts_ref[:, : 2 * ff], w_ref[:, : 2 * ff])
    out_ref[:, : 2 * ff] = dot_nn(xt_ref[...], acts_ref[:, : 2 * ff]).astype(bf16)
    out_ref[:, 2 * ff :] = (dot_nn(dyt_ref[...], acts_ref[:, 2 * ff :]) * RES).astype(bf16)

    @pl.when(e == pl.num_programs(0) - 1)
    def _():
        width = accx_ref.shape[1]
        dg = dg_ref[...]
        high = dg.astype(bf16).astype(f32)
        mid = (dg - high).astype(bf16).astype(f32)
        low = dg - high - mid
        dg_ref[...] = high + pltpu.roll(mid, 32, 1) + pltpu.roll(low, 64, 1)

        def give(ref, k, rows):
            ref[k, :, :width] = accx_ref[rows, :].astype(bf16)
            ref[k, :, width:] = dg_ref[rows, :].astype(bf16)

        def give_mix(ref, k, rows):
            ref[k] = accm_ref[rows, :].astype(bf16)

        split_blocks(at_ref, give, mine_ref, theirs_ref, mine_ref.shape[1])
        split_blocks(at_ref, give_mix, mix_mine_ref, mix_theirs_ref, mine_ref.shape[1])


def params(mb):
    return pltpu.CompilerParams(vmem_limit_bytes=mb * VMEM_MB)


def attend(x_all, gain, weights, cos, sin, begin):
    total, width = x_all.shape
    shape = lambda n, w: jax.ShapeDtypeStruct((n, w), bf16)
    one = shape(total, LANES)
    return pl.pallas_call(
        attend_kernel,
        out_shape=(shape(total, width), one, one, one, shape(total + width, LANES)),
        compiler_params=params(48),
    )(x_all, gain, weights, cos, sin, begin)


def attend_back(at, *ins):
    total, width = ins[0].shape
    block = jax.ShapeDtypeStruct((4, total // 8, width), bf16)
    outs = (
        block,
        block,
        jax.ShapeDtypeStruct((1, width), f32),
        jax.ShapeDtypeStruct((total, 2 * LANES), bf16),
    )
    return pl.pallas_call(
        attend_back_kernel,
        grid_spec=pltpu.PrefetchScalarGridSpec(
            num_scalar_prefetch=1,
            grid=(1,),
            in_specs=[whole(v) for v in ins],
            out_specs=[whole(v) for v in outs],
            scratch_shapes=[
                pltpu.VMEM((total, LANES), bf16),
                pltpu.VMEM((total, LANES), f32),
                pltpu.VMEM((total, LANES), f32),
                pltpu.VMEM((total, width), bf16),
            ],
        ),
        out_shape=outs,
        compiler_params=params(32),
    )(at, *ins)


def attend_weights(*ins, kinds):
    width = ins[3].shape[1]
    return pl.pallas_call(
        attend_weights_kernel,
        out_shape=(
            jax.ShapeDtypeStruct((width, 3 * LANES), bf16),
            jax.ShapeDtypeStruct((kinds, width), f32),
        ),
        compiler_params=params(24),
    )(*ins)


def experts(at, x, dy, gates, weights, count):
    total, width = x.shape
    ff = weights.shape[1] // (3 * count)
    block = jax.ShapeDtypeStruct((4, total // 8, width + LANES), bf16)
    mix = jax.ShapeDtypeStruct((4, total // 8, width), bf16)
    each = pl.BlockSpec((width, 3 * ff), lambda e, at: (0, e))
    return pl.pallas_call(
        experts_kernel,
        grid_spec=pltpu.PrefetchScalarGridSpec(
            num_scalar_prefetch=1,
            grid=(count,),
            in_specs=[whole(x), whole(dy), whole(gates), each],
            out_specs=[whole(block), whole(block), whole(mix), whole(mix), each],
            scratch_shapes=[
                pltpu.VMEM((total, 3 * ff), bf16),
                pltpu.VMEM((width, total), bf16),
                pltpu.VMEM((width, total), bf16),
                pltpu.VMEM((total, width), f32),
                pltpu.VMEM((total, width), f32),
                pltpu.VMEM((total, LANES), f32),
            ],
        ),
        out_shape=(block, block, mix, mix, jax.ShapeDtypeStruct((width, 3 * ff * count), bf16)),
        compiler_params=params(60),
        cost_estimate=pl.CostEstimate(
            flops=18 * total * width * ff * count,
            bytes_accessed=4 * width * 3 * ff * count,
            transcendentals=total * ff * count,
        ),
    )(at, x, dy, gates, weights)


def tables(lengths_row, group):
    ends = jnp.cumsum(lengths_row)
    starts = ends - lengths_row
    places = jnp.arange(group, dtype=jnp.int32)
    inside = (places[:, None] >= starts[None, :]) & (places[:, None] < ends[None, :])
    begin = jnp.sum(jnp.where(inside, starts[None, :], 0), axis=1)
    frequency = BASE ** (-(jnp.arange(HEAD // 2, dtype=f32) * 2.0 / HEAD))
    angles = (places - begin).astype(f32)[:, None] * frequency[None, :]
    cos, sin = jnp.cos(angles), jnp.sin(angles)
    return (
        begin.reshape(1, group),
        jnp.concatenate([cos] * 4, axis=1),
        jnp.concatenate([-sin, sin, -sin, sin], axis=1),
    )


def local(
    layer_input, lengths, choices, query_weight, key_matrix, value_matrix, project_weight,
    gate_weight, up_weight, down_weight, router_weight, attention_gain, expert_gain, grad_output,
):
    me = lax.axis_index("col")
    tokens, width = layer_input.shape
    group = tokens * 8
    kinds = router_weight.shape[1]
    count, _, ff = gate_weight.shape
    own = lambda v: lax.dynamic_slice_in_dim(v, me * tokens, tokens, axis=0)

    at = jnp.stack([me // 2, me % 2]).astype(jnp.int32)
    spots = jnp.arange(LANES, dtype=jnp.int32)
    named = jnp.any(choices[:, :, None] == spots[None, None, :], axis=1).astype(bf16)
    share = pack(gate_weight, up_weight, down_weight)
    expert_weights = lax.all_gather(share, "row", axis=0, tiled=True)
    small = gather_row_small(
        jnp.concatenate([query_weight, key_matrix, value_matrix, project_weight.T], axis=1)
    )
    *entering, small = gather_col(jnp.concatenate([layer_input, grad_output, named], axis=1), at, small)
    x_all, dy_all, named_all = merge(at, *entering, (width, width, LANES))

    begin, cos, sin = tables(lengths[0], group)
    gain_one = attention_gain.reshape(1, width)
    normed, q, kk, vv, heads = attend(x_all, gain_one, small, cos, sin, begin)
    heads_mine, heads_other, _ = gather_col(heads, at)
    router = router_weight.T
    gain_two = expert_gain.reshape(1, width)
    expert_in, gates_all, middle, gates = project(
        at, heads_mine, heads_other, x_all, named_all, gain_two, router
    )
    mine, theirs, mix_mine, mix_theirs, expert_wgrad = experts(
        at, expert_in, dy_all, gates_all, expert_weights, count
    )
    expert_sum = lax.psum_scatter(expert_wgrad, "row", scatter_dimension=0, tiled=True)

    arrived, _ = sum_col([(mine, core_swap(theirs))])
    middle_grad, sent, gain_two_part = turn(*arrived, middle, gates, grad_output, gain_two, router)
    back_mine, back_other, _ = gather_col(sent, at)
    ag_all, logits_all = merge(at, back_mine, back_other, (width, LANES))

    dn_mine, dn_theirs, gain_part, dqkv = attend_back(
        at, ag_all, q, kk, vv, heads, x_all, cos, sin, begin, small
    )
    sent = []

    def opening(_):
        wg, rows = attend_weights(dqkv, normed, heads, ag_all, expert_in, logits_all, kinds=kinds)
        sent.append(exchange_row(wg))
        both = jnp.concatenate(two_parts(jnp.concatenate([gain_two_part, gain_part], axis=0)), axis=0)
        gains = jnp.sum(send_all(both, "col").astype(f32), axis=0)
        return jnp.concatenate([rows, gains[:2] + gains[2:]], axis=0)

    def third(rows):
        return row_step(rows, 2), sent[0]

    pairs = [(dn_mine, core_swap(dn_theirs)), (mix_mine, core_swap(mix_theirs))]
    terms, (rows, pieces) = sum_col(pairs, None, [opening, lambda v: row_step(v, 1), third])
    input_grad, block_output = close(*terms, layer_input, middle_grad, gain_one, middle)
    rows = row_step(row_step(rows, 4), 8)
    small_sum = jnp.sum(pieces.astype(f32), axis=0)
    gate_grad, up_grad, down_grad = unpack(expert_sum, count, ff)
    return (
        block_output,
        input_grad,
        small_sum[:, :LANES],
        small_sum[:, LANES : LANES + HEAD],
        small_sum[:, LANES + HEAD : 2 * LANES],
        small_sum[:, 2 * LANES :].T,
        gate_grad,
        up_grad,
        down_grad,
        rows[:kinds].T,
        rows[kinds + 1],
        rows[kinds],
    )


def solution(mesh):
    both = P(("row", "col"), None)
    in_specs = (
        both, P("row", None), both, P("row", "col"), P("row", "col"), P("row", "col"), P("col", "row"),
        P("col", "row", None), P("col", "row", None), P("col", None, "row"), P(), P(), P(), both,
    )
    out_specs = (
        both, both, P("row", "col"), P("row", "col"), P("row", "col"), P("col", "row"),
        P("col", "row", None), P("col", "row", None), P("col", None, "row"), P(), P(), P(),
    )
    return jax.shard_map(local, mesh=mesh, in_specs=in_specs, out_specs=out_specs, check_vma=False)
```
